128 devices in a mesh: row: 8 (over x, core), col: 16 (over z, y).
Axes of the slice: x: 4, y: 4, z: 4, core: 2. Of those that a mesh axis runs over, the one named last changes fastest.
Arguments:
- embeddings: float32 [49152, 128], P(('row', 'col')), may hold values from -17 to 17
- counts: int32 [32, 49152], P(None, ('row', 'col')), may hold values from 0 to 20, as said below
- raw_weights: float32 [32], replicated, may hold values from 0.25 to 4
Outputs:
- center: float32 [49152], P(('row', 'col'))
- scale_u: float32 [32, 49152], P(None, ('row', 'col'))
- scale_v: float32 [32, 49152], P(None, ('row', 'col'))
- misfit: float32 [32], replicated
The draws below stay inside these ranges and needn't reach their ends.
Inputs may be any that keep to these rules, and one draw needn't show every extreme that they name: non-negative cell counts; every time point has at least one cell.
All inputs are finite; a program needn't handle non-finite values.
Results may differ from the reference program's by a relative error of at most 0.0021.
The reference program's roundings to bfloat16 on the way count: a program that leaves them out, or rounds other values in their place, can miss the bound.
Values may be sent and summed in bfloat16 or wider, within the bound.
A program may use at most 128 MiB of HBM per device.

```python
import math
import jax
import jax.numpy as jnp
from jax import lax

E = 128
HIST = 32
ITERS = 2
N = 49152


def cluster_ids():
    position = jnp.arange(N, dtype=jnp.int32)
    return position // 64


def draw_embeddings(key, part):
    member = cluster_ids()
    key = jax.random.fold_in(key, 3)
    centre_key, jitter_key, spread_key = jax.random.split(key, 3)
    groups = N // 64
    centres = jnp.clip(jax.random.normal(centre_key, (groups, E), jnp.float32), -4.0, 4.0)
    jitter = jnp.clip(jax.random.normal(jitter_key, (N, E), jnp.float32), -4.0, 4.0)
    spread = jax.random.uniform(spread_key, (N, 1), jnp.float32, 0.25, 0.62)
    points = centres[member] + spread * jitter
    return points.astype(jnp.float32)


def draw_counts(key, part):
    member = cluster_ids()
    key = jax.random.fold_in(key, 11)
    first_key, second_key = jax.random.split(key)
    groups = N // 64
    position = jnp.arange(N, dtype=jnp.int32)
    cluster_start = jnp.arange(groups, dtype=jnp.int32) * 64
    cluster_range = 1 + 6 * cluster_start // N
    liking = 1 + jax.random.randint(first_key, (HIST, groups), 0, cluster_range[None, :])
    factors = liking[:, member]
    ceiling = 3 * factors
    sampled = jax.random.randint(second_key, (HIST, N), 0, ceiling)
    first_cell = position == 0
    filled = jnp.where(first_cell[None, :], 20, sampled)
    return jnp.minimum(filled, 20).astype(jnp.int32)


def setup_inputs(seed: int = 0) -> dict:
    key_list = jax.random.split(jax.random.key(seed), 4)
    return {
        "embeddings": draw_embeddings(jax.random.fold_in(key_list[3], 71), 0),
        "counts": draw_counts(jax.random.fold_in(key_list[3], 71), 0),
        "raw_weights": jnp.clip(jnp.exp(jax.random.uniform(key_list[2], (HIST,), jnp.float32, math.log(0.25), math.log(4.0))), 0.25, 4.0),
    }


EPS_KERNEL = 0.2
EPS_NORM = 1e-06

def kernel_block(left, right):
    gram = lax.dot_general(left, right, (((1,), (1,)), ((), ())), preferred_element_type=jnp.float32)
    return jnp.exp((2.0 * gram - 2.0) / EPS_KERNEL).astype(jnp.bfloat16)

def reference(embeddings, counts, raw_weights):
    total_pts = embeddings.shape[0]
    histograms = counts.shape[0]
    squares = lax.optimization_barrier(jnp.sum(embeddings * embeddings, axis=1, keepdims=True))
    unit = (embeddings * lax.rsqrt(squares + EPS_NORM)).astype(jnp.bfloat16)
    totals = lax.optimization_barrier(jnp.sum(counts.astype(jnp.float32), axis=1))
    target = counts.astype(jnp.float32) * (total_pts / totals)[:, None]
    weights = raw_weights / jnp.sum(raw_weights)
    block = math.gcd(total_pts, 512)
    nblocks = total_pts // block
    blocks = unit.reshape(nblocks, block, unit.shape[1])

    def apply_rows(vector):

        def one_block(rows):
            tile = kernel_block(rows, unit)
            return lax.dot_general(vector, tile, (((1,), (1,)), ((), ())), preferred_element_type=jnp.float32)
        parts = lax.map(one_block, blocks)
        return jnp.transpose(parts, (1, 0, 2)).reshape(histograms, total_pts)

    def apply_columns(vector):
        pieces = jnp.transpose(vector.reshape(histograms, nblocks, block), (1, 0, 2))

        def one_block(running, item):
            rows, piece = item
            tile = kernel_block(rows, unit)
            return (running + jnp.dot(piece, tile, preferred_element_type=jnp.float32), None)
        start_sum = jnp.zeros((histograms, total_pts), jnp.float32)
        running, _ = lax.scan(one_block, start_sum, (blocks, pieces))
        return running
    scale_v = jnp.ones((histograms, total_pts), jnp.float32)
    for sweep_index in range(ITERS):
        row_sum = apply_rows(scale_v.astype(jnp.bfloat16))
        scale_u = target / row_sum
        col_sum = apply_columns(scale_u.astype(jnp.bfloat16))
        raw_center = jnp.exp(lax.optimization_barrier(jnp.sum(weights[:, None] * jnp.log(col_sum), axis=0)))
        center = raw_center * (total_pts / jnp.sum(raw_center))
        misfit = lax.optimization_barrier(jnp.sum(jnp.abs(scale_v * col_sum - center[None, :]), axis=1)) / total_pts
        scale_v = center[None, :] / col_sum
    return (center, scale_u, scale_v, misfit)
```

```python
import functools

import jax
import jax.numpy as jnp
from jax import lax
from jax.experimental import pallas as pl
from jax.experimental.pallas import tpu as pltpu
from jax.sharding import PartitionSpec as P

GROUP_I = ((0, 0), (0, 1), (1, 0), (3, 0), (1, 1), (3, 1), (2, 0), (2, 1))
GROUP_J = ((0, 0), (1, 0), (3, 0), (2, 0), (0, 1), (1, 1), (3, 1), (2, 1))
MESH = pl.DeviceIdType.MESH
SLOPE = 14.426950408889634
HIST = 32
OWN = 384
PER_I, PER_J = 16, 8
ROWS, COLS = OWN * PER_I, OWN * PER_J
BUILD_I, BUILD_J = 1536, 768
PASS_J = 768


def body(
    total_pts,
    emb_ref,
    counts_ref,
    weights_ref,
    center_ref,
    scale_u_ref,
    scale_v_ref,
    misfit_ref,
    tile,
    unit_i,
    unit_j,
    x_buf,
    y_part,
    y_recv,
    first_part,
    first_recv,
    target,
    v_first,
    wide_i,
    wide_j,
    mass_i,
    mass_j,
    send_unit_i,
    recv_unit_i,
    send_unit_j,
    recv_unit_j,
    send_first,
    recv_first,
    send_x,
    recv_x,
    send_y,
    recv_y,
    send_wide_i,
    recv_wide_i,
    send_wide_j,
    recv_wide_j,
    send_mass_i,
    recv_mass_i,
    send_mass_j,
    recv_mass_j,
):
    row, col = lax.axis_index("row"), lax.axis_index("col")
    x, core = lax.div(row, 2), lax.rem(row, 2)
    z, y = lax.div(col, 4), lax.rem(col, 4)
    half, parity = lax.div(y, 2), lax.rem(y, 2)

    def flip(bit, by):
        return 1 - bit if by else bit

    def device(nx, ncore, nz, nhalf, nparity):
        return (nx * 2 + ncore, nz * 4 + nhalf * 2 + nparity)

    def device_i(k):
        dx, dp = GROUP_I[k // 2]
        return device(lax.rem(x + 4 - dx, 4), flip(core, k % 2), z, half, flip(parity, dp))

    def device_j(k):
        dz, dh = GROUP_J[k]
        return device(x, core, lax.rem(z + 4 - dz, 4), flip(half, dh), parity)

    def owner_j(k):
        dz, dh = GROUP_J[k]
        return device(x, core, lax.rem(z + dz, 4), flip(half, dh), parity)

    def copy_i(k, src, dst, send, recv):
        return pltpu.make_async_remote_copy(
            src_ref=src, dst_ref=dst, send_sem=send.at[k], recv_sem=recv.at[k],
            device_id=device_i(k), device_id_type=MESH,
        )

    def copy_j(k, src, dst, send, recv):
        return pltpu.make_async_remote_copy(
            src_ref=src, dst_ref=dst, send_sem=send.at[k], recv_sem=recv.at[k],
            device_id=device_j(k), device_id_type=MESH,
        )

    def copy_to_owner(k, src, dst, send, recv):
        return pltpu.make_async_remote_copy(
            src_ref=src, dst_ref=dst, send_sem=send.at[k], recv_sem=recv.at[k],
            device_id=owner_j(k), device_id_type=MESH,
        )

    barrier = pltpu.get_barrier_semaphore()
    for k in range(1, PER_I):
        pl.semaphore_signal(barrier, inc=1, device_id=device_i(k), device_id_type=MESH)
    for k in range(1, PER_J):
        pl.semaphore_signal(barrier, inc=1, device_id=device_j(k), device_id_type=MESH)

    emb = emb_ref[...]
    squares = jnp.sum(emb * emb, axis=1, keepdims=True)
    unit = (emb * lax.rsqrt(squares + 1e-6)).astype(jnp.bfloat16)
    unit_i[0:OWN, :] = unit
    unit_j[0:OWN, :] = unit
    counts = counts_ref[...].astype(jnp.float32)

    def lanes(value):
        return value[:, 0:128] + value[:, 128:256] + value[:, 256:384]

    raw_weights = weights_ref[...]
    eye = lax.broadcasted_iota(jnp.int32, (HIST, HIST), 0) == lax.broadcasted_iota(
        jnp.int32, (HIST, HIST), 1
    )
    weights = jnp.sum(
        jnp.where(eye, raw_weights / jnp.sum(raw_weights), 0.0), axis=1, keepdims=True
    )

    def rows_of(k):
        return pl.ds(k * OWN, OWN)

    pl.semaphore_wait(barrier, PER_I + PER_J - 2)

    unit_copies_i = {
        k: copy_i(k, unit_i.at[rows_of(0)], unit_i.at[rows_of(k)], send_unit_i, recv_unit_i)
        for k in range(1, PER_I)
    }
    unit_copies_j = {
        k: copy_j(k, unit_j.at[rows_of(0)], unit_j.at[rows_of(k)], send_unit_j, recv_unit_j)
        for k in range(1, PER_J)
    }
    unit_copies_i[1].start()
    for s in range(1, 8):
        unit_copies_j[s].start()
        unit_copies_i[2 * s].start()
        unit_copies_i[2 * s + 1].start()

    def reduce_j(value, buf, index, send, recv):
        buf[index, 0] = value
        copies = [
            copy_j(k, buf.at[index, 0], buf.at[index, k], send.at[index], recv.at[index])
            for k in range(1, PER_J)
        ]
        for copy in copies:
            copy.start()
        return copies

    def reduce_i(value, buf, index, send, recv):
        buf[index, 0] = value
        copies = [
            copy_i(k, buf.at[index, 0], buf.at[index, k], send.at[index], recv.at[index])
            for k in range(1, PER_I)
        ]
        for copy in copies:
            copy.start()
        return copies

    def finish(copies, buf, index):
        for copy in copies:
            copy.wait()
        return jnp.sum(buf[index], axis=0)

    totals_j = reduce_j(lanes(counts), wide_j, 0, send_wide_j, recv_wide_j)

    first_part[...] = jnp.zeros_like(first_part)

    def build(n, carry):
        t = (n >= 1).astype(jnp.int32) + (n >= 4).astype(jnp.int32) + (n >= 9).astype(jnp.int32)
        m = n - t * t
        down = (m <= t).astype(jnp.int32)
        i = down * t + (1 - down) * (m - t - 1)
        j = down * m + (1 - down) * t
        for step in range(4):

            @pl.when(n == step * step)
            def _():
                for s in (2 * step, 2 * step + 1):
                    if s:
                        unit_copies_j[s].wait()
                        unit_copies_i[2 * s].wait()
                    unit_copies_i[2 * s + 1].wait()

        at_i = pl.ds(pl.multiple_of(i * BUILD_I, BUILD_I), BUILD_I)
        at_j = pl.ds(pl.multiple_of(j * BUILD_J, BUILD_J), BUILD_J)
        gram = lax.dot_general(
            unit_i[at_i, :], unit_j[at_j, :], (((1,), (1,)), ((), ())),
            preferred_element_type=jnp.float32,
        )
        value = jnp.exp2(gram * SLOPE - SLOPE)
        tile[at_i, at_j] = value.astype(jnp.bfloat16)
        first_part[:, at_j] += jnp.sum(value.reshape(BUILD_I // 8, 8, BUILD_J), axis=0)
        return carry

    lax.fori_loop(0, 16, build, 0)

    totals_i = reduce_i(finish(totals_j, wide_j, 0), wide_i, 0, send_wide_i, recv_wide_i)

    first_copies = [
        copy_to_owner(k, first_part.at[:, rows_of(k)], first_recv.at[k], send_first, recv_first)
        for k in range(1, PER_J)
    ]
    for copy in first_copies:
        copy.start()
    totals = jnp.sum(finish(totals_i, wide_i, 0), axis=1, keepdims=True)
    target[...] = counts * (total_pts / totals)
    first_recv[0] = first_part[:, 0:OWN]
    for copy in first_copies:
        copy.wait()
    row_sum = jnp.sum(jnp.sum(first_recv[...], axis=0), axis=0, keepdims=True)

    def run_pass(index, value):
        x_buf[index, :, 0:OWN] = value.astype(jnp.bfloat16)
        gather = [
            copy_i(
                k, x_buf.at[index, :, rows_of(0)], x_buf.at[index, :, rows_of(k)],
                send_x.at[index], recv_x.at[index],
            )
            for k in range(1, PER_I)
        ]
        for copy in gather:
            copy.start()
        copies = {
            k: copy_to_owner(
                k, y_part.at[index, :, rows_of(k)], y_recv.at[index, k],
                send_y.at[index], recv_y.at[index],
            )
            for k in range(1, PER_J)
        }
        for copy in gather:
            copy.wait()

        def chunk(n, carry):
            q = 3 - n
            at = pl.ds(pl.multiple_of(q * PASS_J, PASS_J), PASS_J)
            y_part[index, :, at] = jnp.dot(
                x_buf[index], tile[:, at], preferred_element_type=jnp.float32
            )
            for which in range(4):

                @pl.when(q == which)
                def _():
                    for k in (2 * which + 1, 2 * which):
                        if k:
                            copies[k].start()

            return carry

        lax.fori_loop(0, 4, chunk, 0)
        y_recv[index, 0] = y_part[index, :, 0:OWN]
        for copy in copies.values():
            copy.wait()
        return jnp.sum(y_recv[index], axis=0)

    def raw(col_sum):
        return jnp.exp(jnp.sum(weights * jnp.log(col_sum), axis=0, keepdims=True))

    def spread(value):
        return jnp.broadcast_to(lanes(value), (8, 128))

    def scalar(value):
        return jnp.sum(value[0:1, :], axis=1, keepdims=True)

    col_sum = run_pass(0, target[...] / row_sum)
    raw_center = raw(col_sum)
    mass_copies = reduce_j(spread(raw_center), mass_j, 0, send_mass_j, recv_mass_j)
    v_first[...] = raw_center / col_sum

    row_sum = run_pass(1, v_first[...])
    mass_copies = reduce_i(
        finish(mass_copies, mass_j, 0), mass_i, 0, send_mass_i, recv_mass_i
    )
    factor = total_pts / scalar(finish(mass_copies, mass_i, 0))
    scale_u = target[...] / (row_sum * factor)
    scale_u_ref[...] = scale_u
    scale_v = v_first[...] * factor
    col_sum = run_pass(2, scale_u)
    raw_center = raw(col_sum)
    mass_copies = reduce_j(spread(raw_center), mass_j, 1, send_mass_j, recv_mass_j)
    mass_copies = reduce_i(
        finish(mass_copies, mass_j, 1), mass_i, 1, send_mass_i, recv_mass_i
    )
    factor = total_pts / scalar(finish(mass_copies, mass_i, 1))
    center = raw_center * factor
    error = lanes(jnp.abs(scale_v * col_sum - center))
    error_copies = reduce_j(error, wide_j, 1, send_wide_j, recv_wide_j)
    center_ref[...] = center
    scale_v_ref[...] = center / col_sum
    error_copies = reduce_i(
        finish(error_copies, wide_j, 1), wide_i, 1, send_wide_i, recv_wide_i
    )
    misfit = jnp.sum(finish(error_copies, wide_i, 1), axis=1, keepdims=True) / total_pts
    misfit_ref[...] = jnp.sum(jnp.where(eye, misfit, 0.0), axis=0, keepdims=True)


def shards(embeddings, counts, raw_weights):
    total_pts = embeddings.shape[0] * lax.axis_size("row") * lax.axis_size("col")
    vmem = pl.BlockSpec(memory_space=pltpu.VMEM)
    f32, bf16, dma = jnp.float32, jnp.bfloat16, pltpu.SemaphoreType.DMA
    pair_i, pair_j = [dma((PER_I,))] * 2, [dma((PER_J,))] * 2
    center, scale_u, scale_v, misfit = pl.pallas_call(
        functools.partial(body, total_pts),
        out_shape=(
            jax.ShapeDtypeStruct((1, OWN), f32),
            jax.ShapeDtypeStruct((HIST, OWN), f32),
            jax.ShapeDtypeStruct((HIST, OWN), f32),
            jax.ShapeDtypeStruct((1, HIST), f32),
        ),
        in_specs=[vmem] * 3,
        out_specs=(vmem,) * 4,
        scratch_shapes=[
            pltpu.VMEM((ROWS, COLS), bf16),
            pltpu.VMEM((ROWS, 128), bf16),
            pltpu.VMEM((COLS, 128), bf16),
            pltpu.VMEM((3, HIST, ROWS), bf16),
            pltpu.VMEM((3, HIST, COLS), f32),
            pltpu.VMEM((3, PER_J, HIST, OWN), f32),
            pltpu.VMEM((8, COLS), f32),
            pltpu.VMEM((PER_J, 8, OWN), f32),
            pltpu.VMEM((HIST, OWN), f32),
            pltpu.VMEM((HIST, OWN), f32),
            pltpu.VMEM((2, PER_I, HIST, 128), f32),
            pltpu.VMEM((2, PER_J, HIST, 128), f32),
            pltpu.VMEM((2, PER_I, 8, 128), f32),
            pltpu.VMEM((2, PER_J, 8, 128), f32),
            *pair_i,
            *pair_j,
            *pair_j,
            *[dma((3, PER_I))] * 2,
            *[dma((3, PER_J))] * 2,
            *[dma((2, PER_I))] * 2,
            *[dma((2, PER_J))] * 2,
            *[dma((2, PER_I))] * 2,
            *[dma((2, PER_J))] * 2,
        ],
        compiler_params=pltpu.CompilerParams(
            collective_id=0, has_side_effects=True, vmem_limit_bytes=62 * 1024 * 1024
        ),
    )(embeddings, counts, raw_weights.reshape(1, HIST))
    return center.reshape(OWN), scale_u, scale_v, misfit.reshape(HIST)


def solution(mesh):
    placed = (P(("row", "col"), None), P(None, ("row", "col")), P())
    return jax.shard_map(
        shards,
        mesh=mesh,
        in_specs=placed,
        out_specs=(P(("row", "col")), P(None, ("row", "col")), P(None, ("row", "col")), P()),
        check_vma=False,
    )
```

```python
import functools

import jax
import jax.numpy as jnp
from jax import lax
from jax.experimental import pallas as pl
from jax.experimental.pallas import tpu as pltpu
from jax.sharding import PartitionSpec as P

GROUP_I = GROUP_J = ((0, 0), (0, 1), (1, 0), (3, 0), (1, 1), (3, 1), (2, 0), (2, 1))
MESH = pl.DeviceIdType.MESH
SLOPE = 14.426950408889634
HIST = 32
OWN = 384
PER_I, PER_J = 16, 8
ROWS, COLS = OWN * PER_I, OWN * PER_J
BUILD_I, BUILD_J = 1536, 768
PASS_J = 768
EARLY = 4


def body(
    total_pts,
    emb_hbm,
    counts_hbm,
    weights_hbm,
    center_ref,
    scale_u_ref,
    scale_v_ref,
    misfit_ref,
    tile,
    unit_i,
    unit_j,
    x_buf,
    y_part,
    y_recv,
    first_part,
    first_recv,
    target,
    v_first,
    emb_ref,
    counts_ref,
    weights_ref,
    wide_i,
    wide_j,
    moved_j,
    mass_i,
    raw_j,
    load_sem,
    ready,
    send_unit_i,
    recv_unit_i,
    send_unit_j,
    recv_unit_j,
    send_first,
    recv_first,
    send_x,
    recv_x,
    send_y,
    recv_y,
    send_wide_i,
    recv_wide_i,
    send_wide_j,
    recv_wide_j,
    send_mass_i,
    recv_mass_i,
    send_raw_j,
    recv_raw_j,
    send_moved_j,
    recv_moved_j,
):
    row, col = lax.axis_index("row"), lax.axis_index("col")
    x, core = lax.div(row, 2), lax.rem(row, 2)
    z, y = lax.div(col, 4), lax.rem(col, 4)

    def device(nx, ncore, nz, ny):
        return (nx * 2 + ncore, nz * 4 + ny)

    def device_i(k):
        dx, pair = GROUP_I[k // 2]
        ncore = 1 - core if k % 2 else core
        return device(lax.rem(x + 4 - dx, 4), ncore, z, y + 1 - 2 * lax.rem(y, 2) if pair else y)

    def device_j(k):
        dz, pair = GROUP_J[k]
        return device(x, core, lax.rem(z + 4 - dz, 4), 3 - y if pair else y)

    def owner_j(k):
        dz, pair = GROUP_J[k]
        return device(x, core, lax.rem(z + dz, 4), 3 - y if pair else y)

    sibling = device(x, 1 - core, z, y)
    near = [sibling] + [device_i(2 * s) for s in (1, 2, 3)] + [device_j(s) for s in (1, 2, 3)]

    def remote(device_id, src, dst, send, recv):
        return pltpu.make_async_remote_copy(
            src_ref=src, dst_ref=dst, send_sem=send, recv_sem=recv,
            device_id=device_id, device_id_type=MESH,
        )

    def tell_near(semaphore):
        for neighbour in near:
            pl.semaphore_signal(semaphore, inc=1, device_id=neighbour, device_id_type=MESH)

    def rows_of(k):
        return pl.ds(k * OWN, OWN)

    def lanes(value):
        return value[:, 0:128] + value[:, 128:256] + value[:, 256:384]

    barrier = pltpu.get_barrier_semaphore()
    tell_near(barrier)
    loads = [
        pltpu.make_async_copy(src, dst, load_sem.at[n])
        for n, (src, dst) in enumerate(((emb_hbm, emb_ref), (counts_hbm, counts_ref), (weights_hbm, weights_ref)))
    ]
    for load in loads:
        load.start()
    for load in loads:
        load.wait()

    emb = emb_ref[...]
    squares = jnp.sum(emb * emb, axis=1, keepdims=True)
    unit = (emb * lax.rsqrt(squares + 1e-6)).astype(jnp.bfloat16)
    unit_i[0:OWN, :] = unit
    unit_j[0:OWN, :] = unit
    counts = counts_ref[...].astype(jnp.float32)
    raw_weights = weights_ref[...]
    eye = lax.broadcasted_iota(jnp.int32, (HIST, HIST), 0) == lax.broadcasted_iota(
        jnp.int32, (HIST, HIST), 1
    )
    weights = jnp.sum(
        jnp.where(eye, raw_weights / jnp.sum(raw_weights), 0.0), axis=1, keepdims=True
    )
    first_part[...] = jnp.zeros_like(first_part)

    unit_copies_i = {
        k: remote(
            device_i(k), unit_i.at[rows_of(0)], unit_i.at[rows_of(k)],
            send_unit_i.at[k], recv_unit_i.at[k],
        )
        for k in (1, 2, 4, 6, 8, 10, 12, 14)
    }
    unit_copies_j = {
        k: remote(
            device_j(k), unit_j.at[rows_of(0)], unit_j.at[rows_of(k)],
            send_unit_j.at[k], recv_unit_j.at[k],
        )
        for k in range(1, PER_J)
    }
    forwards = {
        s: remote(
            sibling, unit_i.at[rows_of(2 * s)], unit_i.at[rows_of(2 * s + 1)],
            send_unit_i.at[2 * s + 1], recv_unit_i.at[2 * s + 1],
        )
        for s in range(1, 8)
    }

    def send_units(slots):
        for s in slots:
            unit_copies_i[2 * s].start()
            unit_copies_j[s].start()

    pl.semaphore_wait(barrier, len(near))
    unit_copies_i[1].start()
    send_units((1, 2, 3))
    tell_near(ready.at[0])
    pl.semaphore_wait(ready.at[0], len(near))
    send_units((4, 5, 6))
    tell_near(ready.at[1])
    pl.semaphore_wait(ready.at[1], len(near))
    send_units((7,))

    def exchange_j(buf, index, send, recv):
        return [
            remote(
                device_j(k), buf.at[index, 0], buf.at[index, k],
                send.at[index, k], recv.at[index, k],
            )
            for k in range(1, PER_J)
        ]

    def exchange_i(buf, index, send, recv):
        return [
            remote(
                device_i(k), buf.at[index, 0], buf.at[index, k],
                send.at[index, k], recv.at[index, k],
            )
            for k in range(1, PER_I)
        ]

    def start(copies):
        for copy in copies:
            copy.start()

    def received(copies):
        for copy in copies:
            copy.wait_recv()

    def sent(copies):
        for copy in copies:
            copy.wait_send()

    totals_j = exchange_j(wide_j, 0, send_wide_j, recv_wide_j)
    totals_i = exchange_i(wide_i, 0, send_wide_i, recv_wide_i)
    wide_j[0, 0] = lanes(counts)
    start(totals_j)

    def build(n, carry):
        t = (n >= 1).astype(jnp.int32) + (n >= 4).astype(jnp.int32) + (n >= 9).astype(jnp.int32)
        m = n - t * t
        down = (m <= t).astype(jnp.int32)
        i = down * t + (1 - down) * (m - t - 1)
        j = down * m + (1 - down) * t

        def forward(slots):
            for s in slots:
                unit_copies_i[2 * s].wait_recv()
                forwards[s].start()

        def arrived(slots):
            for s in slots:
                unit_copies_j[s].wait_recv()
                forwards[s].wait_recv()

        @pl.when(n == 0)
        def _():
            forward((1, 2, 3))
            unit_copies_i[1].wait_recv()
            arrived((1,))

        @pl.when(n == 1)
        def _():
            arrived((2, 3))

        @pl.when(n == 2)
        def _():
            forward((4, 5))

        @pl.when(n == 4)
        def _():
            arrived((4, 5))

        @pl.when(n == 7)
        def _():
            forward((6, 7))

        @pl.when(n == 9)
        def _():
            arrived((6, 7))
            received(totals_j)
            wide_i[0, 0] = jnp.sum(wide_j[0], axis=0)
            start(totals_i)

        at_i = pl.ds(pl.multiple_of(i * BUILD_I, BUILD_I), BUILD_I)
        at_j = pl.ds(pl.multiple_of(j * BUILD_J, BUILD_J), BUILD_J)
        gram = lax.dot_general(
            unit_i[at_i, :], unit_j[at_j, :], (((1,), (1,)), ((), ())),
            preferred_element_type=jnp.float32,
        )
        value = jnp.exp2(gram * SLOPE - SLOPE)
        tile[at_i, at_j] = value.astype(jnp.bfloat16)
        first_part[:, at_j] += jnp.sum(value.reshape(BUILD_I // 8, 8, BUILD_J), axis=0)
        return carry

    lax.fori_loop(0, 16, build, 0)

    first_copies = [
        remote(
            owner_j(k), first_part.at[:, rows_of(k)], first_recv.at[k],
            send_first.at[k], recv_first.at[k],
        )
        for k in range(1, PER_J)
    ]
    start(first_copies)
    first_recv[0] = first_part[:, 0:OWN]
    sent(unit_copies_i.values())
    sent(unit_copies_j.values())
    sent(forwards.values())
    sent(totals_j)
    received(totals_i)
    totals = jnp.sum(jnp.sum(wide_i[0], axis=0), axis=1, keepdims=True)
    target[...] = counts * (total_pts / totals)
    received(first_copies)
    row_sum = jnp.sum(jnp.sum(first_recv[...], axis=0), axis=0, keepdims=True)

    def run_pass(index, value, before, between):
        x_buf[index, :, 0:OWN] = value.astype(jnp.bfloat16)
        gather = [
            remote(
                device_i(k), x_buf.at[index, :, rows_of(0)], x_buf.at[index, :, rows_of(k)],
                send_x.at[index, k], recv_x.at[index, k],
            )
            for k in range(1, PER_I)
        ]
        start(gather)
        copies = {
            k: remote(
                owner_j(k), y_part.at[index, :, rows_of(k)], y_recv.at[index, k],
                send_y.at[index, k], recv_y.at[index, k],
            )
            for k in range(1, PER_J)
        }
        y_part[index] = jnp.zeros_like(y_part[index])
        before()

        def by_rows(s, carry):
            for which in range(EARLY):

                @pl.when(s == which)
                def _():
                    received(gather[max(2 * which - 1, 0) : 2 * which + 1])

            at = pl.ds(pl.multiple_of(s * 2 * OWN, 2 * OWN), 2 * OWN)
            y_part[index] += jnp.dot(
                x_buf[index, :, at], tile[at, :], preferred_element_type=jnp.float32
            )
            return carry

        lax.fori_loop(0, EARLY, by_rows, 0)
        between()
        received(gather[2 * EARLY - 1 :])
        late = pl.ds(EARLY * 2 * OWN, ROWS - EARLY * 2 * OWN)

        def by_columns(n, carry):
            q = 3 - n
            at = pl.ds(pl.multiple_of(q * PASS_J, PASS_J), PASS_J)
            y_part[index, :, at] += jnp.dot(
                x_buf[index, :, late], tile[late, at], preferred_element_type=jnp.float32
            )
            for which in range(4):

                @pl.when(q == which)
                def _():
                    for k in (2 * which + 1, 2 * which):
                        if k:
                            copies[k].start()

            return carry

        lax.fori_loop(0, 4, by_columns, 0)
        y_recv[index, 0] = y_part[index, :, 0:OWN]
        sent(gather)
        received(copies.values())
        return jnp.sum(y_recv[index], axis=0), lambda: sent(copies.values())

    def raw(col_sum):
        return jnp.exp(jnp.sum(weights * jnp.log(col_sum), axis=0, keepdims=True))

    def scalar(value):
        return jnp.sum(value[0:1, :], axis=1, keepdims=True)

    def nothing():
        return None

    def first_sent():
        sent(first_copies)
        sent(totals_i)

    col_sum, y_sent = run_pass(0, target[...] / row_sum, first_sent, nothing)
    raw_center = raw(col_sum)
    v_first[...] = raw_center / col_sum
    mass_copies_j = exchange_j(raw_j, 0, send_raw_j, recv_raw_j)
    mass_copies_i = exchange_i(mass_i, 0, send_mass_i, recv_mass_i)

    def mass_begin():
        raw_j[0, 0] = jnp.broadcast_to(raw_center, (8, OWN))
        start(mass_copies_j)
        y_sent()

    def mass_next():
        received(mass_copies_j)
        mass_i[0, 0] = lanes(jnp.sum(raw_j[0], axis=0))
        start(mass_copies_i)
        sent(mass_copies_j)

    row_sum, y_sent = run_pass(1, v_first[...], mass_begin, mass_next)
    received(mass_copies_i)
    factor = total_pts / scalar(jnp.sum(mass_i[0], axis=0))
    scale_u = target[...] / (row_sum * factor)
    scale_u_ref[...] = scale_u
    scale_v = v_first[...] * factor

    def second_sent():
        sent(mass_copies_i)
        y_sent()

    col_sum, y_sent = run_pass(2, scale_u, second_sent, nothing)
    raw_center = raw(col_sum)
    raw_j[1, 0] = jnp.broadcast_to(raw_center, (8, OWN))
    mass_copies_j = exchange_j(raw_j, 1, send_raw_j, recv_raw_j)
    start(mass_copies_j)
    mass_copies_i = exchange_i(mass_i, 1, send_mass_i, recv_mass_i)
    error_copies_j = exchange_j(moved_j, 0, send_moved_j, recv_moved_j)
    error_copies_i = exchange_i(wide_i, 1, send_wide_i, recv_wide_i)
    moved_j[0, 0] = scale_v * col_sum
    start(error_copies_j)
    y_sent()
    received(mass_copies_j)
    mass_i[1, 0] = lanes(jnp.sum(raw_j[1], axis=0))
    start(mass_copies_i)
    sent(mass_copies_j)
    received(error_copies_j)
    sent(error_copies_j)
    received(mass_copies_i)
    factor = total_pts / scalar(jnp.sum(mass_i[1], axis=0))
    error = jnp.zeros((HIST, OWN), jnp.float32)
    for k in range(PER_J):
        error += jnp.abs(moved_j[0, k] - raw_j[1, k, 0:1, :] * factor)
    wide_i[1, 0] = lanes(error)
    start(error_copies_i)
    center = raw_center * factor
    center_ref[...] = center
    scale_v_ref[...] = center / col_sum
    sent(mass_copies_i)
    received(error_copies_i)
    misfit = jnp.sum(jnp.sum(wide_i[1], axis=0), axis=1, keepdims=True) / total_pts
    misfit_ref[...] = jnp.sum(jnp.where(eye, misfit, 0.0), axis=0, keepdims=True)
    sent(error_copies_i)


def shards(embeddings, counts, raw_weights):
    total_pts = embeddings.shape[0] * lax.axis_size("row") * lax.axis_size("col")
    vmem = pl.BlockSpec(memory_space=pltpu.VMEM)
    f32, bf16, dma = jnp.float32, jnp.bfloat16, pltpu.SemaphoreType.DMA
    pair_i, pair_j = [dma((PER_I,))] * 2, [dma((PER_J,))] * 2
    center, scale_u, scale_v, misfit = pl.pallas_call(
        functools.partial(body, total_pts),
        out_shape=(
            jax.ShapeDtypeStruct((1, OWN), f32),
            jax.ShapeDtypeStruct((HIST, OWN), f32),
            jax.ShapeDtypeStruct((HIST, OWN), f32),
            jax.ShapeDtypeStruct((1, HIST), f32),
        ),
        in_specs=[pl.BlockSpec(memory_space=pl.ANY)] * 3,
        out_specs=(vmem,) * 4,
        scratch_shapes=[
            pltpu.VMEM((ROWS, COLS), bf16),
            pltpu.VMEM((ROWS, 128), bf16),
            pltpu.VMEM((COLS, 128), bf16),
            pltpu.VMEM((3, HIST, ROWS), bf16),
            pltpu.VMEM((3, HIST, COLS), f32),
            pltpu.VMEM((3, PER_J, HIST, OWN), f32),
            pltpu.VMEM((8, COLS), f32),
            pltpu.VMEM((PER_J, 8, OWN), f32),
            pltpu.VMEM((HIST, OWN), f32),
            pltpu.VMEM((HIST, OWN), f32),
            pltpu.VMEM((OWN, 128), f32),
            pltpu.VMEM((HIST, OWN), jnp.int32),
            pltpu.VMEM((1, HIST), f32),
            pltpu.VMEM((2, PER_I, HIST, 128), f32),
            pltpu.VMEM((1, PER_J, HIST, 128), f32),
            pltpu.VMEM((1, PER_J, HIST, OWN), f32),
            pltpu.VMEM((2, PER_I, 8, 128), f32),
            pltpu.VMEM((2, PER_J, 8, OWN), f32),
            dma((3,)),
            pltpu.SemaphoreType.REGULAR((2,)),
            *pair_i,
            *pair_j,
            *pair_j,
            *[dma((3, PER_I))] * 2,
            *[dma((3, PER_J))] * 2,
            *[dma((2, PER_I))] * 2,
            *[dma((1, PER_J))] * 2,
            *[dma((2, PER_I))] * 2,
            *[dma((2, PER_J))] * 2,
            *[dma((1, PER_J))] * 2,
        ],
        compiler_params=pltpu.CompilerParams(
            collective_id=0, has_side_effects=True, vmem_limit_bytes=62 * 1024 * 1024
        ),
    )(embeddings, counts, raw_weights.reshape(1, HIST))
    return center.reshape(OWN), scale_u, scale_v, misfit.reshape(HIST)


def solution(mesh):
    placed = (P(("row", "col"), None), P(None, ("row", "col")), P())
    return jax.shard_map(
        shards,
        mesh=mesh,
        in_specs=placed,
        out_specs=(P(("row", "col")), P(None, ("row", "col")), P(None, ("row", "col")), P()),
        check_vma=False,
    )
```

```python
import functools

import jax
import jax.numpy as jnp
from jax import lax
from jax.experimental import pallas as pl
from jax.experimental.pallas import tpu as pltpu
from jax.sharding import PartitionSpec as P

GROUP_I = GROUP_J = ((0, 0), (0, 1), (1, 0), (3, 0), (1, 1), (3, 1), (2, 0), (2, 1))
MESH = pl.DeviceIdType.MESH
SLOPE = 14.426950408889634
HIST = 32
OWN = 384
PER_I, PER_J = 16, 8
ROWS, COLS = OWN * PER_I, OWN * PER_J
BUILD_I, BUILD_J = 1536, 768
PASS_J = 768
EARLY = 6


def body(
    total_pts,
    emb_hbm,
    counts_hbm,
    weights_hbm,
    center_ref,
    scale_u_ref,
    scale_v_ref,
    misfit_ref,
    tile,
    unit_i,
    unit_j,
    x_buf,
    y_part,
    y_send,
    y_recv,
    first_part,
    first_recv,
    target,
    v_first,
    emb_ref,
    counts_ref,
    weights_ref,
    wide_i,
    wide_j,
    moved_j,
    mass_i,
    raw_j,
    load_sem,
    ready,
    send_unit_i,
    recv_unit_i,
    send_unit_j,
    recv_unit_j,
    send_first,
    recv_first,
    send_x,
    recv_x,
    send_y,
    recv_y,
    send_wide_i,
    recv_wide_i,
    send_wide_j,
    recv_wide_j,
    send_mass_i,
    recv_mass_i,
    send_raw_j,
    recv_raw_j,
    send_moved_j,
    recv_moved_j,
):
    row, col = lax.axis_index("row"), lax.axis_index("col")
    x, core = lax.div(row, 2), lax.rem(row, 2)
    z, y = lax.div(col, 4), lax.rem(col, 4)

    def device(nx, ncore, nz, ny):
        return (nx * 2 + ncore, nz * 4 + ny)

    def device_i(k):
        dx, pair = GROUP_I[k // 2]
        ncore = 1 - core if k % 2 else core
        return device(lax.rem(x + 4 - dx, 4), ncore, z, y + 1 - 2 * lax.rem(y, 2) if pair else y)

    def device_j(k):
        dz, pair = GROUP_J[k]
        return device(x, core, lax.rem(z + 4 - dz, 4), 3 - y if pair else y)

    def owner_j(k):
        dz, pair = GROUP_J[k]
        return device(x, core, lax.rem(z + dz, 4), 3 - y if pair else y)

    sibling = device(x, 1 - core, z, y)
    near = [sibling] + [device_i(2 * s) for s in (1, 2, 3)] + [device_j(s) for s in (1, 2, 3)]

    def remote(device_id, src, dst, send, recv):
        return pltpu.make_async_remote_copy(
            src_ref=src, dst_ref=dst, send_sem=send, recv_sem=recv,
            device_id=device_id, device_id_type=MESH,
        )

    def tell_near(semaphore):
        for neighbour in near:
            pl.semaphore_signal(semaphore, inc=1, device_id=neighbour, device_id_type=MESH)

    def rows_of(k):
        return pl.ds(k * OWN, OWN)

    def lanes(value):
        return value[:, 0:128] + value[:, 128:256] + value[:, 256:384]

    loads = [
        pltpu.make_async_copy(src, dst, load_sem.at[n])
        for n, (src, dst) in enumerate(((emb_hbm, emb_ref), (counts_hbm, counts_ref), (weights_hbm, weights_ref)))
    ]
    for load in loads:
        load.start()
    barrier = pltpu.get_barrier_semaphore()
    tell_near(barrier)
    loads[0].wait()

    emb = emb_ref[...]
    squares = jnp.sum(emb * emb, axis=1, keepdims=True)
    unit = (emb * lax.rsqrt(squares + 1e-6)).astype(jnp.bfloat16)
    unit_i[0:OWN, :] = unit
    unit_j[0:OWN, :] = unit

    unit_copies_i = {
        k: remote(
            device_i(k), unit_i.at[rows_of(0)], unit_i.at[rows_of(k)],
            send_unit_i.at[k], recv_unit_i.at[k],
        )
        for k in (1, 2, 4, 6, 8, 10, 12, 14)
    }
    unit_copies_j = {
        k: remote(
            device_j(k), unit_j.at[rows_of(0)], unit_j.at[rows_of(k)],
            send_unit_j.at[k], recv_unit_j.at[k],
        )
        for k in range(1, PER_J)
    }
    forwards = {
        s: remote(
            sibling, unit_i.at[rows_of(2 * s)], unit_i.at[rows_of(2 * s + 1)],
            send_unit_i.at[2 * s + 1], recv_unit_i.at[2 * s + 1],
        )
        for s in range(1, 8)
    }

    def send_units(slots):
        for s in slots:
            unit_copies_i[2 * s].start()
            unit_copies_j[s].start()

    pl.semaphore_wait(barrier, len(near))
    unit_copies_i[1].start()
    send_units((1, 2, 3))
    tell_near(ready.at[0])
    pl.semaphore_wait(ready.at[0], len(near))
    send_units((4, 5, 6))
    tell_near(ready.at[1])
    pl.semaphore_wait(ready.at[1], len(near))
    send_units((7,))

    def exchange_j(buf, index, send, recv):
        return [
            remote(
                device_j(k), buf.at[index, 0], buf.at[index, k],
                send.at[index, k], recv.at[index, k],
            )
            for k in range(1, PER_J)
        ]

    def exchange_i(buf, index, send, recv):
        return [
            remote(
                device_i(k), buf.at[index, 0], buf.at[index, k],
                send.at[index, k], recv.at[index, k],
            )
            for k in range(1, PER_I)
        ]

    def start(copies):
        for copy in copies:
            copy.start()

    def received(copies):
        for copy in copies:
            copy.wait_recv()

    def sent(copies):
        for copy in copies:
            copy.wait_send()

    loads[1].wait()
    loads[2].wait()
    counts = counts_ref[...].astype(jnp.float32)
    raw_weights = weights_ref[...]
    eye = lax.broadcasted_iota(jnp.int32, (HIST, HIST), 0) == lax.broadcasted_iota(
        jnp.int32, (HIST, HIST), 1
    )
    weights = jnp.sum(
        jnp.where(eye, raw_weights / jnp.sum(raw_weights), 0.0), axis=1, keepdims=True
    )
    totals_j = exchange_j(wide_j, 0, send_wide_j, recv_wide_j)
    totals_i = exchange_i(wide_i, 0, send_wide_i, recv_wide_i)
    wide_j[0, 0] = lanes(counts)
    start(totals_j)
    first_part[...] = jnp.zeros_like(first_part)
    first_copies = {
        k: remote(
            owner_j(k), first_part.at[:, rows_of(k)], first_recv.at[k],
            send_first.at[k], recv_first.at[k],
        )
        for k in range(1, PER_J)
    }

    def build(n, carry):
        t = (n >= 1).astype(jnp.int32) + (n >= 4).astype(jnp.int32) + (n >= 9).astype(jnp.int32)
        m = n - t * t
        down = (m < t).astype(jnp.int32)
        i = down * m + (1 - down) * t
        j = down * t + (1 - down) * (2 * t - m)

        def forward(slots):
            for s in slots:
                unit_copies_i[2 * s].wait_recv()
                forwards[s].start()

        def columns_arrived(slots):
            for s in slots:
                unit_copies_j[s].wait_recv()

        def rows_arrived(slots):
            for s in slots:
                forwards[s].wait_recv()

        @pl.when(n == 0)
        def _():
            forward((1,))
            unit_copies_i[1].wait_recv()
            columns_arrived((1,))
            forward((2, 3))
            rows_arrived((1,))

        @pl.when(n == 1)
        def _():
            columns_arrived((2, 3))

        @pl.when(n == 2)
        def _():
            rows_arrived((2, 3))

        @pl.when(n == 4)
        def _():
            columns_arrived((4, 5))
            forward((4, 5))

        @pl.when(n == 6)
        def _():
            rows_arrived((4, 5))
            received(totals_j)
            wide_i[0, 0] = jnp.sum(wide_j[0], axis=0)
            start(totals_i)

        @pl.when(n == 9)
        def _():
            columns_arrived((6, 7))
            forward((6, 7))

        @pl.when(n == 12)
        def _():
            rows_arrived((6, 7))

        at_i = pl.ds(pl.multiple_of(i * BUILD_I, BUILD_I), BUILD_I)
        at_j = pl.ds(pl.multiple_of(j * BUILD_J, BUILD_J), BUILD_J)
        gram = lax.dot_general(
            unit_i[at_i, :], unit_j[at_j, :], (((1,), (1,)), ((), ())),
            preferred_element_type=jnp.float32,
        )
        value = jnp.exp2(gram * SLOPE - SLOPE)
        tile[at_i, at_j] = value.astype(jnp.bfloat16)
        first_part[:, at_j] += jnp.sum(value.reshape(BUILD_I // 8, 8, BUILD_J), axis=0)
        for which in range(4):

            @pl.when(n == 15 - which)
            def _():
                for k in (2 * which + 1, 2 * which):
                    if k:
                        first_copies[k].start()

        return carry

    lax.fori_loop(0, 16, build, 0)

    first_recv[0] = first_part[:, 0:OWN]
    sent(unit_copies_i.values())
    sent(unit_copies_j.values())
    sent(forwards.values())
    sent(totals_j)
    received(totals_i)
    totals = jnp.sum(jnp.sum(wide_i[0], axis=0), axis=1, keepdims=True)
    target[...] = counts * (total_pts / totals)
    received(first_copies.values())
    row_sum = jnp.sum(jnp.sum(first_recv[...], axis=0), axis=0, keepdims=True)

    def run_pass(index, value, before, between):
        x_buf[index, :, 0:OWN] = value.astype(jnp.bfloat16)
        gather = [
            remote(
                device_i(k), x_buf.at[index, :, rows_of(0)], x_buf.at[index, :, rows_of(k)],
                send_x.at[index, k], recv_x.at[index, k],
            )
            for k in range(1, PER_I)
        ]
        start(gather)
        copies = {
            k: remote(
                owner_j(k), y_send.at[index, :, rows_of(k)], y_recv.at[index, k],
                send_y.at[index, k], recv_y.at[index, k],
            )
            for k in range(1, PER_J)
        }
        y_part[...] = jnp.zeros_like(y_part)
        before()

        def by_rows(s, carry):
            for which in range(EARLY):

                @pl.when(s == which)
                def _():
                    received(gather[max(2 * which - 1, 0) : 2 * which + 1])

            at = pl.ds(pl.multiple_of(s * 2 * OWN, 2 * OWN), 2 * OWN)
            y_part[...] += jnp.dot(
                x_buf[index, :, at], tile[at, :], preferred_element_type=jnp.float32
            )
            return carry

        lax.fori_loop(0, EARLY, by_rows, 0)
        between()
        received(gather[2 * EARLY - 1 :])
        late = pl.ds(EARLY * 2 * OWN, ROWS - EARLY * 2 * OWN)

        def by_columns(n, carry):
            q = 3 - n
            at = pl.ds(pl.multiple_of(q * PASS_J, PASS_J), PASS_J)
            value = y_part[:, at] + jnp.dot(
                x_buf[index, :, late], tile[late, at], preferred_element_type=jnp.float32
            )
            y_part[:, at] = value
            y_send[index, :, at] = value.astype(jnp.bfloat16)
            for which in range(4):

                @pl.when(q == which)
                def _():
                    for k in (2 * which + 1, 2 * which):
                        if k:
                            copies[k].start()

            return carry

        lax.fori_loop(0, 4, by_columns, 0)
        sent(gather)
        received(copies.values())
        total = y_part[:, 0:OWN]
        for k in range(1, PER_J):
            total += y_recv[index, k].astype(jnp.float32)
        return total, lambda: sent(copies.values())

    def raw(col_sum):
        return jnp.exp(jnp.sum(weights * jnp.log(col_sum), axis=0, keepdims=True))

    def scalar(value):
        return jnp.sum(value[0:1, :], axis=1, keepdims=True)

    def nothing():
        return None

    def first_sent():
        sent(first_copies.values())
        sent(totals_i)

    col_sum, y_sent = run_pass(0, target[...] / row_sum, first_sent, nothing)
    raw_center = raw(col_sum)
    v_first[...] = raw_center / col_sum
    mass_copies_j = exchange_j(raw_j, 0, send_raw_j, recv_raw_j)
    mass_copies_i = exchange_i(mass_i, 0, send_mass_i, recv_mass_i)

    def mass_begin():
        raw_j[0, 0] = jnp.broadcast_to(raw_center, (8, OWN))
        start(mass_copies_j)
        y_sent()

    def mass_next():
        received(mass_copies_j)
        mass_i[0, 0] = lanes(jnp.sum(raw_j[0], axis=0))
        start(mass_copies_i)
        sent(mass_copies_j)

    row_sum, y_sent = run_pass(1, v_first[...], mass_begin, mass_next)
    received(mass_copies_i)
    factor = total_pts / scalar(jnp.sum(mass_i[0], axis=0))
    scale_u = target[...] / (row_sum * factor)
    scale_u_ref[...] = scale_u
    scale_v = v_first[...] * factor

    def second_sent():
        sent(mass_copies_i)
        y_sent()

    col_sum, y_sent = run_pass(2, scale_u, second_sent, nothing)
    raw_center = raw(col_sum)
    raw_j[1, 0] = jnp.broadcast_to(raw_center, (8, OWN))
    mass_copies_j = exchange_j(raw_j, 1, send_raw_j, recv_raw_j)
    start(mass_copies_j)
    mass_copies_i = exchange_i(mass_i, 1, send_mass_i, recv_mass_i)
    error_copies_j = exchange_j(moved_j, 0, send_moved_j, recv_moved_j)
    error_copies_i = exchange_i(mass_i, 2, send_mass_i, recv_mass_i)
    moved_j[0, 0] = scale_v * col_sum
    start(error_copies_j)
    y_sent()
    received(mass_copies_j)
    mass_i[1, 0] = lanes(jnp.sum(raw_j[1], axis=0))
    start(mass_copies_i)
    sent(mass_copies_j)
    received(error_copies_j)
    sent(error_copies_j)
    received(mass_copies_i)
    factor = total_pts / scalar(jnp.sum(mass_i[1], axis=0))
    error = jnp.zeros((HIST, OWN), jnp.float32)
    for k in range(PER_J):
        error += jnp.abs(moved_j[0, k] - raw_j[1, k, 0:1, :] * factor)
    error = jnp.sum(lanes(error), axis=1, keepdims=True) / total_pts
    wide_eye = lax.broadcasted_iota(jnp.int32, (HIST, 128), 0) == lax.broadcasted_iota(
        jnp.int32, (HIST, 128), 1
    )
    mass_i[2, 0] = jnp.broadcast_to(
        jnp.sum(jnp.where(wide_eye, error, 0.0), axis=0, keepdims=True), (8, 128)
    )
    start(error_copies_i)
    center = raw_center * factor
    center_ref[...] = center
    scale_v_ref[...] = center / col_sum
    sent(mass_copies_i)
    received(error_copies_i)
    misfit_ref[...] = jnp.sum(mass_i[2], axis=0)[0:1, 0:HIST]
    sent(error_copies_i)


def shards(embeddings, counts, raw_weights):
    total_pts = embeddings.shape[0] * lax.axis_size("row") * lax.axis_size("col")
    vmem = pl.BlockSpec(memory_space=pltpu.VMEM)
    f32, bf16, dma = jnp.float32, jnp.bfloat16, pltpu.SemaphoreType.DMA
    pair_i, pair_j = [dma((PER_I,))] * 2, [dma((PER_J,))] * 2
    center, scale_u, scale_v, misfit = pl.pallas_call(
        functools.partial(body, total_pts),
        out_shape=(
            jax.ShapeDtypeStruct((1, OWN), f32),
            jax.ShapeDtypeStruct((HIST, OWN), f32),
            jax.ShapeDtypeStruct((HIST, OWN), f32),
            jax.ShapeDtypeStruct((1, HIST), f32),
        ),
        in_specs=[pl.BlockSpec(memory_space=pl.ANY)] * 3,
        out_specs=(vmem,) * 4,
        scratch_shapes=[
            pltpu.VMEM((ROWS, COLS), bf16),
            pltpu.VMEM((ROWS, 128), bf16),
            pltpu.VMEM((COLS, 128), bf16),
            pltpu.VMEM((3, HIST, ROWS), bf16),
            pltpu.VMEM((HIST, COLS), f32),
            pltpu.VMEM((3, HIST, COLS), bf16),
            pltpu.VMEM((3, PER_J, HIST, OWN), bf16),
            pltpu.VMEM((8, COLS), f32),
            pltpu.VMEM((PER_J, 8, OWN), f32),
            pltpu.VMEM((HIST, OWN), f32),
            pltpu.VMEM((HIST, OWN), f32),
            pltpu.VMEM((OWN, 128), f32),
            pltpu.VMEM((HIST, OWN), jnp.int32),
            pltpu.VMEM((1, HIST), f32),
            pltpu.VMEM((1, PER_I, HIST, 128), f32),
            pltpu.VMEM((1, PER_J, HIST, 128), f32),
            pltpu.VMEM((1, PER_J, HIST, OWN), f32),
            pltpu.VMEM((3, PER_I, 8, 128), f32),
            pltpu.VMEM((2, PER_J, 8, OWN), f32),
            dma((3,)),
            pltpu.SemaphoreType.REGULAR((2,)),
            *pair_i,
            *pair_j,
            *pair_j,
            *[dma((3, PER_I))] * 2,
            *[dma((3, PER_J))] * 2,
            *[dma((1, PER_I))] * 2,
            *[dma((1, PER_J))] * 2,
            *[dma((3, PER_I))] * 2,
            *[dma((2, PER_J))] * 2,
            *[dma((1, PER_J))] * 2,
        ],
        compiler_params=pltpu.CompilerParams(
            collective_id=0, has_side_effects=True, vmem_limit_bytes=62 * 1024 * 1024
        ),
    )(embeddings, counts, raw_weights.reshape(1, HIST))
    return center.reshape(OWN), scale_u, scale_v, misfit.reshape(HIST)


def solution(mesh):
    placed = (P(("row", "col"), None), P(None, ("row", "col")), P())
    return jax.shard_map(
        shards,
        mesh=mesh,
        in_specs=placed,
        out_specs=(P(("row", "col")), P(None, ("row", "col")), P(None, ("row", "col")), P()),
        check_vma=False,
    )
```

```python
import functools

import jax
import jax.numpy as jnp
from jax import lax
from jax.experimental import pallas as pl
from jax.experimental.pallas import tpu as pltpu
from jax.sharding import PartitionSpec as P

GROUP_I = ((0, 0), (1, 0), (3, 0), (0, 1), (3, 1), (2, 0), (1, 1), (2, 1))
GROUP_J = ((0, 0), (0, 1), (3, 0), (1, 0), (3, 1), (2, 0), (1, 1), (2, 1))
MESH = pl.DeviceIdType.MESH
SLOPE = 14.426950408889634
HIST = 32
OWN = 384
PER_I, PER_J = 16, 8
ROWS, COLS = OWN * PER_I, OWN * PER_J
BUILD_I, BUILD_J = 1536, 768
PASS_J = 768
EARLY = 3


def body(
    total_pts,
    emb_hbm,
    counts_hbm,
    weights_hbm,
    center_hbm,
    scale_u_hbm,
    scale_v_hbm,
    misfit_hbm,
    tile,
    unit_i,
    unit_j,
    x_buf,
    y_part,
    y_send,
    y_recv,
    first_part,
    first_recv,
    target,
    v_first,
    emb_ref,
    counts_ref,
    weights_ref,
    wide_i,
    wide_j,
    moved_j,
    mass_i,
    raw_j,
    center_ref,
    scale_u_ref,
    scale_v_ref,
    misfit_ref,
    load_sem,
    store_sem,
    ready,
    send_unit_i,
    recv_unit_i,
    send_unit_j,
    recv_unit_j,
    send_first,
    recv_first,
    send_x,
    recv_x,
    send_y,
    recv_y,
    send_wide_i,
    recv_wide_i,
    send_wide_j,
    recv_wide_j,
    send_mass_i,
    recv_mass_i,
    send_raw_j,
    recv_raw_j,
    send_moved_j,
    recv_moved_j,
):
    row, col = lax.axis_index("row"), lax.axis_index("col")
    x, core = lax.div(row, 2), lax.rem(row, 2)
    z, y = lax.div(col, 4), lax.rem(col, 4)

    def device(nx, ncore, nz, ny):
        return (nx * 2 + ncore, nz * 4 + ny)

    def device_i(k):
        dx, pair = GROUP_I[k // 2]
        ncore = 1 - core if k % 2 else core
        return device(lax.rem(x + 4 - dx, 4), ncore, z, y + 1 - 2 * lax.rem(y, 2) if pair else y)

    def device_j(k):
        dz, pair = GROUP_J[k]
        return device(x, core, lax.rem(z + 4 - dz, 4), 3 - y if pair else y)

    def owner_j(k):
        dz, pair = GROUP_J[k]
        return device(x, core, lax.rem(z + dz, 4), 3 - y if pair else y)

    sibling = device(x, 1 - core, z, y)
    near = [sibling] + [device_i(2 * s) for s in (1, 2, 3)] + [device_j(s) for s in (1, 2, 3)]

    def remote(device_id, src, dst, send, recv):
        return pltpu.make_async_remote_copy(
            src_ref=src, dst_ref=dst, send_sem=send, recv_sem=recv,
            device_id=device_id, device_id_type=MESH,
        )

    def start(copies):
        for copy in copies:
            copy.start()

    def received(copies):
        for copy in copies:
            copy.wait_recv()

    def sent(copies):
        for copy in copies:
            copy.wait_send()

    def tell_near(semaphore):
        for neighbour in near:
            pl.semaphore_signal(semaphore, inc=1, device_id=neighbour, device_id_type=MESH)

    def rows_of(k):
        return pl.ds(k * OWN, OWN)

    def lanes(value):
        return value[:, 0:128] + value[:, 128:256] + value[:, 256:384]

    loads = [
        pltpu.make_async_copy(src, dst, load_sem.at[n])
        for n, (src, dst) in enumerate(((emb_hbm, emb_ref), (counts_hbm, counts_ref), (weights_hbm, weights_ref)))
    ]
    for load in loads:
        load.start()
    barrier = pltpu.get_barrier_semaphore()
    tell_near(barrier)
    loads[0].wait()

    emb = emb_ref[...]
    squares = jnp.sum(emb * emb, axis=1, keepdims=True)
    unit = (emb * lax.rsqrt(squares + 1e-6)).astype(jnp.bfloat16)
    unit_i[0:OWN, :] = unit
    unit_j[0:OWN, :] = unit

    unit_copies_i = {
        k: remote(
            device_i(k), unit_i.at[rows_of(0)], unit_i.at[rows_of(k)],
            send_unit_i.at[k], recv_unit_i.at[k],
        )
        for k in (1, 2, 4, 6, 8, 10, 12, 14)
    }
    unit_copies_j = {
        k: remote(
            device_j(k), unit_j.at[rows_of(0)], unit_j.at[rows_of(k)],
            send_unit_j.at[k], recv_unit_j.at[k],
        )
        for k in range(1, PER_J)
    }
    forwards = {
        s: remote(
            sibling, unit_i.at[rows_of(2 * s)], unit_i.at[rows_of(2 * s + 1)],
            send_unit_i.at[2 * s + 1], recv_unit_i.at[2 * s + 1],
        )
        for s in range(1, 8)
    }

    def send_units(slots):
        for s in slots:
            unit_copies_i[2 * s].start()
            unit_copies_j[s].start()

    pl.semaphore_wait(barrier, len(near))
    unit_copies_i[1].start()
    send_units((1, 2, 3))
    tell_near(ready.at[0])
    pl.semaphore_wait(ready.at[0], len(near))
    sent([unit_copies_i[k] for k in (2, 4, 6)])
    sent([unit_copies_j[k] for k in (1, 2, 3)])
    send_units((4, 5, 6))
    tell_near(ready.at[1])
    pl.semaphore_wait(ready.at[1], len(near))
    send_units((7,))

    def exchange_j(buf, index, send, recv):
        return [
            remote(
                device_j(k), buf.at[index, 0], buf.at[index, k],
                send.at[index, k], recv.at[index, k],
            )
            for k in range(1, PER_J)
        ]

    def exchange_i(buf, index, send, recv):
        return [
            remote(
                device_i(k), buf.at[index, 0], buf.at[index, k],
                send.at[index, k], recv.at[index, k],
            )
            for k in range(1, PER_I)
        ]

    loads[1].wait()
    loads[2].wait()
    counts = counts_ref[...].astype(jnp.float32)
    raw_weights = weights_ref[...]
    eye = lax.broadcasted_iota(jnp.int32, (HIST, HIST), 0) == lax.broadcasted_iota(
        jnp.int32, (HIST, HIST), 1
    )
    weights = jnp.sum(
        jnp.where(eye, raw_weights / jnp.sum(raw_weights), 0.0), axis=1, keepdims=True
    )
    totals_j = exchange_j(wide_j, 0, send_wide_j, recv_wide_j)
    totals_i = exchange_i(wide_i, 0, send_wide_i, recv_wide_i)
    wide_j[0, 0] = lanes(counts)
    start(totals_j)
    first_part[...] = jnp.zeros_like(first_part)
    first_copies = {
        k: remote(
            owner_j(k), first_part.at[:, rows_of(k)], first_recv.at[k],
            send_first.at[k], recv_first.at[k],
        )
        for k in range(1, PER_J)
    }

    def build(n, carry):
        t = (n >= 1).astype(jnp.int32) + (n >= 4).astype(jnp.int32) + (n >= 9).astype(jnp.int32)
        m = n - t * t
        down = (m < t).astype(jnp.int32)
        i = down * m + (1 - down) * t
        j = down * t + (1 - down) * (2 * t - m)

        def forward(slots):
            for s in slots:
                unit_copies_i[2 * s].wait_recv()
                forwards[s].start()

        def columns_arrived(slots):
            for s in slots:
                unit_copies_j[s].wait_recv()

        def rows_arrived(slots):
            for s in slots:
                forwards[s].wait_recv()

        @pl.when(n == 0)
        def _():
            forward((1,))
            unit_copies_i[1].wait_recv()
            columns_arrived((1,))
            forward((2, 3))
            rows_arrived((1,))

        @pl.when(n == 1)
        def _():
            columns_arrived((2, 3))

        @pl.when(n == 2)
        def _():
            rows_arrived((2, 3))

        @pl.when(n == 4)
        def _():
            columns_arrived((4, 5))
            forward((4, 5))

        @pl.when(n == 6)
        def _():
            rows_arrived((4, 5))
            received(totals_j)
            wide_i[0, 0] = jnp.sum(wide_j[0], axis=0)
            start(totals_i)

        @pl.when(n == 9)
        def _():
            columns_arrived((6, 7))
            forward((6, 7))

        @pl.when(n == 12)
        def _():
            rows_arrived((6, 7))

        at_i = pl.ds(pl.multiple_of(i * BUILD_I, BUILD_I), BUILD_I)
        at_j = pl.ds(pl.multiple_of(j * BUILD_J, BUILD_J), BUILD_J)
        gram = lax.dot_general(
            unit_i[at_i, :], unit_j[at_j, :], (((1,), (1,)), ((), ())),
            preferred_element_type=jnp.float32,
        )
        value = jnp.exp2(gram * SLOPE - SLOPE)
        tile[at_i, at_j] = value.astype(jnp.bfloat16)
        first_part[:, at_j] += jnp.sum(value.reshape(BUILD_I // 8, 8, BUILD_J), axis=0)
        for which in range(4):

            @pl.when(n == 15 - which)
            def _():
                for k in (2 * which + 1, 2 * which):
                    if k:
                        first_copies[k].start()

        return carry

    lax.fori_loop(0, 16, build, 0)

    first_recv[0] = first_part[:, 0:OWN]
    sent([unit_copies_i[k] for k in (1, 8, 10, 12, 14)])
    sent([unit_copies_j[k] for k in (4, 5, 6, 7)])
    sent(forwards.values())
    sent(totals_j)
    received(totals_i)
    totals = jnp.sum(jnp.sum(wide_i[0], axis=0), axis=1, keepdims=True)
    target[...] = counts * (total_pts / totals)
    received(first_copies.values())
    row_sum = jnp.sum(jnp.sum(first_recv[...], axis=0), axis=0, keepdims=True)

    stores = [
        pltpu.make_async_copy(src, dst, store_sem.at[n])
        for n, (src, dst) in enumerate(
            (
                (center_ref, center_hbm),
                (scale_u_ref, scale_u_hbm),
                (scale_v_ref, scale_v_hbm),
                (misfit_ref, misfit_hbm),
            )
        )
    ]

    def run_pass(index, value, before, between):
        x_buf[index, :, 0:OWN] = value.astype(jnp.bfloat16)
        gather = [
            remote(
                device_i(k), x_buf.at[index, :, rows_of(0)], x_buf.at[index, :, rows_of(k)],
                send_x.at[index, k], recv_x.at[index, k],
            )
            for k in range(1, PER_I)
        ]
        start(gather)
        copies = {
            k: remote(
                owner_j(k), y_send.at[index, :, rows_of(k)], y_recv.at[index, k],
                send_y.at[index, k], recv_y.at[index, k],
            )
            for k in range(1, PER_J)
        }
        y_part[...] = jnp.zeros_like(y_part)
        before()

        def by_rows(s, carry):
            for which in range(EARLY):

                @pl.when(s == which)
                def _():
                    received(gather[max(2 * which - 1, 0) : 2 * which + 1])

            at = pl.ds(pl.multiple_of(s * 2 * OWN, 2 * OWN), 2 * OWN)
            y_part[...] += jnp.dot(
                x_buf[index, :, at], tile[at, :], preferred_element_type=jnp.float32
            )
            return carry

        lax.fori_loop(0, EARLY, by_rows, 0)
        between()
        received(gather[2 * EARLY - 1 :])
        late = pl.ds(EARLY * 2 * OWN, ROWS - EARLY * 2 * OWN)

        def by_columns(n, carry):
            q = 3 - n
            at = pl.ds(pl.multiple_of(q * PASS_J, PASS_J), PASS_J)
            value = y_part[:, at] + jnp.dot(
                x_buf[index, :, late], tile[late, at], preferred_element_type=jnp.float32
            )
            y_part[:, at] = value
            y_send[index, :, at] = value.astype(jnp.bfloat16)
            for which in range(4):

                @pl.when(q == which)
                def _():
                    for k in (2 * which + 1, 2 * which):
                        if k:
                            copies[k].start()

            return carry

        lax.fori_loop(0, 4, by_columns, 0)
        sent(gather)
        received(copies.values())
        total = y_part[:, 0:OWN]
        for k in range(1, PER_J):
            total += y_recv[index, k].astype(jnp.float32)
        return total, lambda: sent(copies.values())

    def raw(col_sum):
        return jnp.exp(jnp.sum(weights * jnp.log(col_sum), axis=0, keepdims=True))

    def scalar(value):
        return jnp.sum(value[0:1, :], axis=1, keepdims=True)

    def nothing():
        return None

    def first_sent():
        sent(first_copies.values())
        sent(totals_i)

    col_sum, y_sent = run_pass(0, target[...] / row_sum, first_sent, nothing)
    raw_center = raw(col_sum)
    v_first[...] = raw_center / col_sum
    mass_copies_j = exchange_j(raw_j, 0, send_raw_j, recv_raw_j)
    mass_copies_i = exchange_i(mass_i, 0, send_mass_i, recv_mass_i)

    def mass_begin():
        raw_j[0, 0] = jnp.broadcast_to(raw_center, (8, OWN))
        start(mass_copies_j)
        y_sent()

    def mass_next():
        received(mass_copies_j)
        mass_i[0, 0] = lanes(jnp.sum(raw_j[0], axis=0))
        start(mass_copies_i)
        sent(mass_copies_j)

    row_sum, y_sent = run_pass(1, v_first[...], mass_begin, mass_next)
    received(mass_copies_i)
    factor = total_pts / scalar(jnp.sum(mass_i[0], axis=0))
    scale_u = target[...] / (row_sum * factor)
    scale_u_ref[...] = scale_u
    stores[1].start()
    scale_v = v_first[...] * factor

    def second_sent():
        sent(mass_copies_i)
        y_sent()

    col_sum, y_sent = run_pass(2, scale_u, second_sent, nothing)
    raw_center = raw(col_sum)
    raw_j[1, 0] = jnp.broadcast_to(raw_center, (8, OWN))
    mass_copies_j = exchange_j(raw_j, 1, send_raw_j, recv_raw_j)
    start(mass_copies_j)
    mass_copies_i = exchange_i(mass_i, 1, send_mass_i, recv_mass_i)
    error_copies_j = exchange_j(moved_j, 0, send_moved_j, recv_moved_j)
    error_copies_i = exchange_i(mass_i, 2, send_mass_i, recv_mass_i)
    moved_j[0, 0] = scale_v * col_sum
    start(error_copies_j)
    y_sent()
    received(mass_copies_j)
    mass_i[1, 0] = lanes(jnp.sum(raw_j[1], axis=0))
    start(mass_copies_i)
    sent(mass_copies_j)
    received(error_copies_j)
    sent(error_copies_j)
    received(mass_copies_i)
    factor = total_pts / scalar(jnp.sum(mass_i[1], axis=0))
    error = jnp.zeros((HIST, OWN), jnp.float32)
    for k in range(PER_J):
        error += jnp.abs(moved_j[0, k] - raw_j[1, k, 0:1, :] * factor)
    error = jnp.sum(lanes(error), axis=1, keepdims=True) / total_pts
    wide_eye = lax.broadcasted_iota(jnp.int32, (HIST, 128), 0) == lax.broadcasted_iota(
        jnp.int32, (HIST, 128), 1
    )
    mass_i[2, 0] = jnp.broadcast_to(
        jnp.sum(jnp.where(wide_eye, error, 0.0), axis=0, keepdims=True), (8, 128)
    )
    start(error_copies_i)
    center = raw_center * factor
    center_ref[...] = center
    scale_v_ref[...] = center / col_sum
    stores[0].start()
    stores[2].start()
    sent(mass_copies_i)
    received(error_copies_i)
    misfit_ref[...] = jnp.sum(mass_i[2], axis=0)[0:1, 0:HIST]
    stores[3].start()
    sent(error_copies_i)
    for store in stores:
        store.wait()


def hand_over(center, scale_u, scale_v, misfit, center_out, scale_u_out, scale_v_out, misfit_out):
    center_out[...] = center[0]
    scale_u_out[...] = scale_u[...]
    scale_v_out[...] = scale_v[...]
    misfit_out[...] = misfit[0]


def shards(embeddings, counts, raw_weights):
    total_pts = embeddings.shape[0] * lax.axis_size("row") * lax.axis_size("col")
    vmem = pl.BlockSpec(memory_space=pltpu.VMEM)
    anywhere = pl.BlockSpec(memory_space=pl.ANY)
    f32, bf16, dma = jnp.float32, jnp.bfloat16, pltpu.SemaphoreType.DMA
    pair_i, pair_j = [dma((PER_I,))] * 2, [dma((PER_J,))] * 2
    center, scale_u, scale_v, misfit = pl.pallas_call(
        functools.partial(body, total_pts),
        out_shape=(
            jax.ShapeDtypeStruct((1, OWN), f32),
            jax.ShapeDtypeStruct((HIST, OWN), f32),
            jax.ShapeDtypeStruct((HIST, OWN), f32),
            jax.ShapeDtypeStruct((1, HIST), f32),
        ),
        in_specs=[anywhere] * 3,
        out_specs=(anywhere,) * 4,
        scratch_shapes=[
            pltpu.VMEM((ROWS, COLS), bf16),
            pltpu.VMEM((ROWS, 128), bf16),
            pltpu.VMEM((COLS, 128), bf16),
            pltpu.VMEM((3, HIST, ROWS), bf16),
            pltpu.VMEM((HIST, COLS), f32),
            pltpu.VMEM((3, HIST, COLS), bf16),
            pltpu.VMEM((3, PER_J, HIST, OWN), bf16),
            pltpu.VMEM((8, COLS), f32),
            pltpu.VMEM((PER_J, 8, OWN), f32),
            pltpu.VMEM((HIST, OWN), f32),
            pltpu.VMEM((HIST, OWN), f32),
            pltpu.VMEM((OWN, 128), f32),
            pltpu.VMEM((HIST, OWN), jnp.int32),
            pltpu.VMEM((1, HIST), f32),
            pltpu.VMEM((1, PER_I, HIST, 128), f32),
            pltpu.VMEM((1, PER_J, HIST, 128), f32),
            pltpu.VMEM((1, PER_J, HIST, OWN), f32),
            pltpu.VMEM((3, PER_I, 8, 128), f32),
            pltpu.VMEM((2, PER_J, 8, OWN), f32),
            pltpu.VMEM((1, OWN), f32),
            pltpu.VMEM((HIST, OWN), f32),
            pltpu.VMEM((HIST, OWN), f32),
            pltpu.VMEM((1, HIST), f32),
            dma((3,)),
            dma((4,)),
            pltpu.SemaphoreType.REGULAR((2,)),
            *pair_i,
            *pair_j,
            *pair_j,
            *[dma((3, PER_I))] * 2,
            *[dma((3, PER_J))] * 2,
            *[dma((1, PER_I))] * 2,
            *[dma((1, PER_J))] * 2,
            *[dma((3, PER_I))] * 2,
            *[dma((2, PER_J))] * 2,
            *[dma((1, PER_J))] * 2,
        ],
        compiler_params=pltpu.CompilerParams(
            collective_id=0, has_side_effects=True, vmem_limit_bytes=62 * 1024 * 1024
        ),
    )(embeddings, counts, raw_weights.reshape(1, HIST))
    return pl.pallas_call(
        hand_over,
        out_shape=(
            jax.ShapeDtypeStruct((OWN,), f32),
            jax.ShapeDtypeStruct((HIST, OWN), f32),
            jax.ShapeDtypeStruct((HIST, OWN), f32),
            jax.ShapeDtypeStruct((HIST,), f32),
        ),
        in_specs=[vmem] * 4,
        out_specs=(vmem,) * 4,
    )(center, scale_u, scale_v, misfit)


def solution(mesh):
    placed = (P(("row", "col"), None), P(None, ("row", "col")), P())
    return jax.shard_map(
        shards,
        mesh=mesh,
        in_specs=placed,
        out_specs=(P(("row", "col")), P(None, ("row", "col")), P(None, ("row", "col")), P()),
        check_vma=False,
    )
```

```python
import functools

import jax
import jax.numpy as jnp
from jax import lax
from jax.experimental import pallas as pl
from jax.experimental.pallas import tpu as pltpu
from jax.sharding import PartitionSpec as P

GROUP_I = ((0, 0), (1, 0), (3, 0), (0, 1), (3, 1), (2, 0), (1, 1), (2, 1))
GROUP_J = ((0, 0), (0, 1), (3, 0), (1, 0), (3, 1), (2, 0), (1, 1), (2, 1))
MESH = pl.DeviceIdType.MESH
SLOPE = 14.426950408889634
HIST = 32
OWN = 384
PER_I, PER_J = 16, 8
ROWS, COLS = OWN * PER_I, OWN * PER_J
BUILD_I, BUILD_J = 1536, 768
PASS_J = 768
EARLY = 3
FORWARDED = (1, 2, 3, 4, 5, 6)
ORDER = (1, 2, 3, 4, 5, 15, 14, 13, 12, 11, 10, 9, 8, 7, 6)


def body(
    total_pts,
    emb_hbm,
    counts_hbm,
    weights_hbm,
    center_hbm,
    scale_u_hbm,
    scale_v_hbm,
    misfit_hbm,
    tile,
    unit_i,
    unit_j,
    x_buf,
    y_part,
    y_send,
    y_recv,
    first_part,
    first_recv,
    target,
    v_first,
    emb_ref,
    counts_ref,
    weights_ref,
    counts_all,
    row_all,
    wide_i,
    wide_j,
    moved_j,
    mass_i,
    raw_j,
    center_ref,
    scale_u_ref,
    scale_v_ref,
    misfit_ref,
    load_sem,
    store_sem,
    ready,
    send_unit_i,
    recv_unit_i,
    send_unit_j,
    recv_unit_j,
    send_counts,
    recv_counts,
    send_first,
    recv_first,
    send_x,
    recv_x,
    send_y,
    recv_y,
    send_wide_i,
    recv_wide_i,
    send_wide_j,
    recv_wide_j,
    send_mass_i,
    recv_mass_i,
    send_raw_j,
    recv_raw_j,
    send_moved_j,
    recv_moved_j,
):
    row, col = lax.axis_index("row"), lax.axis_index("col")
    x, core = lax.div(row, 2), lax.rem(row, 2)
    z, y = lax.div(col, 4), lax.rem(col, 4)

    def device(nx, ncore, nz, ny):
        return (nx * 2 + ncore, nz * 4 + ny)

    def device_i(k):
        dx, pair = GROUP_I[k // 2]
        ncore = 1 - core if k % 2 else core
        return device(lax.rem(x + 4 - dx, 4), ncore, z, y + 1 - 2 * lax.rem(y, 2) if pair else y)

    def device_j(k):
        dz, pair = GROUP_J[k]
        return device(x, core, lax.rem(z + 4 - dz, 4), 3 - y if pair else y)

    def owner_j(k):
        dz, pair = GROUP_J[k]
        return device(x, core, lax.rem(z + dz, 4), 3 - y if pair else y)

    sibling = device(x, 1 - core, z, y)
    near = [sibling] + [device_i(2 * s) for s in (1, 2, 3)] + [device_j(s) for s in (1, 2, 3)]

    def remote(device_id, src, dst, send, recv):
        return pltpu.make_async_remote_copy(
            src_ref=src, dst_ref=dst, send_sem=send, recv_sem=recv,
            device_id=device_id, device_id_type=MESH,
        )

    def start(copies):
        for copy in copies:
            copy.start()

    def received(copies):
        for copy in copies:
            copy.wait_recv()

    def sent(copies):
        for copy in copies:
            copy.wait_send()

    def tell_near(semaphore):
        for neighbour in near:
            pl.semaphore_signal(semaphore, inc=1, device_id=neighbour, device_id_type=MESH)

    def rows_of(k):
        return pl.ds(k * OWN, OWN)

    def lanes(value):
        return value[:, 0:128] + value[:, 128:256] + value[:, 256:384]

    loads = [
        pltpu.make_async_copy(src, dst, load_sem.at[n])
        for n, (src, dst) in enumerate(((emb_hbm, emb_ref), (counts_hbm, counts_ref), (weights_hbm, weights_ref)))
    ]
    for load in loads:
        load.start()
    barrier = pltpu.get_barrier_semaphore()
    tell_near(barrier)
    loads[0].wait()

    emb = emb_ref[...]
    squares = jnp.sum(emb * emb, axis=1, keepdims=True)
    unit = (emb * lax.rsqrt(squares + 1e-6)).astype(jnp.bfloat16)
    unit_i[0:OWN, :] = unit
    unit_j[0:OWN, :] = unit

    unit_copies_i = {
        k: remote(
            device_i(k), unit_i.at[rows_of(0)], unit_i.at[rows_of(k)],
            send_unit_i.at[k], recv_unit_i.at[k],
        )
        for k in (1, 2, 4, 6, 8, 10, 12, 14)
    }
    unit_copies_j = {
        k: remote(
            device_j(k), unit_j.at[rows_of(0)], unit_j.at[rows_of(k)],
            send_unit_j.at[k], recv_unit_j.at[k],
        )
        for k in range(1, PER_J)
    }
    forwards = {
        s: remote(
            sibling, unit_i.at[rows_of(2 * s)], unit_i.at[rows_of(2 * s + 1)],
            send_unit_i.at[2 * s + 1], recv_unit_i.at[2 * s + 1],
        )
        for s in range(1, 8)
    }

    def send_units(slots):
        for s in slots:
            unit_copies_i[2 * s].start()
            unit_copies_j[s].start()

    pl.semaphore_wait(barrier, len(near))
    unit_copies_i[1].start()
    send_units((1, 2, 3))
    tell_near(ready.at[0])
    pl.semaphore_wait(ready.at[0], len(near))
    sent([unit_copies_i[k] for k in (2, 4, 6)])
    sent([unit_copies_j[k] for k in (1, 2, 3)])
    send_units((4, 5, 6))
    tell_near(ready.at[1])
    pl.semaphore_wait(ready.at[1], len(near))
    send_units((7,))

    def exchange_j(buf, index, send, recv):
        return [
            remote(
                device_j(k), buf.at[index, 0], buf.at[index, k],
                send.at[index, k], recv.at[index, k],
            )
            for k in range(PER_J - 1, 0, -1)
        ]

    def exchange_i(buf, index, send, recv):
        return [
            remote(
                device_i(k), buf.at[index, 0], buf.at[index, k],
                send.at[index, k], recv.at[index, k],
            )
            for k in range(PER_I - 1, 0, -1)
        ]

    def share(buf, forwarded, send, recv):
        direct = {
            k: remote(
                device_i(k), buf.at[:, rows_of(0)], buf.at[:, rows_of(k)], send.at[k], recv.at[k]
            )
            for k in range(1, PER_I)
            if k % 2 == 0 or k // 2 not in forwarded
        }
        passed_on = {
            s: remote(
                sibling, buf.at[:, rows_of(2 * s)], buf.at[:, rows_of(2 * s + 1)],
                send.at[2 * s + 1], recv.at[2 * s + 1],
            )
            for s in forwarded
        }
        return direct, passed_on

    loads[1].wait()
    loads[2].wait()
    counts = counts_ref[...].astype(jnp.float32)
    raw_weights = weights_ref[...]
    eye = lax.broadcasted_iota(jnp.int32, (HIST, HIST), 0) == lax.broadcasted_iota(
        jnp.int32, (HIST, HIST), 1
    )
    weights = jnp.sum(
        jnp.where(eye, raw_weights / jnp.sum(raw_weights), 0.0), axis=1, keepdims=True
    )
    totals_j = exchange_j(wide_j, 0, send_wide_j, recv_wide_j)
    totals_i = exchange_i(wide_i, 0, send_wide_i, recv_wide_i)
    wide_j[0, 0] = lanes(counts)
    start(totals_j)
    first_part[...] = jnp.zeros_like(first_part)
    first_copies = {
        k: remote(
            owner_j(k), first_part.at[:, rows_of(k)], first_recv.at[k],
            send_first.at[k], recv_first.at[k],
        )
        for k in range(1, PER_J)
    }

    counts_all[:, 0:OWN] = counts.astype(jnp.bfloat16)
    counts_copies, counts_forwards = share(counts_all, tuple(range(1, 8)), send_counts, recv_counts)

    def build(n, carry):
        t = (n >= 1).astype(jnp.int32) + (n >= 4).astype(jnp.int32) + (n >= 9).astype(jnp.int32)
        m = n - t * t
        down = (m < t).astype(jnp.int32)
        i = down * m + (1 - down) * t
        j = down * t + (1 - down) * (2 * t - m)

        def forward(slots):
            for s in slots:
                unit_copies_i[2 * s].wait_recv()
                forwards[s].start()

        def columns_arrived(slots):
            for s in slots:
                unit_copies_j[s].wait_recv()

        def rows_arrived(slots):
            for s in slots:
                forwards[s].wait_recv()

        @pl.when(n == 0)
        def _():
            forward((1,))
            unit_copies_i[1].wait_recv()
            columns_arrived((1,))
            forward((2, 3))
            rows_arrived((1,))

        @pl.when(n == 1)
        def _():
            columns_arrived((2, 3))

        @pl.when(n == 2)
        def _():
            rows_arrived((2, 3))

        @pl.when(n == 4)
        def _():
            columns_arrived((4, 5))
            forward((4, 5))

        @pl.when(n == 6)
        def _():
            rows_arrived((4, 5))
            received(totals_j)
            wide_i[0, 0] = jnp.sum(wide_j[0], axis=0)
            start(totals_i)

        @pl.when(n == 9)
        def _():
            columns_arrived((6, 7))
            forward((6, 7))
            start(counts_copies.values())

        @pl.when(n == 12)
        def _():
            rows_arrived((6, 7))

        at_i = pl.ds(pl.multiple_of(i * BUILD_I, BUILD_I), BUILD_I)
        at_j = pl.ds(pl.multiple_of(j * BUILD_J, BUILD_J), BUILD_J)
        gram = lax.dot_general(
            unit_i[at_i, :], unit_j[at_j, :], (((1,), (1,)), ((), ())),
            preferred_element_type=jnp.float32,
        )
        value = jnp.exp2(gram * SLOPE - SLOPE)
        tile[at_i, at_j] = value.astype(jnp.bfloat16)
        first_part[:, at_j] += jnp.sum(value.reshape(BUILD_I // 8, 8, BUILD_J), axis=0)
        for which in range(4):

            @pl.when(n == 15 - which)
            def _():
                for k in (2 * which + 1, 2 * which):
                    if k:
                        first_copies[k].start()

        return carry

    lax.fori_loop(0, 16, build, 0)
    for s in range(1, 8):
        counts_copies[2 * s].wait_recv()
        counts_forwards[s].start()

    first_recv[0] = first_part[:, 0:OWN]
    sent([unit_copies_i[k] for k in (1, 8, 10, 12, 14)])
    sent([unit_copies_j[k] for k in (4, 5, 6, 7)])
    sent(forwards.values())
    sent(counts_copies.values())
    sent(counts_forwards.values())
    sent(totals_j)
    received(totals_i)
    totals = jnp.sum(jnp.sum(wide_i[0], axis=0), axis=1, keepdims=True)
    per_count = total_pts / totals
    target[...] = counts * per_count
    counts_copies[1].wait_recv()
    received(counts_forwards.values())
    received(first_copies.values())
    row_sum = jnp.sum(jnp.sum(first_recv[...], axis=0), axis=0, keepdims=True)

    stores = [
        pltpu.make_async_copy(src, dst, store_sem.at[n])
        for n, (src, dst) in enumerate(
            (
                (center_ref, center_hbm),
                (scale_u_ref, scale_u_hbm),
                (scale_v_ref, scale_v_hbm),
                (misfit_ref, misfit_hbm),
            )
        )
    ]

    def gather_value(index, value):
        x_buf[index, :, 0:OWN] = value.astype(jnp.bfloat16)
        direct, passed_on = share(x_buf.at[index], FORWARDED, send_x.at[index], recv_x.at[index])
        start(direct[k] for k in ORDER if k in direct)

        def pass_on(slots):
            for s in slots:
                if s in passed_on:
                    direct[2 * s].wait_recv()
                    passed_on[s].start()

        def arrive(first, last):
            if first == 1:
                pass_on((1, 2, 3))
            if first == 2:
                pass_on((4, 5, 6))
            if first == EARLY:
                pass_on((7,))
            for s in range(first, last):
                if s in passed_on:
                    passed_on[s].wait_recv()
                else:
                    received(direct[k] for k in (2 * s, 2 * s + 1) if k)

        def leave():
            sent(direct.values())
            sent(passed_on.values())

        return arrive, leave

    def gather_first(row_sum):
        row_all[:, 0:OWN] = row_sum
        copies = {
            k: remote(
                device_i(k), row_all.at[:, rows_of(0)], row_all.at[:, rows_of(k)],
                send_x.at[0, k], recv_x.at[0, k],
            )
            for k in range(1, PER_I)
        }
        start(copies[k] for k in ORDER)

        def arrive(first, last):
            received(copies[k] for k in range(2 * first, 2 * last) if k)
            at = pl.ds(first * 2 * OWN, (last - first) * 2 * OWN)
            x_buf[0, :, at] = (
                counts_all[:, at].astype(jnp.float32) * per_count / row_all[:, at]
            ).astype(jnp.bfloat16)

        return arrive, lambda: sent(copies.values())

    def run_pass(index, gather, before, between):
        arrive, leave = gather
        copies = {
            k: remote(
                owner_j(k), y_send.at[index, :, rows_of(k)], y_recv.at[index, k],
                send_y.at[index, k], recv_y.at[index, k],
            )
            for k in range(1, PER_J)
        }
        y_part[...] = jnp.zeros_like(y_part)
        before()

        def by_rows(s, carry):
            for which in range(EARLY):

                @pl.when(s == which)
                def _():
                    arrive(which, which + 1)

            at = pl.ds(pl.multiple_of(s * 2 * OWN, 2 * OWN), 2 * OWN)
            y_part[...] += jnp.dot(
                x_buf[index, :, at], tile[at, :], preferred_element_type=jnp.float32
            )
            return carry

        lax.fori_loop(0, EARLY, by_rows, 0)
        between()
        arrive(EARLY, 8)
        late = pl.ds(EARLY * 2 * OWN, ROWS - EARLY * 2 * OWN)

        def by_columns(n, carry):
            q = 3 - n
            at = pl.ds(pl.multiple_of(q * PASS_J, PASS_J), PASS_J)
            value = y_part[:, at] + jnp.dot(
                x_buf[index, :, late], tile[late, at], preferred_element_type=jnp.float32
            )
            y_part[:, at] = value
            y_send[index, :, at] = value.astype(jnp.bfloat16)
            for which in range(4):

                @pl.when(q == which)
                def _():
                    for k in (2 * which + 1, 2 * which):
                        if k:
                            copies[k].start()

            return carry

        lax.fori_loop(0, 4, by_columns, 0)
        leave()
        received(copies.values())
        total = y_part[:, 0:OWN]
        for k in range(1, PER_J):
            total += y_recv[index, k].astype(jnp.float32)
        return total, lambda: sent(copies.values())

    def raw(col_sum):
        return jnp.exp(jnp.sum(weights * jnp.log(col_sum), axis=0, keepdims=True))

    def scalar(value):
        return jnp.sum(value[0:1, :], axis=1, keepdims=True)

    def nothing():
        return None

    def first_sent():
        sent(first_copies.values())
        sent(totals_i)

    col_sum, y_sent = run_pass(0, gather_first(row_sum), first_sent, nothing)
    raw_center = raw(col_sum)
    v_first[...] = raw_center / col_sum
    mass_copies_j = exchange_j(raw_j, 0, send_raw_j, recv_raw_j)
    mass_copies_i = exchange_i(mass_i, 0, send_mass_i, recv_mass_i)

    def mass_begin():
        raw_j[0, 0] = jnp.broadcast_to(raw_center, (8, OWN))
        start(mass_copies_j)
        y_sent()

    def mass_next():
        received(mass_copies_j)
        mass_i[0, 0] = lanes(jnp.sum(raw_j[0], axis=0))
        start(mass_copies_i)
        sent(mass_copies_j)

    row_sum, y_sent = run_pass(1, gather_value(1, v_first[...]), mass_begin, mass_next)
    received(mass_copies_i)
    factor = total_pts / scalar(jnp.sum(mass_i[0], axis=0))
    scale_u = target[...] / (row_sum * factor)
    scale_v = v_first[...] * factor

    def second_sent():
        scale_u_ref[...] = scale_u
        stores[1].start()
        sent(mass_copies_i)
        y_sent()

    col_sum, y_sent = run_pass(2, gather_value(2, scale_u), second_sent, nothing)
    raw_center = raw(col_sum)
    raw_j[1, 0] = jnp.broadcast_to(raw_center, (8, OWN))
    mass_copies_j = exchange_j(raw_j, 1, send_raw_j, recv_raw_j)
    start(mass_copies_j)
    mass_copies_i = exchange_i(mass_i, 1, send_mass_i, recv_mass_i)
    error_copies_j = exchange_j(moved_j, 0, send_moved_j, recv_moved_j)
    error_copies_i = exchange_i(mass_i, 2, send_mass_i, recv_mass_i)
    moved_j[0, 0] = scale_v * col_sum
    start(error_copies_j)
    y_sent()
    received(mass_copies_j)
    mass_i[1, 0] = lanes(jnp.sum(raw_j[1], axis=0))
    start(mass_copies_i)
    sent(mass_copies_j)
    received(error_copies_j)
    sent(error_copies_j)
    received(mass_copies_i)
    factor = total_pts / scalar(jnp.sum(mass_i[1], axis=0))
    error = jnp.zeros((HIST, OWN), jnp.float32)
    for k in range(PER_J):
        error += jnp.abs(moved_j[0, k] - raw_j[1, k, 0:1, :] * factor)
    error = jnp.sum(lanes(error), axis=1, keepdims=True) / total_pts
    wide_eye = lax.broadcasted_iota(jnp.int32, (HIST, 128), 0) == lax.broadcasted_iota(
        jnp.int32, (HIST, 128), 1
    )
    mass_i[2, 0] = jnp.broadcast_to(
        jnp.sum(jnp.where(wide_eye, error, 0.0), axis=0, keepdims=True), (8, 128)
    )
    start(error_copies_i)
    center = raw_center * factor
    center_ref[...] = center
    scale_v_ref[...] = center / col_sum
    stores[0].start()
    stores[2].start()
    sent(mass_copies_i)
    received(error_copies_i)
    misfit_ref[...] = jnp.sum(mass_i[2], axis=0)[0:1, 0:HIST]
    stores[3].start()
    sent(error_copies_i)
    for store in stores:
        store.wait()


def hand_over(center, scale_u, scale_v, misfit, center_out, scale_u_out, scale_v_out, misfit_out):
    center_out[...] = center[0]
    scale_u_out[...] = scale_u[...]
    scale_v_out[...] = scale_v[...]
    misfit_out[...] = misfit[0]


def shards(embeddings, counts, raw_weights):
    total_pts = embeddings.shape[0] * lax.axis_size("row") * lax.axis_size("col")
    vmem = pl.BlockSpec(memory_space=pltpu.VMEM)
    anywhere = pl.BlockSpec(memory_space=pl.ANY)
    f32, bf16, dma = jnp.float32, jnp.bfloat16, pltpu.SemaphoreType.DMA
    pair_i, pair_j = [dma((PER_I,))] * 2, [dma((PER_J,))] * 2
    center, scale_u, scale_v, misfit = pl.pallas_call(
        functools.partial(body, total_pts),
        out_shape=(
            jax.ShapeDtypeStruct((1, OWN), f32),
            jax.ShapeDtypeStruct((HIST, OWN), f32),
            jax.ShapeDtypeStruct((HIST, OWN), f32),
            jax.ShapeDtypeStruct((1, HIST), f32),
        ),
        in_specs=[anywhere] * 3,
        out_specs=(anywhere,) * 4,
        scratch_shapes=[
            pltpu.VMEM((ROWS, COLS), bf16),
            pltpu.VMEM((ROWS, 128), bf16),
            pltpu.VMEM((COLS, 128), bf16),
            pltpu.VMEM((3, HIST, ROWS), bf16),
            pltpu.VMEM((HIST, COLS), f32),
            pltpu.VMEM((3, HIST, COLS), bf16),
            pltpu.VMEM((3, PER_J, HIST, OWN), bf16),
            pltpu.VMEM((8, COLS), f32),
            pltpu.VMEM((PER_J, 8, OWN), f32),
            pltpu.VMEM((HIST, OWN), f32),
            pltpu.VMEM((HIST, OWN), f32),
            pltpu.VMEM((OWN, 128), f32),
            pltpu.VMEM((HIST, OWN), jnp.int32),
            pltpu.VMEM((1, HIST), f32),
            pltpu.VMEM((HIST, ROWS), bf16),
            pltpu.VMEM((1, ROWS), f32),
            pltpu.VMEM((1, PER_I, HIST, 128), f32),
            pltpu.VMEM((1, PER_J, HIST, 128), f32),
            pltpu.VMEM((1, PER_J, HIST, OWN), f32),
            pltpu.VMEM((3, PER_I, 8, 128), f32),
            pltpu.VMEM((2, PER_J, 8, OWN), f32),
            pltpu.VMEM((1, OWN), f32),
            pltpu.VMEM((HIST, OWN), f32),
            pltpu.VMEM((HIST, OWN), f32),
            pltpu.VMEM((1, HIST), f32),
            dma((3,)),
            dma((4,)),
            pltpu.SemaphoreType.REGULAR((2,)),
            *pair_i,
            *pair_j,
            *pair_i,
            *pair_j,
            *[dma((3, PER_I))] * 2,
            *[dma((3, PER_J))] * 2,
            *[dma((1, PER_I))] * 2,
            *[dma((1, PER_J))] * 2,
            *[dma((3, PER_I))] * 2,
            *[dma((2, PER_J))] * 2,
            *[dma((1, PER_J))] * 2,
        ],
        compiler_params=pltpu.CompilerParams(
            collective_id=0, has_side_effects=True, vmem_limit_bytes=62 * 1024 * 1024
        ),
    )(embeddings, counts, raw_weights.reshape(1, HIST))
    return pl.pallas_call(
        hand_over,
        out_shape=(
            jax.ShapeDtypeStruct((OWN,), f32),
            jax.ShapeDtypeStruct((HIST, OWN), f32),
            jax.ShapeDtypeStruct((HIST, OWN), f32),
            jax.ShapeDtypeStruct((HIST,), f32),
        ),
        in_specs=[vmem] * 4,
        out_specs=(vmem,) * 4,
    )(center, scale_u, scale_v, misfit)


def solution(mesh):
    placed = (P(("row", "col"), None), P(None, ("row", "col")), P())
    return jax.shard_map(
        shards,
        mesh=mesh,
        in_specs=placed,
        out_specs=(P(("row", "col")), P(None, ("row", "col")), P(None, ("row", "col")), P()),
        check_vma=False,
    )
```

```python
import functools

import jax
import jax.numpy as jnp
from jax import lax
from jax.experimental import pallas as pl
from jax.experimental.pallas import tpu as pltpu
from jax.sharding import PartitionSpec as P

GROUP_I = ((0, 0), (1, 0), (3, 0), (0, 1), (3, 1), (2, 0), (1, 1), (2, 1))
GROUP_J = ((0, 0), (0, 1), (3, 0), (1, 0), (3, 1), (2, 0), (1, 1), (2, 1))
MESH = pl.DeviceIdType.MESH
SLOPE = 14.426950408889634
HIST = 32
OWN = 384
PER_I, PER_J = 16, 8
ROWS, COLS = OWN * PER_I, OWN * PER_J
BUILD_I, BUILD_J = 1536, 768
PASS_J = 768
EARLY = 3
FORWARDED = (1, 2, 3, 4, 5, 6)
ORDER = (1, 2, 3, 4, 5, 15, 14, 13, 12, 11, 10, 9, 8, 7, 6)


def body(
    total_pts,
    emb_hbm,
    counts_hbm,
    weights_hbm,
    center_hbm,
    scale_u_hbm,
    scale_v_hbm,
    misfit_hbm,
    tile,
    unit_i,
    unit_j,
    x_buf,
    y_part,
    y_send,
    y_recv,
    first_part,
    first_row,
    first_recv,
    target,
    v_first,
    emb_ref,
    counts_ref,
    weights_ref,
    counts_all,
    row_all,
    wide_i,
    wide_j,
    moved_j,
    mass_i,
    raw_j,
    center_ref,
    scale_u_ref,
    scale_v_ref,
    misfit_ref,
    load_sem,
    store_sem,
    ready,
    send_unit_i,
    recv_unit_i,
    send_unit_j,
    recv_unit_j,
    send_counts,
    recv_counts,
    send_first,
    recv_first,
    send_x,
    recv_x,
    send_y,
    recv_y,
    send_wide_i,
    recv_wide_i,
    send_wide_j,
    recv_wide_j,
    send_mass_i,
    recv_mass_i,
    send_raw_j,
    recv_raw_j,
    send_moved_j,
    recv_moved_j,
):
    row, col = lax.axis_index("row"), lax.axis_index("col")
    x, core = lax.div(row, 2), lax.rem(row, 2)
    z, y = lax.div(col, 4), lax.rem(col, 4)

    def device(nx, ncore, nz, ny):
        return (nx * 2 + ncore, nz * 4 + ny)

    def device_i(k):
        dx, pair = GROUP_I[k // 2]
        ncore = 1 - core if k % 2 else core
        return device(lax.rem(x + 4 - dx, 4), ncore, z, y + 1 - 2 * lax.rem(y, 2) if pair else y)

    def device_j(k):
        dz, pair = GROUP_J[k]
        return device(x, core, lax.rem(z + 4 - dz, 4), 3 - y if pair else y)

    def owner_j(k):
        dz, pair = GROUP_J[k]
        return device(x, core, lax.rem(z + dz, 4), 3 - y if pair else y)

    sibling = device(x, 1 - core, z, y)
    near = [sibling] + [device_i(2 * s) for s in (1, 2, 3)] + [device_j(s) for s in (1, 2, 3)]

    def remote(device_id, src, dst, send, recv):
        return pltpu.make_async_remote_copy(
            src_ref=src, dst_ref=dst, send_sem=send, recv_sem=recv,
            device_id=device_id, device_id_type=MESH,
        )

    def start(copies):
        for copy in copies:
            copy.start()

    def received(copies):
        for copy in copies:
            copy.wait_recv()

    def sent(copies):
        for copy in copies:
            copy.wait_send()

    def tell_near(semaphore):
        for neighbour in near:
            pl.semaphore_signal(semaphore, inc=1, device_id=neighbour, device_id_type=MESH)

    def rows_of(k):
        return pl.ds(k * OWN, OWN)

    def lanes(value):
        return value[:, 0:128] + value[:, 128:256] + value[:, 256:384]

    loads = [
        pltpu.make_async_copy(src, dst, load_sem.at[n])
        for n, (src, dst) in enumerate(((emb_hbm, emb_ref), (counts_hbm, counts_ref), (weights_hbm, weights_ref)))
    ]
    for load in loads:
        load.start()
    barrier = pltpu.get_barrier_semaphore()
    tell_near(barrier)
    loads[0].wait()

    emb = emb_ref[...]
    squares = jnp.sum(emb * emb, axis=1, keepdims=True)
    unit = (emb * lax.rsqrt(squares + 1e-6)).astype(jnp.bfloat16)
    unit_i[0:OWN, :] = unit
    unit_j[0:OWN, :] = unit

    unit_copies_i = {
        k: remote(
            device_i(k), unit_i.at[rows_of(0)], unit_i.at[rows_of(k)],
            send_unit_i.at[k], recv_unit_i.at[k],
        )
        for k in (1, 2, 4, 6, 8, 10, 12, 14)
    }
    unit_copies_j = {
        k: remote(
            device_j(k), unit_j.at[rows_of(0)], unit_j.at[rows_of(k)],
            send_unit_j.at[k], recv_unit_j.at[k],
        )
        for k in range(1, PER_J)
    }
    forwards = {
        s: remote(
            sibling, unit_i.at[rows_of(2 * s)], unit_i.at[rows_of(2 * s + 1)],
            send_unit_i.at[2 * s + 1], recv_unit_i.at[2 * s + 1],
        )
        for s in range(1, 8)
    }

    def send_units(slots):
        for s in slots:
            unit_copies_i[2 * s].start()
            unit_copies_j[s].start()

    pl.semaphore_wait(barrier, len(near))
    unit_copies_i[1].start()
    send_units((1, 2, 3))
    for hops in range(2):
        tell_near(ready.at[hops])
        pl.semaphore_wait(ready.at[hops], len(near))
    sent([unit_copies_i[k] for k in (2, 4, 6)])
    sent([unit_copies_j[k] for k in (1, 2, 3)])
    send_units((7, 4, 5, 6))

    def exchange_j(buf, index, send, recv):
        return [
            remote(
                device_j(k), buf.at[index, 0], buf.at[index, k],
                send.at[index, k], recv.at[index, k],
            )
            for k in range(PER_J - 1, 0, -1)
        ]

    def exchange_i(buf, index, send, recv):
        return [
            remote(
                device_i(k), buf.at[index, 0], buf.at[index, k],
                send.at[index, k], recv.at[index, k],
            )
            for k in range(PER_I - 1, 0, -1)
        ]

    def share(buf, forwarded, send, recv):
        direct = {
            k: remote(
                device_i(k), buf.at[:, rows_of(0)], buf.at[:, rows_of(k)], send.at[k], recv.at[k]
            )
            for k in range(1, PER_I)
            if k % 2 == 0 or k // 2 not in forwarded
        }
        passed_on = {
            s: remote(
                sibling, buf.at[:, rows_of(2 * s)], buf.at[:, rows_of(2 * s + 1)],
                send.at[2 * s + 1], recv.at[2 * s + 1],
            )
            for s in forwarded
        }
        return direct, passed_on

    loads[1].wait()
    loads[2].wait()
    counts = counts_ref[...].astype(jnp.float32)
    raw_weights = weights_ref[...]
    eye = lax.broadcasted_iota(jnp.int32, (HIST, HIST), 0) == lax.broadcasted_iota(
        jnp.int32, (HIST, HIST), 1
    )
    weights = jnp.sum(
        jnp.where(eye, raw_weights / jnp.sum(raw_weights), 0.0), axis=1, keepdims=True
    )
    totals_j = exchange_j(wide_j, 0, send_wide_j, recv_wide_j)
    totals_i = exchange_i(wide_i, 0, send_wide_i, recv_wide_i)
    wide_j[0, 0] = lanes(counts)
    start(totals_j)
    first_part[...] = jnp.zeros_like(first_part)
    first_copies = {
        k: remote(
            owner_j(k), first_row.at[:, rows_of(k)], first_recv.at[k],
            send_first.at[k], recv_first.at[k],
        )
        for k in range(1, PER_J)
    }

    counts_all[:, 0:OWN] = counts.astype(jnp.bfloat16)
    counts_copies, counts_forwards = share(counts_all, tuple(range(1, 8)), send_counts, recv_counts)

    def forward(slots):
        for s in slots:
            unit_copies_i[2 * s].wait_recv()
            forwards[s].start()

    def columns_arrived(slots):
        for s in slots:
            unit_copies_j[s].wait_recv()

    def rows_arrived(slots):
        for s in slots:
            forwards[s].wait_recv()

    def build_block(at_i, at_j):
        gram = lax.dot_general(
            unit_i[at_i, :], unit_j[at_j, :], (((1,), (1,)), ((), ())),
            preferred_element_type=jnp.float32,
        )
        value = jnp.exp2(gram * SLOPE - SLOPE)
        tile[at_i, at_j] = value.astype(jnp.bfloat16)
        first_part[:, at_j] += jnp.sum(
            value.reshape(at_i.size // 8, 8, at_j.size), axis=0
        )

    def build(n, carry):
        t = (n >= 1).astype(jnp.int32) + (n >= 4).astype(jnp.int32) + (n >= 9).astype(jnp.int32)
        m = n - t * t
        down = (m < t).astype(jnp.int32)
        i = down * m + (1 - down) * t
        j = down * t + (1 - down) * (2 * t - m)

        @pl.when(n == 0)
        def _():
            forward((1,))
            unit_copies_i[1].wait_recv()
            columns_arrived((1,))
            forward((2, 3))
            rows_arrived((1,))

        @pl.when(n == 1)
        def _():
            columns_arrived((2, 3))

        @pl.when(n == 2)
        def _():
            rows_arrived((2, 3))

        @pl.when(n == 4)
        def _():
            columns_arrived((4, 5))
            forward((4, 5))

        @pl.when(n == 6)
        def _():
            rows_arrived((4, 5))
            received(totals_j)
            wide_i[0, 0] = jnp.sum(wide_j[0], axis=0)
            start(totals_i)

        build_block(
            pl.ds(pl.multiple_of(i * BUILD_I, BUILD_I), BUILD_I),
            pl.ds(pl.multiple_of(j * BUILD_J, BUILD_J), BUILD_J),
        )
        return carry

    lax.fori_loop(0, 9, build, 0)
    columns_arrived((6, 7))
    forward((6, 7))
    start(counts_copies.values())
    build_block(pl.ds(0, 3 * BUILD_I), pl.ds(3 * BUILD_J, BUILD_J))
    rows_arrived((6, 7))
    for last in (1, 0):
        build_block(pl.ds(3 * BUILD_I, BUILD_I), pl.ds(last * 2 * BUILD_J, 2 * BUILD_J))
        done = pl.ds(last * 2 * BUILD_J, 2 * BUILD_J)
        first_row[:, done] = jnp.sum(first_part[:, done], axis=0, keepdims=True)
        start(first_copies[k] for k in range(4 * last + 3, 4 * last - 1, -1) if k)
    for s in range(1, 8):
        counts_copies[2 * s].wait_recv()
        counts_forwards[s].start()

    first_recv[0] = first_row[:, 0:OWN]
    sent([unit_copies_i[k] for k in (1, 8, 10, 12, 14)])
    sent([unit_copies_j[k] for k in (4, 5, 6, 7)])
    sent(forwards.values())
    sent(counts_copies.values())
    sent(counts_forwards.values())
    sent(totals_j)
    received(totals_i)
    totals = jnp.sum(jnp.sum(wide_i[0], axis=0), axis=1, keepdims=True)
    per_count = total_pts / totals
    target[...] = counts * per_count
    counts_copies[1].wait_recv()
    received(counts_forwards.values())
    received(first_copies.values())
    row_sum = jnp.sum(first_recv[...], axis=0)

    stores = [
        pltpu.make_async_copy(src, dst, store_sem.at[n])
        for n, (src, dst) in enumerate(
            (
                (center_ref, center_hbm),
                (scale_u_ref, scale_u_hbm),
                (scale_v_ref, scale_v_hbm),
                (misfit_ref, misfit_hbm),
            )
        )
    ]

    def gather_value(index, value):
        x_buf[index, :, 0:OWN] = value.astype(jnp.bfloat16)
        direct, passed_on = share(x_buf.at[index], FORWARDED, send_x.at[index], recv_x.at[index])
        start(direct[k] for k in ORDER if k in direct)

        def pass_on(slots):
            for s in slots:
                if s in passed_on:
                    direct[2 * s].wait_recv()
                    passed_on[s].start()

        def arrive(first, last):
            if first == 1:
                pass_on((1, 2, 3))
            if first == 2:
                pass_on((4, 5, 6))
            if first == EARLY:
                pass_on((7,))
            for s in range(first, last):
                if s in passed_on:
                    passed_on[s].wait_recv()
                else:
                    received(direct[k] for k in (2 * s, 2 * s + 1) if k)

        def leave():
            sent(direct.values())
            sent(passed_on.values())

        return arrive, leave

    def gather_first(row_sum):
        row_all[:, 0:OWN] = row_sum
        copies = {
            k: remote(
                device_i(k), row_all.at[:, rows_of(0)], row_all.at[:, rows_of(k)],
                send_x.at[0, k], recv_x.at[0, k],
            )
            for k in range(1, PER_I)
        }
        start(copies[k] for k in ORDER)

        def arrive(first, last):
            received(copies[k] for k in range(2 * first, 2 * last) if k)
            at = pl.ds(first * 2 * OWN, (last - first) * 2 * OWN)
            x_buf[0, :, at] = (
                counts_all[:, at].astype(jnp.float32) * per_count / row_all[:, at]
            ).astype(jnp.bfloat16)

        return arrive, lambda: sent(copies.values())

    def run_pass(index, gather, before, between):
        arrive, leave = gather
        copies = {
            k: remote(
                owner_j(k), y_send.at[index, :, rows_of(k)], y_recv.at[index, k],
                send_y.at[index, k], recv_y.at[index, k],
            )
            for k in range(1, PER_J)
        }
        y_part[...] = jnp.zeros_like(y_part)
        before()

        def by_rows(s, carry):
            for which in range(EARLY):

                @pl.when(s == which)
                def _():
                    arrive(which, which + 1)

            at = pl.ds(pl.multiple_of(s * 2 * OWN, 2 * OWN), 2 * OWN)
            y_part[...] += jnp.dot(
                x_buf[index, :, at], tile[at, :], preferred_element_type=jnp.float32
            )
            return carry

        lax.fori_loop(0, EARLY, by_rows, 0)
        between()
        arrive(EARLY, 8)
        late = pl.ds(EARLY * 2 * OWN, ROWS - EARLY * 2 * OWN)

        def by_columns(n, carry):
            q = 3 - n
            at = pl.ds(pl.multiple_of(q * PASS_J, PASS_J), PASS_J)
            value = y_part[:, at] + jnp.dot(
                x_buf[index, :, late], tile[late, at], preferred_element_type=jnp.float32
            )
            y_part[:, at] = value
            y_send[index, :, at] = value.astype(jnp.bfloat16)
            for which in range(4):

                @pl.when(q == which)
                def _():
                    for k in (2 * which + 1, 2 * which):
                        if k:
                            copies[k].start()

            return carry

        lax.fori_loop(0, 4, by_columns, 0)
        leave()
        received(copies.values())
        total = y_part[:, 0:OWN]
        for k in range(1, PER_J):
            total += y_recv[index, k].astype(jnp.float32)
        return total, lambda: sent(copies.values())

    def raw(col_sum):
        return jnp.exp(jnp.sum(weights * jnp.log(col_sum), axis=0, keepdims=True))

    def scalar(value):
        return jnp.sum(value, axis=1, keepdims=True)

    def nothing():
        return None

    def first_sent():
        sent(first_copies.values())
        sent(totals_i)

    col_sum, y_sent = run_pass(0, gather_first(row_sum), first_sent, nothing)
    raw_center = raw(col_sum)
    v_first[...] = raw_center / col_sum
    mass_copies_j = exchange_j(raw_j, 0, send_raw_j, recv_raw_j)
    mass_copies_i = exchange_i(mass_i, 0, send_mass_i, recv_mass_i)

    def mass_begin():
        raw_j[0, 0] = raw_center
        start(mass_copies_j)
        y_sent()

    def mass_next():
        received(mass_copies_j)
        mass_i[0, 0] = lanes(jnp.sum(raw_j[0], axis=0))
        start(mass_copies_i)
        sent(mass_copies_j)

    row_sum, y_sent = run_pass(1, gather_value(1, v_first[...]), mass_begin, mass_next)
    received(mass_copies_i)
    factor = total_pts / scalar(jnp.sum(mass_i[0], axis=0))
    scale_u = target[...] / (row_sum * factor)
    scale_v = v_first[...] * factor

    def second_sent():
        scale_u_ref[...] = scale_u
        stores[1].start()
        sent(mass_copies_i)
        y_sent()

    col_sum, y_sent = run_pass(2, gather_value(2, scale_u), second_sent, nothing)
    raw_center = raw(col_sum)
    raw_j[1, 0] = raw_center
    mass_copies_j = exchange_j(raw_j, 1, send_raw_j, recv_raw_j)
    start(mass_copies_j)
    mass_copies_i = exchange_i(mass_i, 1, send_mass_i, recv_mass_i)
    error_copies_j = exchange_j(moved_j, 0, send_moved_j, recv_moved_j)
    error_copies_i = exchange_i(mass_i, 2, send_mass_i, recv_mass_i)
    moved_j[0, 0] = scale_v * col_sum
    start(error_copies_j)
    y_sent()
    received(mass_copies_j)
    mass_i[1, 0] = lanes(jnp.sum(raw_j[1], axis=0))
    start(mass_copies_i)
    sent(mass_copies_j)
    received(error_copies_j)
    sent(error_copies_j)
    received(mass_copies_i)
    factor = total_pts / scalar(jnp.sum(mass_i[1], axis=0))
    error = jnp.zeros((HIST, OWN), jnp.float32)
    for k in range(PER_J):
        error += jnp.abs(moved_j[0, k] - raw_j[1, k] * factor)
    error = jnp.sum(lanes(error), axis=1, keepdims=True) / total_pts
    wide_eye = lax.broadcasted_iota(jnp.int32, (HIST, 128), 0) == lax.broadcasted_iota(
        jnp.int32, (HIST, 128), 1
    )
    mass_i[2, 0] = jnp.sum(jnp.where(wide_eye, error, 0.0), axis=0, keepdims=True)
    start(error_copies_i)
    center = raw_center * factor
    center_ref[...] = center
    scale_v_ref[...] = center / col_sum
    stores[0].start()
    stores[2].start()
    sent(mass_copies_i)
    received(error_copies_i)
    misfit_ref[...] = jnp.sum(mass_i[2], axis=0)[:, 0:HIST]
    stores[3].start()
    sent(error_copies_i)
    for store in stores:
        store.wait()


def hand_over(center, scale_u, scale_v, misfit, center_out, scale_u_out, scale_v_out, misfit_out):
    center_out[...] = center[0]
    scale_u_out[...] = scale_u[...]
    scale_v_out[...] = scale_v[...]
    misfit_out[...] = misfit[0]


def shards(embeddings, counts, raw_weights):
    total_pts = embeddings.shape[0] * lax.axis_size("row") * lax.axis_size("col")
    vmem = pl.BlockSpec(memory_space=pltpu.VMEM)
    anywhere = pl.BlockSpec(memory_space=pl.ANY)
    f32, bf16, dma = jnp.float32, jnp.bfloat16, pltpu.SemaphoreType.DMA
    pair_i, pair_j = [dma((PER_I,))] * 2, [dma((PER_J,))] * 2
    center, scale_u, scale_v, misfit = pl.pallas_call(
        functools.partial(body, total_pts),
        out_shape=(
            jax.ShapeDtypeStruct((1, OWN), f32),
            jax.ShapeDtypeStruct((HIST, OWN), f32),
            jax.ShapeDtypeStruct((HIST, OWN), f32),
            jax.ShapeDtypeStruct((1, HIST), f32),
        ),
        in_specs=[anywhere] * 3,
        out_specs=(anywhere,) * 4,
        scratch_shapes=[
            pltpu.VMEM((ROWS, COLS), bf16),
            pltpu.VMEM((ROWS, 128), bf16),
            pltpu.VMEM((COLS, 128), bf16),
            pltpu.VMEM((3, HIST, ROWS), bf16),
            pltpu.VMEM((HIST, COLS), f32),
            pltpu.VMEM((3, HIST, COLS), bf16),
            pltpu.VMEM((3, PER_J, HIST, OWN), bf16),
            pltpu.VMEM((8, COLS), f32),
            pltpu.VMEM((1, COLS), f32),
            pltpu.VMEM((PER_J, 1, OWN), f32),
            pltpu.VMEM((HIST, OWN), f32),
            pltpu.VMEM((HIST, OWN), f32),
            pltpu.VMEM((OWN, 128), f32),
            pltpu.VMEM((HIST, OWN), jnp.int32),
            pltpu.VMEM((1, HIST), f32),
            pltpu.VMEM((HIST, ROWS), bf16),
            pltpu.VMEM((1, ROWS), f32),
            pltpu.VMEM((1, PER_I, HIST, 128), f32),
            pltpu.VMEM((1, PER_J, HIST, 128), f32),
            pltpu.VMEM((1, PER_J, HIST, OWN), f32),
            pltpu.VMEM((3, PER_I, 1, 128), f32),
            pltpu.VMEM((2, PER_J, 1, OWN), f32),
            pltpu.VMEM((1, OWN), f32),
            pltpu.VMEM((HIST, OWN), f32),
            pltpu.VMEM((HIST, OWN), f32),
            pltpu.VMEM((1, HIST), f32),
            dma((3,)),
            dma((4,)),
            pltpu.SemaphoreType.REGULAR((2,)),
            *pair_i,
            *pair_j,
            *pair_i,
            *pair_j,
            *[dma((3, PER_I))] * 2,
            *[dma((3, PER_J))] * 2,
            *[dma((1, PER_I))] * 2,
            *[dma((1, PER_J))] * 2,
            *[dma((3, PER_I))] * 2,
            *[dma((2, PER_J))] * 2,
            *[dma((1, PER_J))] * 2,
        ],
        compiler_params=pltpu.CompilerParams(
            collective_id=0, has_side_effects=True, vmem_limit_bytes=62 * 1024 * 1024
        ),
    )(embeddings, counts, raw_weights.reshape(1, HIST))
    return pl.pallas_call(
        hand_over,
        out_shape=(
            jax.ShapeDtypeStruct((OWN,), f32),
            jax.ShapeDtypeStruct((HIST, OWN), f32),
            jax.ShapeDtypeStruct((HIST, OWN), f32),
            jax.ShapeDtypeStruct((HIST,), f32),
        ),
        in_specs=[vmem] * 4,
        out_specs=(vmem,) * 4,
    )(center, scale_u, scale_v, misfit)


def solution(mesh):
    placed = (P(("row", "col"), None), P(None, ("row", "col")), P())
    return jax.shard_map(
        shards,
        mesh=mesh,
        in_specs=placed,
        out_specs=(P(("row", "col")), P(None, ("row", "col")), P(None, ("row", "col")), P()),
        check_vma=False,
    )
```

```python
import functools

import jax
import jax.numpy as jnp
from jax import lax
from jax.experimental import pallas as pl
from jax.experimental.pallas import tpu as pltpu
from jax.sharding import PartitionSpec as P

GROUP_I = ((0, 0), (1, 0), (3, 0), (0, 1), (3, 1), (2, 0), (1, 1), (2, 1))
GROUP_J = ((0, 0), (0, 1), (3, 0), (1, 0), (3, 1), (2, 0), (1, 1), (2, 1))
MESH = pl.DeviceIdType.MESH
SLOPE = 14.426950408889634
HIST = 32
OWN = 384
PER_I, PER_J = 16, 8
ROWS, COLS = OWN * PER_I, OWN * PER_J
BUILD_I, BUILD_J = 1536, 768
PASS_J = 768
EARLY = 3
ORDER = (1, 2, 3, 4, 5, 15, 14, 13, 12, 11, 10, 9, 8, 7, 6)


class Together:
    def __init__(self, copies, outgoing, incoming):
        self.copies, self.outgoing, self.incoming = copies, outgoing, incoming

    def start(self):
        for copy in self.copies:
            copy.start()

    def wait_send(self):
        self.outgoing.wait_send()

    def wait_recv(self):
        self.incoming.wait_recv()


def body(
    total_pts,
    emb_hbm,
    counts_hbm,
    weights_hbm,
    center_hbm,
    scale_u_hbm,
    scale_v_hbm,
    misfit_hbm,
    tile,
    unit_i,
    unit_j,
    x_buf,
    y_part,
    y_send,
    y_recv,
    first_part,
    first_row,
    first_recv,
    target,
    v_first,
    emb_ref,
    counts_ref,
    weights_ref,
    counts_all,
    row_all,
    wide_i,
    wide_j,
    moved_j,
    mass_i,
    raw_j,
    center_ref,
    scale_u_ref,
    scale_v_ref,
    misfit_ref,
    load_sem,
    store_sem,
    ready,
    send_unit_i,
    recv_unit_i,
    send_unit_j,
    recv_unit_j,
    send_counts,
    recv_counts,
    send_first,
    recv_first,
    send_x,
    recv_x,
    send_y,
    recv_y,
    send_wide_i,
    recv_wide_i,
    send_wide_j,
    recv_wide_j,
    send_mass_i,
    recv_mass_i,
    send_raw_j,
    recv_raw_j,
    send_moved_j,
    recv_moved_j,
):
    row, col = lax.axis_index("row"), lax.axis_index("col")
    x, core = lax.div(row, 2), lax.rem(row, 2)
    z, y = lax.div(col, 4), lax.rem(col, 4)

    def device(nx, ncore, nz, ny):
        return (nx * 2 + ncore, nz * 4 + ny)

    def device_i(k):
        dx, pair = GROUP_I[k // 2]
        ncore = 1 - core if k % 2 else core
        return device(lax.rem(x + 4 - dx, 4), ncore, z, y + 1 - 2 * lax.rem(y, 2) if pair else y)

    def device_j(k):
        dz, pair = GROUP_J[k]
        return device(x, core, lax.rem(z + 4 - dz, 4), 3 - y if pair else y)

    def owner_j(k):
        dz, pair = GROUP_J[k]
        return device(x, core, lax.rem(z + dz, 4), 3 - y if pair else y)

    sibling = device(x, 1 - core, z, y)
    near = [sibling] + [device_i(2 * s) for s in (1, 2, 3)] + [device_j(s) for s in (1, 2, 3)]

    def remote(device_id, src, dst, send, recv):
        return pltpu.make_async_remote_copy(
            src_ref=src, dst_ref=dst, send_sem=send, recv_sem=recv,
            device_id=device_id, device_id_type=MESH,
        )

    def start(copies):
        for copy in copies:
            copy.start()

    def received(copies):
        for copy in copies:
            copy.wait_recv()

    def sent(copies):
        for copy in copies:
            copy.wait_send()

    def tell_near(semaphore):
        for neighbour in near:
            pl.semaphore_signal(semaphore, inc=1, device_id=neighbour, device_id_type=MESH)

    def rows_of(k):
        return pl.ds(k * OWN, OWN)

    def lanes(value):
        return value[:, 0:128] + value[:, 128:256] + value[:, 256:384]

    loads = [
        pltpu.make_async_copy(src, dst, load_sem.at[n])
        for n, (src, dst) in enumerate(((emb_hbm, emb_ref), (counts_hbm, counts_ref), (weights_hbm, weights_ref)))
    ]
    for load in loads:
        load.start()
    barrier = pltpu.get_barrier_semaphore()
    tell_near(barrier)
    loads[0].wait()

    emb = emb_ref[...]
    squares = jnp.sum(emb * emb, axis=1, keepdims=True)
    unit = (emb * lax.rsqrt(squares + 1e-6)).astype(jnp.bfloat16)
    unit_i[0:OWN, :] = unit
    unit_j[0:OWN, :] = unit

    unit_copies_i = {
        k: remote(
            device_i(k), unit_i.at[rows_of(0)], unit_i.at[rows_of(k)],
            send_unit_i.at[k], recv_unit_i.at[k],
        )
        for k in (1, 2, 4, 6, 8, 10, 12, 14)
    }
    unit_copies_j = {
        k: remote(
            device_j(k), unit_j.at[rows_of(0)], unit_j.at[rows_of(k)],
            send_unit_j.at[k], recv_unit_j.at[k],
        )
        for k in range(1, PER_J)
    }
    forwards = {
        s: remote(
            sibling, unit_i.at[rows_of(2 * s)], unit_i.at[rows_of(2 * s + 1)],
            send_unit_i.at[2 * s + 1], recv_unit_i.at[2 * s + 1],
        )
        for s in range(1, 8)
    }

    def send_units(slots):
        for s in slots:
            unit_copies_i[2 * s].start()
            unit_copies_j[s].start()

    pl.semaphore_wait(barrier, len(near))
    unit_copies_i[1].start()
    send_units((1, 2, 3))
    for hops in range(2):
        tell_near(ready.at[hops])
        pl.semaphore_wait(ready.at[hops], len(near))
    sent([unit_copies_i[k] for k in (2, 4, 6)])
    sent([unit_copies_j[k] for k in (1, 2, 3)])
    send_units((7, 4, 5, 6))

    def together(copies, left, landed, send, recv):
        return Together(
            copies, remote(sibling, left, left, send, recv), remote(sibling, landed, landed, send, recv)
        )

    def exchange_j(buf, index, send, recv):
        copies = [
            remote(device_j(k), buf.at[index, 0], buf.at[index, k], send.at[index], recv.at[index])
            for k in range(PER_J - 1, 0, -1)
        ]
        others = buf.at[index, pl.ds(1, PER_J - 1)]
        return [together(copies, others, others, send.at[index], recv.at[index])]

    def exchange_i(buf, index, send, recv):
        copies = [
            remote(device_i(k), buf.at[index, 0], buf.at[index, k], send.at[index], recv.at[index])
            for k in range(PER_I - 1, 0, -1)
        ]
        others = buf.at[index, pl.ds(1, PER_I - 1)]
        return [together(copies, others, others, send.at[index], recv.at[index])]

    other_i, other_j = pl.ds(OWN, ROWS - OWN), pl.ds(OWN, COLS - OWN)

    loads[1].wait()
    loads[2].wait()
    counts = counts_ref[...].astype(jnp.float32)
    raw_weights = weights_ref[...]
    eye = lax.broadcasted_iota(jnp.int32, (HIST, HIST), 0) == lax.broadcasted_iota(
        jnp.int32, (HIST, HIST), 1
    )
    weights = jnp.sum(
        jnp.where(eye, raw_weights / jnp.sum(raw_weights), 0.0), axis=1, keepdims=True
    )
    totals_j = exchange_j(wide_j, 0, send_wide_j, recv_wide_j)
    totals_i = exchange_i(wide_i, 0, send_wide_i, recv_wide_i)
    wide_j[0, 0] = lanes(counts)
    start(totals_j)
    first_part[...] = jnp.zeros_like(first_part)
    first_copies = {
        k: remote(
            owner_j(k), first_row.at[:, rows_of(k)], first_recv.at[k],
            send_first.at[0], recv_first.at[0],
        )
        for k in range(1, PER_J)
    }
    first_all = together(
        [], first_row.at[:, other_j], first_recv.at[pl.ds(1, PER_J - 1)], send_first.at[0], recv_first.at[0]
    )

    counts_all[:, 0:OWN] = counts.astype(jnp.bfloat16)
    counts_copies = [
        together(
            [
                remote(
                    device_i(k), counts_all.at[:, rows_of(0)], counts_all.at[:, rows_of(k)],
                    send_counts.at[0], recv_counts.at[0],
                )
                for k in range(PER_I - 1, 0, -1)
            ],
            counts_all.at[:, other_i], counts_all.at[:, other_i], send_counts.at[0], recv_counts.at[0],
        )
    ]

    def forward(slots):
        for s in slots:
            unit_copies_i[2 * s].wait_recv()
            forwards[s].start()

    def columns_arrived(slots):
        for s in slots:
            unit_copies_j[s].wait_recv()

    def rows_arrived(slots):
        for s in slots:
            forwards[s].wait_recv()

    def build_block(at_i, at_j):
        gram = lax.dot_general(
            unit_i[at_i, :], unit_j[at_j, :], (((1,), (1,)), ((), ())),
            preferred_element_type=jnp.float32,
        )
        value = jnp.exp2(gram * SLOPE - SLOPE)
        tile[at_i, at_j] = value.astype(jnp.bfloat16)
        first_part[:, at_j] += jnp.sum(
            value.reshape(at_i.size // 8, 8, at_j.size), axis=0
        )

    def build(n, carry):
        t = (n >= 1).astype(jnp.int32) + (n >= 4).astype(jnp.int32) + (n >= 9).astype(jnp.int32)
        m = n - t * t
        down = (m < t).astype(jnp.int32)
        i = down * m + (1 - down) * t
        j = down * t + (1 - down) * (2 * t - m)

        @pl.when(n == 0)
        def _():
            forward((1,))
            unit_copies_i[1].wait_recv()
            columns_arrived((1,))
            forward((2, 3))
            rows_arrived((1,))

        @pl.when(n == 1)
        def _():
            columns_arrived((2, 3))

        @pl.when(n == 2)
        def _():
            rows_arrived((2, 3))

        @pl.when(n == 4)
        def _():
            columns_arrived((4, 5))
            forward((4, 5))

        @pl.when(n == 6)
        def _():
            rows_arrived((4, 5))
            received(totals_j)
            wide_i[0, 0] = jnp.sum(wide_j[0], axis=0)
            start(totals_i)

        build_block(
            pl.ds(pl.multiple_of(i * BUILD_I, BUILD_I), BUILD_I),
            pl.ds(pl.multiple_of(j * BUILD_J, BUILD_J), BUILD_J),
        )
        return carry

    lax.fori_loop(0, 9, build, 0)
    columns_arrived((6, 7))
    forward((6, 7))
    start(counts_copies)
    build_block(pl.ds(0, 3 * BUILD_I), pl.ds(3 * BUILD_J, BUILD_J))
    rows_arrived((6, 7))
    for last in (1, 0):
        build_block(pl.ds(3 * BUILD_I, BUILD_I), pl.ds(last * 2 * BUILD_J, 2 * BUILD_J))
        done = pl.ds(last * 2 * BUILD_J, 2 * BUILD_J)
        first_row[:, done] = jnp.sum(first_part[:, done], axis=0, keepdims=True)
        start(first_copies[k] for k in range(4 * last + 3, 4 * last - 1, -1) if k)

    first_recv[0] = first_row[:, 0:OWN]
    sent([unit_copies_i[k] for k in (1, 8, 10, 12, 14)])
    sent([unit_copies_j[k] for k in (4, 5, 6, 7)])
    sent(forwards.values())
    sent(counts_copies)
    sent(totals_j)
    received(totals_i)
    totals = jnp.sum(jnp.sum(wide_i[0], axis=0), axis=1, keepdims=True)
    per_count = total_pts / totals
    target[...] = counts * per_count
    received(counts_copies)
    first_all.wait_recv()
    row_sum = jnp.sum(first_recv[...], axis=0)

    stores = [
        pltpu.make_async_copy(src, dst, store_sem.at[n])
        for n, (src, dst) in enumerate(
            (
                (center_ref, center_hbm),
                (scale_u_ref, scale_u_hbm),
                (scale_v_ref, scale_v_hbm),
                (misfit_ref, misfit_hbm),
            )
        )
    ]

    def gather(index, buf):
        copies = {
            k: remote(
                device_i(k), buf.at[:, rows_of(0)], buf.at[:, rows_of(k)],
                send_x.at[index], recv_x.at[index, k // 2],
            )
            for k in range(1, PER_I)
        }
        start(copies[k] for k in ORDER)

        def chip(s):
            at = pl.ds(2 * s * OWN, 2 * OWN) if s else rows_of(1)
            return remote(sibling, buf.at[:, at], buf.at[:, at], send_x.at[index], recv_x.at[index, s])

        def leave():
            all_sent = buf.at[:, other_i]
            remote(sibling, all_sent, all_sent, send_x.at[index], recv_x.at[index, 0]).wait_send()

        return chip, leave

    def gather_value(index, value):
        x_buf[index, :, 0:OWN] = value.astype(jnp.bfloat16)
        chip, leave = gather(index, x_buf.at[index])

        def arrive(first, last):
            received(chip(s) for s in range(first, last))

        return arrive, leave

    def gather_first(row_sum):
        row_all[:, 0:OWN] = row_sum
        chip, leave = gather(0, row_all)

        def arrive(first, last):
            received(chip(s) for s in range(first, last))
            at = pl.ds(first * 2 * OWN, (last - first) * 2 * OWN)
            x_buf[0, :, at] = (
                counts_all[:, at].astype(jnp.float32) * per_count / row_all[:, at]
            ).astype(jnp.bfloat16)

        return arrive, leave

    def run_pass(index, gathered, before, between):
        arrive, leave = gathered
        copies = {
            k: remote(
                owner_j(k), y_send.at[index, :, rows_of(k)], y_recv.at[index, k],
                send_y.at[index], recv_y.at[index],
            )
            for k in range(1, PER_J)
        }
        y_part[...] = jnp.zeros_like(y_part)
        before()

        def by_rows(s, carry):
            for which in range(EARLY):

                @pl.when(s == which)
                def _():
                    arrive(which, which + 1)

            at = pl.ds(pl.multiple_of(s * 2 * OWN, 2 * OWN), 2 * OWN)
            y_part[...] += jnp.dot(
                x_buf[index, :, at], tile[at, :], preferred_element_type=jnp.float32
            )
            return carry

        lax.fori_loop(0, EARLY, by_rows, 0)
        between()
        arrive(EARLY, 8)
        late = pl.ds(EARLY * 2 * OWN, ROWS - EARLY * 2 * OWN)

        def by_columns(n, carry):
            q = 3 - n
            at = pl.ds(pl.multiple_of(q * PASS_J, PASS_J), PASS_J)
            value = y_part[:, at] + jnp.dot(
                x_buf[index, :, late], tile[late, at], preferred_element_type=jnp.float32
            )
            y_part[:, at] = value
            y_send[index, :, at] = value.astype(jnp.bfloat16)
            for which in range(4):

                @pl.when(q == which)
                def _():
                    for k in (2 * which + 1, 2 * which):
                        if k:
                            copies[k].start()

            return carry

        lax.fori_loop(0, 4, by_columns, 0)
        leave()
        y_all = together(
            [], y_send.at[index, :, other_j], y_recv.at[index, pl.ds(1, PER_J - 1)],
            send_y.at[index], recv_y.at[index],
        )
        y_all.wait_recv()
        total = y_part[:, 0:OWN]
        for k in range(1, PER_J):
            total += y_recv[index, k].astype(jnp.float32)
        return total, y_all.wait_send

    def raw(col_sum):
        return jnp.exp(jnp.sum(weights * jnp.log(col_sum), axis=0, keepdims=True))

    def scalar(value):
        return jnp.sum(value, axis=1, keepdims=True)

    def nothing():
        return None

    def first_sent():
        first_all.wait_send()
        sent(totals_i)

    col_sum, y_sent = run_pass(0, gather_first(row_sum), first_sent, nothing)
    raw_center = raw(col_sum)
    v_first[...] = raw_center / col_sum
    mass_copies_j = exchange_j(raw_j, 0, send_raw_j, recv_raw_j)
    mass_copies_i = exchange_i(mass_i, 0, send_mass_i, recv_mass_i)

    def mass_begin():
        raw_j[0, 0] = raw_center
        start(mass_copies_j)
        y_sent()

    def mass_next():
        received(mass_copies_j)
        mass_i[0, 0] = lanes(jnp.sum(raw_j[0], axis=0))
        start(mass_copies_i)
        sent(mass_copies_j)

    row_sum, y_sent = run_pass(1, gather_value(1, v_first[...]), mass_begin, mass_next)
    received(mass_copies_i)
    factor = total_pts / scalar(jnp.sum(mass_i[0], axis=0))
    scale_u = target[...] / (row_sum * factor)
    scale_v = v_first[...] * factor

    def second_sent():
        scale_u_ref[...] = scale_u
        stores[1].start()
        sent(mass_copies_i)
        y_sent()

    col_sum, y_sent = run_pass(2, gather_value(2, scale_u), second_sent, nothing)
    raw_center = raw(col_sum)
    raw_j[1, 0] = raw_center
    mass_copies_j = exchange_j(raw_j, 1, send_raw_j, recv_raw_j)
    start(mass_copies_j)
    mass_copies_i = exchange_i(mass_i, 1, send_mass_i, recv_mass_i)
    error_copies_j = exchange_j(moved_j, 0, send_moved_j, recv_moved_j)
    error_copies_i = exchange_i(mass_i, 2, send_mass_i, recv_mass_i)
    moved_j[0, 0] = scale_v * col_sum
    start(error_copies_j)
    y_sent()
    received(mass_copies_j)
    mass_i[1, 0] = lanes(jnp.sum(raw_j[1], axis=0))
    start(mass_copies_i)
    sent(mass_copies_j)
    received(error_copies_j)
    sent(error_copies_j)
    received(mass_copies_i)
    factor = total_pts / scalar(jnp.sum(mass_i[1], axis=0))
    error = jnp.zeros((HIST, OWN), jnp.float32)
    for k in range(PER_J):
        error += jnp.abs(moved_j[0, k] - raw_j[1, k] * factor)
    error = jnp.sum(lanes(error), axis=1, keepdims=True) / total_pts
    wide_eye = lax.broadcasted_iota(jnp.int32, (HIST, 128), 0) == lax.broadcasted_iota(
        jnp.int32, (HIST, 128), 1
    )
    mass_i[2, 0] = jnp.sum(jnp.where(wide_eye, error, 0.0), axis=0, keepdims=True)
    start(error_copies_i)
    center = raw_center * factor
    center_ref[...] = center
    scale_v_ref[...] = center / col_sum
    stores[0].start()
    stores[2].start()
    sent(mass_copies_i)
    received(error_copies_i)
    misfit_ref[...] = jnp.sum(mass_i[2], axis=0)[:, 0:HIST]
    stores[3].start()
    sent(error_copies_i)
    for store in stores:
        store.wait()


def hand_over(center, scale_u, scale_v, misfit, center_out, scale_u_out, scale_v_out, misfit_out):
    center_out[...] = center[0]
    scale_u_out[...] = scale_u[...]
    scale_v_out[...] = scale_v[...]
    misfit_out[...] = misfit[0]


def shards(embeddings, counts, raw_weights):
    total_pts = embeddings.shape[0] * lax.axis_size("row") * lax.axis_size("col")
    vmem = pl.BlockSpec(memory_space=pltpu.VMEM)
    anywhere = pl.BlockSpec(memory_space=pl.ANY)
    f32, bf16, dma = jnp.float32, jnp.bfloat16, pltpu.SemaphoreType.DMA
    pair_i, pair_j = [dma((PER_I,))] * 2, [dma((PER_J,))] * 2
    center, scale_u, scale_v, misfit = pl.pallas_call(
        functools.partial(body, total_pts),
        out_shape=(
            jax.ShapeDtypeStruct((1, OWN), f32),
            jax.ShapeDtypeStruct((HIST, OWN), f32),
            jax.ShapeDtypeStruct((HIST, OWN), f32),
            jax.ShapeDtypeStruct((1, HIST), f32),
        ),
        in_specs=[anywhere] * 3,
        out_specs=(anywhere,) * 4,
        scratch_shapes=[
            pltpu.VMEM((ROWS, COLS), bf16),
            pltpu.VMEM((ROWS, 128), bf16),
            pltpu.VMEM((COLS, 128), bf16),
            pltpu.VMEM((3, HIST, ROWS), bf16),
            pltpu.VMEM((HIST, COLS), f32),
            pltpu.VMEM((3, HIST, COLS), bf16),
            pltpu.VMEM((3, PER_J, HIST, OWN), bf16),
            pltpu.VMEM((8, COLS), f32),
            pltpu.VMEM((1, COLS), f32),
            pltpu.VMEM((PER_J, 1, OWN), f32),
            pltpu.VMEM((HIST, OWN), f32),
            pltpu.VMEM((HIST, OWN), f32),
            pltpu.VMEM((OWN, 128), f32),
            pltpu.VMEM((HIST, OWN), jnp.int32),
            pltpu.VMEM((1, HIST), f32),
            pltpu.VMEM((HIST, ROWS), bf16),
            pltpu.VMEM((1, ROWS), f32),
            pltpu.VMEM((1, PER_I, HIST, 128), f32),
            pltpu.VMEM((1, PER_J, HIST, 128), f32),
            pltpu.VMEM((1, PER_J, HIST, OWN), f32),
            pltpu.VMEM((3, PER_I, 1, 128), f32),
            pltpu.VMEM((2, PER_J, 1, OWN), f32),
            pltpu.VMEM((1, OWN), f32),
            pltpu.VMEM((HIST, OWN), f32),
            pltpu.VMEM((HIST, OWN), f32),
            pltpu.VMEM((1, HIST), f32),
            dma((3,)),
            dma((4,)),
            pltpu.SemaphoreType.REGULAR((2,)),
            *pair_i,
            *pair_j,
            *[dma((1,))] * 2,
            *[dma((1,))] * 2,
            dma((3,)),
            dma((3, PER_I // 2)),
            *[dma((3,))] * 2,
            *[dma((1,))] * 2,
            *[dma((1,))] * 2,
            *[dma((3,))] * 2,
            *[dma((2,))] * 2,
            *[dma((1,))] * 2,
        ],
        compiler_params=pltpu.CompilerParams(
            collective_id=0, has_side_effects=True, vmem_limit_bytes=62 * 1024 * 1024
        ),
    )(embeddings, counts, raw_weights.reshape(1, HIST))
    return pl.pallas_call(
        hand_over,
        out_shape=(
            jax.ShapeDtypeStruct((OWN,), f32),
            jax.ShapeDtypeStruct((HIST, OWN), f32),
            jax.ShapeDtypeStruct((HIST, OWN), f32),
            jax.ShapeDtypeStruct((HIST,), f32),
        ),
        in_specs=[vmem] * 4,
        out_specs=(vmem,) * 4,
    )(center, scale_u, scale_v, misfit)


def solution(mesh):
    placed = (P(("row", "col"), None), P(None, ("row", "col")), P())
    return jax.shard_map(
        shards,
        mesh=mesh,
        in_specs=placed,
        out_specs=(P(("row", "col")), P(None, ("row", "col")), P(None, ("row", "col")), P()),
        check_vma=False,
    )
```

```python
import functools

import jax
import jax.numpy as jnp
from jax import lax
from jax.experimental import pallas as pl
from jax.experimental.pallas import tpu as pltpu
from jax.sharding import PartitionSpec as P

GROUP_I = ((0, 0), (1, 0), (3, 0), (0, 1), (3, 1), (2, 0), (1, 1), (2, 1))
GROUP_J = ((0, 0), (0, 1), (3, 0), (1, 0), (3, 1), (2, 0), (1, 1), (2, 1))
MESH = pl.DeviceIdType.MESH
SLOPE = 14.426950408889634
HIST = 32
OWN = 384
PER_I, PER_J = 16, 8
ROWS, COLS = OWN * PER_I, OWN * PER_J
BUILD_I, BUILD_J = 1536, 768
PASS_J = 768
EARLY = 4
ORDER = (1, 2, 3, 4, 5, 15, 14, 13, 12, 11, 10, 9, 8, 7, 6)


class Together:
    def __init__(self, copies, outgoing, incoming):
        self.copies, self.outgoing, self.incoming = copies, outgoing, incoming

    def start(self):
        for copy in self.copies:
            copy.start()

    def wait_send(self):
        self.outgoing.wait_send()

    def wait_recv(self):
        self.incoming.wait_recv()


def body(
    total_pts,
    emb_hbm,
    counts_hbm,
    weights_hbm,
    center_hbm,
    scale_u_hbm,
    scale_v_hbm,
    misfit_hbm,
    tile,
    unit_i,
    unit_j,
    x_buf,
    y_part,
    y_send,
    y_recv,
    first_part,
    first_row,
    first_recv,
    target,
    v_first,
    emb_ref,
    counts_ref,
    weights_ref,
    counts_all,
    row_all,
    wide_i,
    wide_j,
    moved_j,
    mass_i,
    raw_j,
    center_ref,
    scale_u_ref,
    scale_v_ref,
    misfit_ref,
    load_sem,
    store_sem,
    ready,
    send_unit_i,
    recv_unit_i,
    send_unit_j,
    recv_unit_j,
    send_counts,
    recv_counts,
    send_first,
    recv_first,
    send_x,
    recv_x,
    send_y,
    recv_y,
    send_wide_i,
    recv_wide_i,
    send_wide_j,
    recv_wide_j,
    send_mass_i,
    recv_mass_i,
    send_raw_j,
    recv_raw_j,
    send_moved_j,
    recv_moved_j,
):
    row, col = lax.axis_index("row"), lax.axis_index("col")
    x, core = lax.div(row, 2), lax.rem(row, 2)
    z, y = lax.div(col, 4), lax.rem(col, 4)

    def device(nx, ncore, nz, ny):
        return (nx * 2 + ncore, nz * 4 + ny)

    def device_i(k):
        dx, pair = GROUP_I[k // 2]
        ncore = 1 - core if k % 2 else core
        return device(lax.rem(x + 4 - dx, 4), ncore, z, y + 1 - 2 * lax.rem(y, 2) if pair else y)

    def device_j(k):
        dz, pair = GROUP_J[k]
        return device(x, core, lax.rem(z + 4 - dz, 4), 3 - y if pair else y)

    def owner_j(k):
        dz, pair = GROUP_J[k]
        return device(x, core, lax.rem(z + dz, 4), 3 - y if pair else y)

    sibling = device(x, 1 - core, z, y)
    near = [sibling] + [device_i(2 * s) for s in (1, 2, 3)] + [device_j(s) for s in (1, 2, 3)]

    def remote(device_id, src, dst, send, recv):
        return pltpu.make_async_remote_copy(
            src_ref=src, dst_ref=dst, send_sem=send, recv_sem=recv,
            device_id=device_id, device_id_type=MESH,
        )

    def start(copies):
        for copy in copies:
            copy.start()

    def received(copies):
        for copy in copies:
            copy.wait_recv()

    def sent(copies):
        for copy in copies:
            copy.wait_send()

    def tell_near(semaphore):
        for neighbour in near:
            pl.semaphore_signal(semaphore, inc=1, device_id=neighbour, device_id_type=MESH)

    def rows_of(k):
        return pl.ds(k * OWN, OWN)

    def lanes(value):
        return value[:, 0:128] + value[:, 128:256] + value[:, 256:384]

    loads = [
        pltpu.make_async_copy(src, dst, load_sem.at[n])
        for n, (src, dst) in enumerate(((emb_hbm, emb_ref), (counts_hbm, counts_ref), (weights_hbm, weights_ref)))
    ]
    for load in loads:
        load.start()
    barrier = pltpu.get_barrier_semaphore()
    tell_near(barrier)
    loads[0].wait()

    emb = emb_ref[...]
    squares = jnp.sum(emb * emb, axis=1, keepdims=True)
    unit = (emb * lax.rsqrt(squares + 1e-6)).astype(jnp.bfloat16)
    unit_i[0:OWN, :] = unit
    unit_j[0:OWN, :] = unit

    unit_copies_i = {
        k: remote(
            device_i(k), unit_i.at[rows_of(0)], unit_i.at[rows_of(k)],
            send_unit_i.at[0 if k < 8 else 1], recv_unit_i.at[4 if k == 1 else k // 4],
        )
        for k in (1, 2, 4, 6, 8, 10, 12, 14)
    }
    unit_copies_j = {
        k: remote(
            device_j(k), unit_j.at[rows_of(0)], unit_j.at[rows_of(k)],
            send_unit_j.at[0 if k < 4 else 1], recv_unit_j.at[k // 2],
        )
        for k in range(1, PER_J)
    }
    forwards = {
        s: remote(
            sibling, unit_i.at[rows_of(2 * s)], unit_i.at[rows_of(2 * s + 1)],
            send_unit_i.at[2], recv_unit_i.at[5 + s // 2],
        )
        for s in range(1, 8)
    }

    def send_units(slots):
        for s in slots:
            unit_copies_i[2 * s].start()
            unit_copies_j[s].start()

    def units(buf, shares, semaphore):
        some = buf.at[pl.ds(0, shares * OWN)]
        return remote(sibling, some, some, semaphore, semaphore)

    pl.semaphore_wait(barrier, len(near))
    unit_copies_i[1].start()
    send_units((1, 2, 3))
    for hops in range(2):
        tell_near(ready.at[hops])
        pl.semaphore_wait(ready.at[hops], len(near))
    units(unit_i, 4, send_unit_i.at[0]).wait_send()
    units(unit_j, 3, send_unit_j.at[0]).wait_send()
    send_units((7, 4, 5, 6))

    def together(copies, left, landed, send, recv):
        return Together(
            copies, remote(sibling, left, left, send, recv), remote(sibling, landed, landed, send, recv)
        )

    def exchange_j(buf, index, send, recv):
        copies = [
            remote(device_j(k), buf.at[index, 0], buf.at[index, k], send.at[index], recv.at[index])
            for k in range(PER_J - 1, 0, -1)
        ]
        others = buf.at[index, pl.ds(1, PER_J - 1)]
        return [together(copies, others, others, send.at[index], recv.at[index])]

    def exchange_i(buf, index, send, recv):
        copies = [
            remote(device_i(k), buf.at[index, 0], buf.at[index, k], send.at[index], recv.at[index])
            for k in range(PER_I - 1, 0, -1)
        ]
        others = buf.at[index, pl.ds(1, PER_I - 1)]
        return [together(copies, others, others, send.at[index], recv.at[index])]

    other_i, other_j = pl.ds(OWN, ROWS - OWN), pl.ds(OWN, COLS - OWN)

    loads[1].wait()
    loads[2].wait()
    counts = counts_ref[...].astype(jnp.float32)
    raw_weights = weights_ref[...]
    eye = lax.broadcasted_iota(jnp.int32, (HIST, HIST), 0) == lax.broadcasted_iota(
        jnp.int32, (HIST, HIST), 1
    )
    weights = jnp.sum(
        jnp.where(eye, raw_weights / jnp.sum(raw_weights), 0.0), axis=1, keepdims=True
    )
    totals_j = exchange_j(wide_j, 0, send_wide_j, recv_wide_j)
    totals_i = exchange_i(wide_i, 0, send_wide_i, recv_wide_i)
    wide_j[0, 0] = lanes(counts)
    start(totals_j)
    first_part[...] = jnp.zeros_like(first_part)
    first_copies = {
        k: remote(
            owner_j(k), first_row.at[:, rows_of(k)], first_recv.at[k],
            send_first.at[0], recv_first.at[0],
        )
        for k in range(1, PER_J)
    }
    first_all = together(
        [], first_row.at[:, other_j], first_recv.at[pl.ds(1, PER_J - 1)], send_first.at[0], recv_first.at[0]
    )

    counts_all[:, 0:OWN] = counts.astype(jnp.bfloat16)
    counts_copies = [
        together(
            [
                remote(
                    device_i(k), counts_all.at[:, rows_of(0)], counts_all.at[:, rows_of(k)],
                    send_counts.at[0], recv_counts.at[0],
                )
                for k in range(PER_I - 1, 0, -1)
            ],
            counts_all.at[:, other_i], counts_all.at[:, other_i], send_counts.at[0], recv_counts.at[0],
        )
    ]

    def forward(slots):
        units(unit_i, len(slots), recv_unit_i.at[slots[0] // 2]).wait_recv()
        for s in slots:
            forwards[s].start()

    def columns_arrived(slots):
        units(unit_j, len(slots), recv_unit_j.at[slots[0] // 2]).wait_recv()

    def rows_arrived(slots):
        units(unit_i, len(slots), recv_unit_i.at[5 + slots[0] // 2]).wait_recv()

    def build_block(at_i, at_j):
        gram = lax.dot_general(
            unit_i[at_i, :], unit_j[at_j, :], (((1,), (1,)), ((), ())),
            preferred_element_type=jnp.float32,
        )
        value = jnp.exp2(gram * SLOPE - SLOPE)
        tile[at_i, at_j] = value.astype(jnp.bfloat16)
        first_part[:, at_j] += jnp.sum(
            value.reshape(at_i.size // 8, 8, at_j.size), axis=0
        )

    def build(n, carry):
        t = (n >= 1).astype(jnp.int32) + (n >= 4).astype(jnp.int32) + (n >= 9).astype(jnp.int32)
        m = n - t * t
        down = (m < t).astype(jnp.int32)
        i = down * m + (1 - down) * t
        j = down * t + (1 - down) * (2 * t - m)

        @pl.when(n == 0)
        def _():
            forward((1,))
            unit_copies_i[1].wait_recv()
            columns_arrived((1,))
            forward((2, 3))
            rows_arrived((1,))

        @pl.when(n == 1)
        def _():
            columns_arrived((2, 3))

        @pl.when(n == 2)
        def _():
            rows_arrived((2, 3))

        @pl.when(n == 4)
        def _():
            columns_arrived((4, 5))
            forward((4, 5))

        @pl.when(n == 6)
        def _():
            rows_arrived((4, 5))
            received(totals_j)
            wide_i[0, 0] = jnp.sum(wide_j[0], axis=0)
            start(totals_i)

        build_block(
            pl.ds(pl.multiple_of(i * BUILD_I, BUILD_I), BUILD_I),
            pl.ds(pl.multiple_of(j * BUILD_J, BUILD_J), BUILD_J),
        )
        return carry

    lax.fori_loop(0, 9, build, 0)
    columns_arrived((6, 7))
    forward((6, 7))
    start(counts_copies)
    build_block(pl.ds(0, 3 * BUILD_I), pl.ds(3 * BUILD_J, BUILD_J))
    rows_arrived((6, 7))
    for last in (1, 0):
        build_block(pl.ds(3 * BUILD_I, BUILD_I), pl.ds(last * 2 * BUILD_J, 2 * BUILD_J))
        done = pl.ds(last * 2 * BUILD_J, 2 * BUILD_J)
        first_row[:, done] = jnp.sum(first_part[:, done], axis=0, keepdims=True)
        start(first_copies[k] for k in range(4 * last + 3, 4 * last - 1, -1) if k)

    first_recv[0] = first_row[:, 0:OWN]
    units(unit_i, 4, send_unit_i.at[1]).wait_send()
    units(unit_j, 4, send_unit_j.at[1]).wait_send()
    units(unit_i, 7, send_unit_i.at[2]).wait_send()
    sent(counts_copies)
    sent(totals_j)
    received(totals_i)
    totals = jnp.sum(jnp.sum(wide_i[0], axis=0), axis=1, keepdims=True)
    per_count = total_pts / totals
    target[...] = counts * per_count
    received(counts_copies)
    first_all.wait_recv()
    row_sum = jnp.sum(first_recv[...], axis=0)

    stores = [
        pltpu.make_async_copy(src, dst, store_sem.at[n])
        for n, (src, dst) in enumerate(
            (
                (center_ref, center_hbm),
                (scale_u_ref, scale_u_hbm),
                (scale_v_ref, scale_v_hbm),
                (misfit_ref, misfit_hbm),
            )
        )
    ]

    def gather(index, buf):
        copies = {
            k: remote(
                device_i(k), buf.at[:, rows_of(0)], buf.at[:, rows_of(k)],
                send_x.at[index], recv_x.at[index, min(k // 2, EARLY)],
            )
            for k in range(1, PER_I)
        }
        start(copies[k] for k in ORDER)

        def chips(first, last):
            at = pl.ds(max(2 * first, 1) * OWN, (2 * last - max(2 * first, 1)) * OWN)
            remote(
                sibling, buf.at[:, at], buf.at[:, at], send_x.at[index], recv_x.at[index, first]
            ).wait_recv()

        def leave():
            all_sent = buf.at[:, other_i]
            remote(sibling, all_sent, all_sent, send_x.at[index], recv_x.at[index, 0]).wait_send()

        return chips, leave

    def gather_value(index, value):
        x_buf[index, :, 0:OWN] = value.astype(jnp.bfloat16)
        return gather(index, x_buf.at[index])

    def gather_first(row_sum):
        row_all[:, 0:OWN] = row_sum
        chips, leave = gather(0, row_all)

        def arrive(first, last):
            chips(first, last)
            at = pl.ds(first * 2 * OWN, (last - first) * 2 * OWN)
            x_buf[0, :, at] = (
                counts_all[:, at].astype(jnp.float32) * per_count / row_all[:, at]
            ).astype(jnp.bfloat16)

        return arrive, leave

    def run_pass(index, gathered, before, between):
        arrive, leave = gathered
        copies = {
            k: remote(
                owner_j(k), y_send.at[index, :, rows_of(k)], y_recv.at[index, k],
                send_y.at[index], recv_y.at[index],
            )
            for k in range(1, PER_J)
        }
        y_part[...] = jnp.zeros_like(y_part)
        before()

        def by_rows(s, carry):
            for which in range(EARLY):

                @pl.when(s == which)
                def _():
                    arrive(which, which + 1)

            at = pl.ds(pl.multiple_of(s * 2 * OWN, 2 * OWN), 2 * OWN)
            y_part[...] += jnp.dot(
                x_buf[index, :, at], tile[at, :], preferred_element_type=jnp.float32
            )
            return carry

        lax.fori_loop(0, EARLY, by_rows, 0)
        between()
        arrive(EARLY, 8)
        late = pl.ds(EARLY * 2 * OWN, ROWS - EARLY * 2 * OWN)

        def by_columns(n, carry):
            q = 3 - n
            at = pl.ds(pl.multiple_of(q * PASS_J, PASS_J), PASS_J)
            value = y_part[:, at] + jnp.dot(
                x_buf[index, :, late], tile[late, at], preferred_element_type=jnp.float32
            )
            y_part[:, at] = value
            y_send[index, :, at] = value.astype(jnp.bfloat16)
            for which in range(4):

                @pl.when(q == which)
                def _():
                    for k in (2 * which + 1, 2 * which):
                        if k:
                            copies[k].start()

            return carry

        lax.fori_loop(0, 4, by_columns, 0)
        leave()
        y_all = together(
            [], y_send.at[index, :, other_j], y_recv.at[index, pl.ds(1, PER_J - 1)],
            send_y.at[index], recv_y.at[index],
        )
        y_all.wait_recv()
        total = y_part[:, 0:OWN]
        for k in range(1, PER_J):
            total += y_recv[index, k].astype(jnp.float32)
        return total, y_all.wait_send

    def raw(col_sum):
        return jnp.exp(jnp.sum(weights * jnp.log(col_sum), axis=0, keepdims=True))

    def scalar(value):
        return jnp.sum(value, axis=1, keepdims=True)

    def nothing():
        return None

    def first_sent():
        first_all.wait_send()
        sent(totals_i)

    col_sum, y_sent = run_pass(0, gather_first(row_sum), first_sent, nothing)
    raw_center = raw(col_sum)
    v_first[...] = raw_center / col_sum
    mass_copies_j = exchange_j(raw_j, 0, send_raw_j, recv_raw_j)
    mass_copies_i = exchange_i(mass_i, 0, send_mass_i, recv_mass_i)

    def mass_begin():
        raw_j[0, 0] = raw_center
        start(mass_copies_j)
        y_sent()

    def mass_next():
        received(mass_copies_j)
        mass_i[0, 0] = lanes(jnp.sum(raw_j[0], axis=0))
        start(mass_copies_i)
        sent(mass_copies_j)

    row_sum, y_sent = run_pass(1, gather_value(1, v_first[...]), mass_begin, mass_next)
    received(mass_copies_i)
    factor = total_pts / scalar(jnp.sum(mass_i[0], axis=0))
    scale_u = target[...] / (row_sum * factor)
    scale_v = v_first[...] * factor

    def second_sent():
        scale_u_ref[...] = scale_u
        stores[1].start()
        sent(mass_copies_i)
        y_sent()

    col_sum, y_sent = run_pass(2, gather_value(2, scale_u), second_sent, nothing)
    raw_center = raw(col_sum)
    raw_j[1, 0] = raw_center
    mass_copies_j = exchange_j(raw_j, 1, send_raw_j, recv_raw_j)
    start(mass_copies_j)
    mass_copies_i = exchange_i(mass_i, 1, send_mass_i, recv_mass_i)
    error_copies_j = exchange_j(moved_j, 0, send_moved_j, recv_moved_j)
    error_copies_i = exchange_i(mass_i, 2, send_mass_i, recv_mass_i)
    moved_j[0, 0] = scale_v * col_sum
    start(error_copies_j)
    y_sent()
    received(mass_copies_j)
    mass_i[1, 0] = lanes(jnp.sum(raw_j[1], axis=0))
    start(mass_copies_i)
    sent(mass_copies_j)
    received(error_copies_j)
    sent(error_copies_j)
    received(mass_copies_i)
    factor = total_pts / scalar(jnp.sum(mass_i[1], axis=0))
    error = jnp.zeros((HIST, OWN), jnp.float32)
    for k in range(PER_J):
        error += jnp.abs(moved_j[0, k] - raw_j[1, k] * factor)
    error = jnp.sum(lanes(error), axis=1, keepdims=True) / total_pts
    wide_eye = lax.broadcasted_iota(jnp.int32, (HIST, 128), 0) == lax.broadcasted_iota(
        jnp.int32, (HIST, 128), 1
    )
    mass_i[2, 0] = jnp.sum(jnp.where(wide_eye, error, 0.0), axis=0, keepdims=True)
    start(error_copies_i)
    center = raw_center * factor
    center_ref[...] = center
    scale_v_ref[...] = center / col_sum
    stores[0].start()
    stores[2].start()
    sent(mass_copies_i)
    received(error_copies_i)
    misfit_ref[...] = jnp.sum(mass_i[2], axis=0)[:, 0:HIST]
    stores[3].start()
    sent(error_copies_i)
    for store in stores:
        store.wait()


def hand_over(center, scale_u, scale_v, misfit, center_out, scale_u_out, scale_v_out, misfit_out):
    center_out[...] = center[0]
    scale_u_out[...] = scale_u[...]
    scale_v_out[...] = scale_v[...]
    misfit_out[...] = misfit[0]


def shards(embeddings, counts, raw_weights):
    total_pts = embeddings.shape[0] * lax.axis_size("row") * lax.axis_size("col")
    vmem = pl.BlockSpec(memory_space=pltpu.VMEM)
    anywhere = pl.BlockSpec(memory_space=pl.ANY)
    f32, bf16, dma = jnp.float32, jnp.bfloat16, pltpu.SemaphoreType.DMA
    center, scale_u, scale_v, misfit = pl.pallas_call(
        functools.partial(body, total_pts),
        out_shape=(
            jax.ShapeDtypeStruct((1, OWN), f32),
            jax.ShapeDtypeStruct((HIST, OWN), f32),
            jax.ShapeDtypeStruct((HIST, OWN), f32),
            jax.ShapeDtypeStruct((1, HIST), f32),
        ),
        in_specs=[anywhere] * 3,
        out_specs=(anywhere,) * 4,
        scratch_shapes=[
            pltpu.VMEM((ROWS, COLS), bf16),
            pltpu.VMEM((ROWS, 128), bf16),
            pltpu.VMEM((COLS, 128), bf16),
            pltpu.VMEM((3, HIST, ROWS), bf16),
            pltpu.VMEM((HIST, COLS), f32),
            pltpu.VMEM((3, HIST, COLS), bf16),
            pltpu.VMEM((3, PER_J, HIST, OWN), bf16),
            pltpu.VMEM((8, COLS), f32),
            pltpu.VMEM((1, COLS), f32),
            pltpu.VMEM((PER_J, 1, OWN), f32),
            pltpu.VMEM((HIST, OWN), f32),
            pltpu.VMEM((HIST, OWN), f32),
            pltpu.VMEM((OWN, 128), f32),
            pltpu.VMEM((HIST, OWN), jnp.int32),
            pltpu.VMEM((1, HIST), f32),
            pltpu.VMEM((HIST, ROWS), bf16),
            pltpu.VMEM((1, ROWS), f32),
            pltpu.VMEM((1, PER_I, HIST, 128), f32),
            pltpu.VMEM((1, PER_J, HIST, 128), f32),
            pltpu.VMEM((1, PER_J, HIST, OWN), f32),
            pltpu.VMEM((3, PER_I, 1, 128), f32),
            pltpu.VMEM((2, PER_J, 1, OWN), f32),
            pltpu.VMEM((1, OWN), f32),
            pltpu.VMEM((HIST, OWN), f32),
            pltpu.VMEM((HIST, OWN), f32),
            pltpu.VMEM((1, HIST), f32),
            dma((3,)),
            dma((4,)),
            pltpu.SemaphoreType.REGULAR((2,)),
            dma((3,)),
            dma((9,)),
            dma((2,)),
            dma((4,)),
            *[dma((1,))] * 2,
            *[dma((1,))] * 2,
            dma((3,)),
            dma((3, EARLY + 1)),
            *[dma((3,))] * 2,
            *[dma((1,))] * 2,
            *[dma((1,))] * 2,
            *[dma((3,))] * 2,
            *[dma((2,))] * 2,
            *[dma((1,))] * 2,
        ],
        compiler_params=pltpu.CompilerParams(
            collective_id=0, has_side_effects=True, vmem_limit_bytes=62 * 1024 * 1024
        ),
    )(embeddings, counts, raw_weights.reshape(1, HIST))
    return pl.pallas_call(
        hand_over,
        out_shape=(
            jax.ShapeDtypeStruct((OWN,), f32),
            jax.ShapeDtypeStruct((HIST, OWN), f32),
            jax.ShapeDtypeStruct((HIST, OWN), f32),
            jax.ShapeDtypeStruct((HIST,), f32),
        ),
        in_specs=[vmem] * 4,
        out_specs=(vmem,) * 4,
    )(center, scale_u, scale_v, misfit)


def solution(mesh):
    placed = (P(("row", "col"), None), P(None, ("row", "col")), P())
    return jax.shard_map(
        shards,
        mesh=mesh,
        in_specs=placed,
        out_specs=(P(("row", "col")), P(None, ("row", "col")), P(None, ("row", "col")), P()),
        check_vma=False,
    )
```

```python
import functools

import jax
import jax.numpy as jnp
from jax import lax
from jax.experimental import pallas as pl
from jax.experimental.pallas import tpu as pltpu
from jax.sharding import PartitionSpec as P

GROUP_I = ((0, 0), (1, 0), (3, 0), (0, 1), (3, 1), (2, 0), (1, 1), (2, 1))
GROUP_J = ((0, 0), (0, 1), (3, 0), (1, 0), (3, 1), (2, 0), (1, 1), (2, 1))
MESH = pl.DeviceIdType.MESH
SLOPE = 14.426950408889634
HIST = 32
OWN = 384
PER_I, PER_J = 16, 8
ROWS, COLS = OWN * PER_I, OWN * PER_J
BUILD_I, BUILD_J = 1536, 768
PASS_J = 768
EARLY = 4
ORDER = (1, 2, 3, 4, 5, 15, 14, 13, 12, 11, 10, 9, 8, 7, 6)


class Together:
    def __init__(self, copies, outgoing, incoming):
        self.copies, self.outgoing, self.incoming = copies, outgoing, incoming

    def start(self):
        for copy in self.copies:
            copy.start()

    def wait_send(self):
        self.outgoing.wait_send()

    def wait_recv(self):
        self.incoming.wait_recv()


def body(
    total_pts,
    emb_hbm,
    counts_hbm,
    weights_hbm,
    center_hbm,
    scale_u_hbm,
    scale_v_hbm,
    misfit_hbm,
    tile,
    unit_i,
    unit_j,
    x_buf,
    y_part,
    y_send,
    y_recv,
    first_part,
    first_row,
    first_recv,
    target,
    v_first,
    emb_ref,
    counts_ref,
    weights_ref,
    counts_all,
    row_all,
    wide_i,
    wide_j,
    moved_j,
    mass_i,
    raw_j,
    center_ref,
    scale_u_ref,
    scale_v_ref,
    misfit_ref,
    load_sem,
    store_sem,
    ready,
    send_unit_i,
    recv_unit_i,
    send_unit_j,
    recv_unit_j,
    send_counts,
    recv_counts,
    send_first,
    recv_first,
    send_x,
    recv_x,
    send_y,
    recv_y,
    send_wide_i,
    recv_wide_i,
    send_wide_j,
    recv_wide_j,
    send_mass_i,
    recv_mass_i,
    send_raw_j,
    recv_raw_j,
    send_moved_j,
    recv_moved_j,
):
    row, col = lax.axis_index("row"), lax.axis_index("col")
    x, core = lax.div(row, 2), lax.rem(row, 2)
    z, y = lax.div(col, 4), lax.rem(col, 4)

    def device(nx, ncore, nz, ny):
        return (nx * 2 + ncore, nz * 4 + ny)

    def device_i(k):
        dx, pair = GROUP_I[k // 2]
        ncore = 1 - core if k % 2 else core
        return device(lax.rem(x + 4 - dx, 4), ncore, z, y + 1 - 2 * lax.rem(y, 2) if pair else y)

    def device_j(k):
        dz, pair = GROUP_J[k]
        return device(x, core, lax.rem(z + 4 - dz, 4), 3 - y if pair else y)

    def owner_j(k):
        dz, pair = GROUP_J[k]
        return device(x, core, lax.rem(z + dz, 4), 3 - y if pair else y)

    sibling = device(x, 1 - core, z, y)
    near = [sibling] + [device_i(2 * s) for s in (1, 2, 3)] + [device_j(s) for s in (1, 2, 3)]

    def remote(device_id, src, dst, send, recv):
        return pltpu.make_async_remote_copy(
            src_ref=src, dst_ref=dst, send_sem=send, recv_sem=recv,
            device_id=device_id, device_id_type=MESH,
        )

    def start(copies):
        for copy in copies:
            copy.start()

    def received(copies):
        for copy in copies:
            copy.wait_recv()

    def sent(copies):
        for copy in copies:
            copy.wait_send()

    def tell_near(semaphore):
        for neighbour in near:
            pl.semaphore_signal(semaphore, inc=1, device_id=neighbour, device_id_type=MESH)

    def rows_of(k):
        return pl.ds(k * OWN, OWN)

    def lanes(value):
        return value[:, 0:128] + value[:, 128:256] + value[:, 256:384]

    loads = [
        pltpu.make_async_copy(src, dst, load_sem.at[n])
        for n, (src, dst) in enumerate(((emb_hbm, emb_ref), (counts_hbm, counts_ref), (weights_hbm, weights_ref)))
    ]
    for load in loads:
        load.start()
    barrier = pltpu.get_barrier_semaphore()
    tell_near(barrier)
    loads[0].wait()

    emb = emb_ref[...]
    squares = jnp.sum(emb * emb, axis=1, keepdims=True)
    unit = (emb * lax.rsqrt(squares + 1e-6)).astype(jnp.bfloat16)
    unit_i[0:OWN, :] = unit
    unit_j[0:OWN, :] = unit

    unit_copies_i = {
        k: remote(
            device_i(k), unit_i.at[rows_of(0)], unit_i.at[rows_of(k)],
            send_unit_i.at[0 if k < 8 else 1], recv_unit_i.at[4 if k == 1 else k // 4],
        )
        for k in (1, 2, 4, 6, 8, 10, 12, 14)
    }
    unit_copies_j = {
        k: remote(
            device_j(k), unit_j.at[rows_of(0)], unit_j.at[rows_of(k)],
            send_unit_j.at[0 if k < 4 else 1], recv_unit_j.at[k // 2],
        )
        for k in range(1, PER_J)
    }
    forwards = {
        s: remote(
            sibling, unit_i.at[rows_of(2 * s)], unit_i.at[rows_of(2 * s + 1)],
            send_unit_i.at[2], recv_unit_i.at[5 + s // 2],
        )
        for s in range(1, 8)
    }

    def send_units(slots):
        for s in slots:
            unit_copies_i[2 * s].start()
            unit_copies_j[s].start()

    def units(buf, shares, semaphore):
        some = buf.at[pl.ds(0, shares * OWN)]
        return remote(sibling, some, some, semaphore, semaphore)

    pl.semaphore_wait(barrier, len(near))
    unit_copies_i[1].start()
    send_units((1, 2, 3))
    for hops in range(2):
        tell_near(ready.at[hops])
        pl.semaphore_wait(ready.at[hops], len(near))
    units(unit_i, 4, send_unit_i.at[0]).wait_send()
    units(unit_j, 3, send_unit_j.at[0]).wait_send()
    send_units((7, 4, 5, 6))

    def together(copies, left, landed, send, recv):
        return Together(
            copies, remote(sibling, left, left, send, recv), remote(sibling, landed, landed, send, recv)
        )

    def exchange_j(buf, index, send, recv):
        copies = [
            remote(device_j(k), buf.at[index, 0], buf.at[index, k], send.at[index], recv.at[index])
            for k in range(PER_J - 1, 0, -1)
        ]
        others = buf.at[index, pl.ds(1, PER_J - 1)]
        return [together(copies, others, others, send.at[index], recv.at[index])]

    def exchange_i(buf, index, send, recv):
        copies = [
            remote(device_i(k), buf.at[index, 0], buf.at[index, k], send.at[index], recv.at[index])
            for k in range(PER_I - 1, 0, -1)
        ]
        others = buf.at[index, pl.ds(1, PER_I - 1)]
        return [together(copies, others, others, send.at[index], recv.at[index])]

    other_i, other_j = pl.ds(OWN, ROWS - OWN), pl.ds(OWN, COLS - OWN)

    loads[1].wait()
    loads[2].wait()
    counts = counts_ref[...].astype(jnp.float32)
    raw_weights = weights_ref[...]
    eye = lax.broadcasted_iota(jnp.int32, (HIST, HIST), 0) == lax.broadcasted_iota(
        jnp.int32, (HIST, HIST), 1
    )
    weights = jnp.sum(
        jnp.where(eye, raw_weights / jnp.sum(raw_weights), 0.0), axis=1, keepdims=True
    )
    totals_j = exchange_j(wide_j, 0, send_wide_j, recv_wide_j)
    totals_i = exchange_i(wide_i, 0, send_wide_i, recv_wide_i)
    wide_eye = lax.broadcasted_iota(jnp.int32, (HIST, 128), 0) == lax.broadcasted_iota(
        jnp.int32, (HIST, 128), 1
    )

    def as_row(value):
        return jnp.sum(jnp.where(wide_eye, value, 0.0), axis=0, keepdims=True)

    wide_j[0, 0] = as_row(jnp.sum(lanes(counts), axis=1, keepdims=True))
    start(totals_j)
    first_part[...] = jnp.zeros_like(first_part)
    first_copies = {
        k: remote(
            owner_j(k), first_row.at[:, rows_of(k)], first_recv.at[k],
            send_first.at[0], recv_first.at[0],
        )
        for k in range(1, PER_J)
    }
    first_all = together(
        [], first_row.at[:, other_j], first_recv.at[pl.ds(1, PER_J - 1)], send_first.at[0], recv_first.at[0]
    )

    counts_all[:, 0:OWN] = counts.astype(jnp.bfloat16)
    counts_copies = [
        together(
            [
                remote(
                    device_i(k), counts_all.at[:, rows_of(0)], counts_all.at[:, rows_of(k)],
                    send_counts.at[0], recv_counts.at[0],
                )
                for k in range(PER_I - 1, 0, -1)
            ],
            counts_all.at[:, other_i], counts_all.at[:, other_i], send_counts.at[0], recv_counts.at[0],
        )
    ]

    def forward(slots):
        units(unit_i, len(slots), recv_unit_i.at[slots[0] // 2]).wait_recv()
        for s in slots:
            forwards[s].start()

    def columns_arrived(slots):
        units(unit_j, len(slots), recv_unit_j.at[slots[0] // 2]).wait_recv()

    def rows_arrived(slots):
        units(unit_i, len(slots), recv_unit_i.at[5 + slots[0] // 2]).wait_recv()

    def build_block(at_i, at_j):
        gram = lax.dot_general(
            unit_i[at_i, :], unit_j[at_j, :], (((1,), (1,)), ((), ())),
            preferred_element_type=jnp.float32,
        )
        value = jnp.exp2(gram * SLOPE - SLOPE)
        tile[at_i, at_j] = value.astype(jnp.bfloat16)
        first_part[:, at_j] += jnp.sum(
            value.reshape(at_i.size // 8, 8, at_j.size), axis=0
        )

    def build(n, carry):
        t = (n >= 1).astype(jnp.int32) + (n >= 4).astype(jnp.int32) + (n >= 9).astype(jnp.int32)
        m = n - t * t
        down = (m < t).astype(jnp.int32)
        i = down * m + (1 - down) * t
        j = down * t + (1 - down) * (2 * t - m)

        @pl.when(n == 0)
        def _():
            forward((1,))
            unit_copies_i[1].wait_recv()
            columns_arrived((1,))
            forward((2, 3))
            rows_arrived((1,))

        @pl.when(n == 1)
        def _():
            columns_arrived((2, 3))

        @pl.when(n == 2)
        def _():
            rows_arrived((2, 3))

        @pl.when(n == 4)
        def _():
            columns_arrived((4, 5))
            forward((4, 5))

        @pl.when(n == 6)
        def _():
            rows_arrived((4, 5))
            received(totals_j)
            wide_i[0, 0] = jnp.sum(wide_j[0], axis=0)
            start(totals_i)

        build_block(
            pl.ds(pl.multiple_of(i * BUILD_I, BUILD_I), BUILD_I),
            pl.ds(pl.multiple_of(j * BUILD_J, BUILD_J), BUILD_J),
        )
        return carry

    lax.fori_loop(0, 9, build, 0)
    columns_arrived((6, 7))
    forward((6, 7))
    start(counts_copies)
    build_block(pl.ds(0, 3 * BUILD_I), pl.ds(3 * BUILD_J, BUILD_J))
    rows_arrived((6, 7))
    for last in (1, 0):
        build_block(pl.ds(3 * BUILD_I, BUILD_I), pl.ds(last * 2 * BUILD_J, 2 * BUILD_J))
        done = pl.ds(last * 2 * BUILD_J, 2 * BUILD_J)
        first_row[:, done] = jnp.sum(first_part[:, done], axis=0, keepdims=True)
        start(first_copies[k] for k in range(4 * last + 3, 4 * last - 1, -1) if k)

    first_recv[0] = first_row[:, 0:OWN]
    units(unit_i, 4, send_unit_i.at[1]).wait_send()
    units(unit_j, 4, send_unit_j.at[1]).wait_send()
    units(unit_i, 7, send_unit_i.at[2]).wait_send()
    sent(counts_copies)
    sent(totals_j)
    received(totals_i)
    totals = jnp.sum(
        jnp.where(wide_eye, jnp.sum(wide_i[0], axis=0), 0.0), axis=1, keepdims=True
    )
    per_count = total_pts / totals
    target[...] = counts * per_count
    received(counts_copies)
    first_all.wait_recv()
    row_sum = jnp.sum(first_recv[...], axis=0)

    stores = [
        pltpu.make_async_copy(src, dst, store_sem.at[n])
        for n, (src, dst) in enumerate(
            (
                (center_ref, center_hbm),
                (scale_u_ref, scale_u_hbm),
                (scale_v_ref, scale_v_hbm),
                (misfit_ref, misfit_hbm),
            )
        )
    ]

    def gather(index, buf):
        copies = {
            k: remote(
                device_i(k), buf.at[:, rows_of(0)], buf.at[:, rows_of(k)],
                send_x.at[index], recv_x.at[index, min(k // 2, EARLY)],
            )
            for k in range(1, PER_I)
        }
        start(copies[k] for k in ORDER)

        def chips(first, last):
            at = pl.ds(max(2 * first, 1) * OWN, (2 * last - max(2 * first, 1)) * OWN)
            remote(
                sibling, buf.at[:, at], buf.at[:, at], send_x.at[index], recv_x.at[index, first]
            ).wait_recv()

        def leave():
            all_sent = buf.at[:, other_i]
            remote(sibling, all_sent, all_sent, send_x.at[index], recv_x.at[index, 0]).wait_send()

        return chips, leave

    def gather_value(index, value):
        x_buf[index, :, 0:OWN] = value.astype(jnp.bfloat16)
        return gather(index, x_buf.at[index])

    def gather_first(row_sum):
        row_all[:, 0:OWN] = row_sum
        chips, leave = gather(0, row_all)

        def arrive(first, last):
            chips(first, last)
            at = pl.ds(first * 2 * OWN, (last - first) * 2 * OWN)
            x_buf[0, :, at] = (
                counts_all[:, at].astype(jnp.float32) * per_count / row_all[:, at]
            ).astype(jnp.bfloat16)

        return arrive, leave

    def run_pass(index, gathered, before, between):
        arrive, leave = gathered
        copies = {
            k: remote(
                owner_j(k), y_send.at[index, :, rows_of(k)], y_recv.at[index, k],
                send_y.at[index], recv_y.at[index],
            )
            for k in range(1, PER_J)
        }
        y_part[...] = jnp.zeros_like(y_part)
        before()

        def by_rows(s, carry):
            for which in range(EARLY):

                @pl.when(s == which)
                def _():
                    arrive(which, which + 1)

            at = pl.ds(pl.multiple_of(s * 2 * OWN, 2 * OWN), 2 * OWN)
            y_part[...] += jnp.dot(
                x_buf[index, :, at], tile[at, :], preferred_element_type=jnp.float32
            )
            return carry

        lax.fori_loop(0, EARLY, by_rows, 0)
        between()
        arrive(EARLY, 8)
        late = pl.ds(EARLY * 2 * OWN, ROWS - EARLY * 2 * OWN)

        def by_columns(n, carry):
            q = 3 - n
            at = pl.ds(pl.multiple_of(q * PASS_J, PASS_J), PASS_J)
            value = y_part[:, at] + jnp.dot(
                x_buf[index, :, late], tile[late, at], preferred_element_type=jnp.float32
            )
            y_part[:, at] = value
            y_send[index, :, at] = value.astype(jnp.bfloat16)
            for which in range(4):

                @pl.when(q == which)
                def _():
                    for k in (2 * which + 1, 2 * which):
                        if k:
                            copies[k].start()

            return carry

        lax.fori_loop(0, 4, by_columns, 0)
        leave()
        y_all = together(
            [], y_send.at[index, :, other_j], y_recv.at[index, pl.ds(1, PER_J - 1)],
            send_y.at[index], recv_y.at[index],
        )
        y_all.wait_recv()
        total = y_part[:, 0:OWN]
        for k in range(1, PER_J):
            total += y_recv[index, k].astype(jnp.float32)
        return total, y_all.wait_send

    def raw(col_sum):
        return jnp.exp(jnp.sum(weights * jnp.log(col_sum), axis=0, keepdims=True))

    def scalar(value):
        return jnp.sum(value, axis=1, keepdims=True)

    def nothing():
        return None

    def first_sent():
        first_all.wait_send()
        sent(totals_i)

    col_sum, y_sent = run_pass(0, gather_first(row_sum), first_sent, nothing)
    raw_center = raw(col_sum)
    v_first[...] = raw_center / col_sum
    mass_copies_j = exchange_j(raw_j, 0, send_raw_j, recv_raw_j)
    mass_copies_i = exchange_i(mass_i, 0, send_mass_i, recv_mass_i)

    def mass_begin():
        raw_j[0, 0] = raw_center
        start(mass_copies_j)
        y_sent()

    def mass_next():
        received(mass_copies_j)
        mass_i[0, 0] = lanes(jnp.sum(raw_j[0], axis=0))
        start(mass_copies_i)
        sent(mass_copies_j)

    row_sum, y_sent = run_pass(1, gather_value(1, v_first[...]), mass_begin, mass_next)
    received(mass_copies_i)
    factor = total_pts / scalar(jnp.sum(mass_i[0], axis=0))
    scale_u = target[...] / (row_sum * factor)
    scale_v = v_first[...] * factor

    def second_sent():
        scale_u_ref[...] = scale_u
        stores[1].start()
        sent(mass_copies_i)
        y_sent()

    col_sum, y_sent = run_pass(2, gather_value(2, scale_u), second_sent, nothing)
    raw_center = raw(col_sum)
    raw_j[1, 0] = raw_center
    mass_copies_j = exchange_j(raw_j, 1, send_raw_j, recv_raw_j)
    start(mass_copies_j)
    mass_copies_i = exchange_i(mass_i, 1, send_mass_i, recv_mass_i)
    error_copies_j = exchange_j(moved_j, 0, send_moved_j, recv_moved_j)
    error_copies_i = exchange_i(mass_i, 2, send_mass_i, recv_mass_i)
    moved_j[0, 0] = scale_v * col_sum
    start(error_copies_j)
    y_sent()
    received(mass_copies_j)
    mass_i[1, 0] = lanes(jnp.sum(raw_j[1], axis=0))
    start(mass_copies_i)
    sent(mass_copies_j)
    received(error_copies_j)
    sent(error_copies_j)
    received(mass_copies_i)
    factor = total_pts / scalar(jnp.sum(mass_i[1], axis=0))
    error = jnp.zeros((HIST, OWN), jnp.float32)
    for k in range(PER_J):
        error += jnp.abs(moved_j[0, k] - raw_j[1, k] * factor)
    error = jnp.sum(lanes(error), axis=1, keepdims=True) / total_pts
    mass_i[2, 0] = as_row(error)
    start(error_copies_i)
    center = raw_center * factor
    center_ref[...] = center
    scale_v_ref[...] = center / col_sum
    stores[0].start()
    stores[2].start()
    sent(mass_copies_i)
    received(error_copies_i)
    misfit_ref[...] = jnp.sum(mass_i[2], axis=0)[:, 0:HIST]
    stores[3].start()
    sent(error_copies_i)
    for store in stores:
        store.wait()


def hand_over(center, scale_u, scale_v, misfit, center_out, scale_u_out, scale_v_out, misfit_out):
    center_out[...] = center[0]
    scale_u_out[...] = scale_u[...]
    scale_v_out[...] = scale_v[...]
    misfit_out[...] = misfit[0]


def shards(embeddings, counts, raw_weights):
    total_pts = embeddings.shape[0] * lax.axis_size("row") * lax.axis_size("col")
    vmem = pl.BlockSpec(memory_space=pltpu.VMEM)
    anywhere = pl.BlockSpec(memory_space=pl.ANY)
    f32, bf16, dma = jnp.float32, jnp.bfloat16, pltpu.SemaphoreType.DMA
    center, scale_u, scale_v, misfit = pl.pallas_call(
        functools.partial(body, total_pts),
        out_shape=(
            jax.ShapeDtypeStruct((1, OWN), f32),
            jax.ShapeDtypeStruct((HIST, OWN), f32),
            jax.ShapeDtypeStruct((HIST, OWN), f32),
            jax.ShapeDtypeStruct((1, HIST), f32),
        ),
        in_specs=[anywhere] * 3,
        out_specs=(anywhere,) * 4,
        scratch_shapes=[
            pltpu.VMEM((ROWS, COLS), bf16),
            pltpu.VMEM((ROWS, 128), bf16),
            pltpu.VMEM((COLS, 128), bf16),
            pltpu.VMEM((3, HIST, ROWS), bf16),
            pltpu.VMEM((HIST, COLS), f32),
            pltpu.VMEM((3, HIST, COLS), bf16),
            pltpu.VMEM((3, PER_J, HIST, OWN), bf16),
            pltpu.VMEM((8, COLS), f32),
            pltpu.VMEM((1, COLS), f32),
            pltpu.VMEM((PER_J, 1, OWN), f32),
            pltpu.VMEM((HIST, OWN), f32),
            pltpu.VMEM((HIST, OWN), f32),
            pltpu.VMEM((OWN, 128), f32),
            pltpu.VMEM((HIST, OWN), jnp.int32),
            pltpu.VMEM((1, HIST), f32),
            pltpu.VMEM((HIST, ROWS), bf16),
            pltpu.VMEM((1, ROWS), f32),
            pltpu.VMEM((1, PER_I, 1, 128), f32),
            pltpu.VMEM((1, PER_J, 1, 128), f32),
            pltpu.VMEM((1, PER_J, HIST, OWN), f32),
            pltpu.VMEM((3, PER_I, 1, 128), f32),
            pltpu.VMEM((2, PER_J, 1, OWN), f32),
            pltpu.VMEM((1, OWN), f32),
            pltpu.VMEM((HIST, OWN), f32),
            pltpu.VMEM((HIST, OWN), f32),
            pltpu.VMEM((1, HIST), f32),
            dma((3,)),
            dma((4,)),
            pltpu.SemaphoreType.REGULAR((2,)),
            dma((3,)),
            dma((9,)),
            dma((2,)),
            dma((4,)),
            *[dma((1,))] * 2,
            *[dma((1,))] * 2,
            dma((3,)),
            dma((3, EARLY + 1)),
            *[dma((3,))] * 2,
            *[dma((1,))] * 2,
            *[dma((1,))] * 2,
            *[dma((3,))] * 2,
            *[dma((2,))] * 2,
            *[dma((1,))] * 2,
        ],
        compiler_params=pltpu.CompilerParams(
            collective_id=0, has_side_effects=True, vmem_limit_bytes=62 * 1024 * 1024
        ),
    )(embeddings, counts, raw_weights.reshape(1, HIST))
    return pl.pallas_call(
        hand_over,
        out_shape=(
            jax.ShapeDtypeStruct((OWN,), f32),
            jax.ShapeDtypeStruct((HIST, OWN), f32),
            jax.ShapeDtypeStruct((HIST, OWN), f32),
            jax.ShapeDtypeStruct((HIST,), f32),
        ),
        in_specs=[vmem] * 4,
        out_specs=(vmem,) * 4,
    )(center, scale_u, scale_v, misfit)


def solution(mesh):
    placed = (P(("row", "col"), None), P(None, ("row", "col")), P())
    return jax.shard_map(
        shards,
        mesh=mesh,
        in_specs=placed,
        out_specs=(P(("row", "col")), P(None, ("row", "col")), P(None, ("row", "col")), P()),
        check_vma=False,
    )
```

```python
import functools

import jax
import jax.numpy as jnp
from jax import lax
from jax.experimental import pallas as pl
from jax.experimental.pallas import tpu as pltpu
from jax.sharding import PartitionSpec as P

GROUP_I = ((0, 0), (1, 0), (3, 0), (0, 1), (3, 1), (2, 0), (1, 1), (2, 1))
GROUP_J = ((0, 0), (0, 1), (3, 0), (1, 0), (3, 1), (2, 0), (1, 1), (2, 1))
MESH = pl.DeviceIdType.MESH
SLOPE = 14.426950408889634
HIST = 32
OWN = 384
PER_I, PER_J = 16, 8
ROWS, COLS = OWN * PER_I, OWN * PER_J
BUILD_I, BUILD_J = 1536, 768
PASS_J = 768
EARLY = 4
ORDER = (1, 2, 3, 4, 5, 6, 7, 15, 14, 13, 12, 11, 10, 9, 8)


class Together:
    def __init__(self, copies, outgoing, incoming):
        self.copies, self.outgoing, self.incoming = copies, outgoing, incoming

    def start(self):
        for copy in self.copies:
            copy.start()

    def wait_send(self):
        self.outgoing.wait_send()

    def wait_recv(self):
        self.incoming.wait_recv()


def body(
    total_pts,
    emb_hbm,
    counts_hbm,
    weights_hbm,
    center_hbm,
    scale_u_hbm,
    scale_v_hbm,
    misfit_hbm,
    tile,
    unit_i,
    unit_j,
    x_buf,
    y_part,
    y_send,
    y_recv,
    first_part,
    first_row,
    first_recv,
    target,
    v_first,
    emb_ref,
    counts_ref,
    weights_ref,
    counts_all,
    row_all,
    wide_i,
    wide_j,
    moved_j,
    mass_i,
    raw_j,
    center_ref,
    scale_u_ref,
    scale_v_ref,
    misfit_ref,
    load_sem,
    store_sem,
    ready,
    send_unit_i,
    recv_unit_i,
    send_unit_j,
    recv_unit_j,
    send_counts,
    recv_counts,
    send_first,
    recv_first,
    send_x,
    recv_x,
    send_y,
    recv_y,
    send_wide_i,
    recv_wide_i,
    send_wide_j,
    recv_wide_j,
    send_mass_i,
    recv_mass_i,
    send_raw_j,
    recv_raw_j,
    send_moved_j,
    recv_moved_j,
):
    row, col = lax.axis_index("row"), lax.axis_index("col")
    x, core = lax.div(row, 2), lax.rem(row, 2)
    z, y = lax.div(col, 4), lax.rem(col, 4)

    def device(nx, ncore, nz, ny):
        return (nx * 2 + ncore, nz * 4 + ny)

    def device_i(k):
        dx, pair = GROUP_I[k // 2]
        ncore = 1 - core if k % 2 else core
        return device(lax.rem(x + 4 - dx, 4), ncore, z, y + 1 - 2 * lax.rem(y, 2) if pair else y)

    def device_j(k):
        dz, pair = GROUP_J[k]
        return device(x, core, lax.rem(z + 4 - dz, 4), 3 - y if pair else y)

    def owner_j(k):
        dz, pair = GROUP_J[k]
        return device(x, core, lax.rem(z + dz, 4), 3 - y if pair else y)

    sibling = device(x, 1 - core, z, y)
    near = [sibling] + [device_i(2 * s) for s in (1, 2, 3)] + [device_j(s) for s in (1, 2, 3)]

    def remote(device_id, src, dst, send, recv):
        return pltpu.make_async_remote_copy(
            src_ref=src, dst_ref=dst, send_sem=send, recv_sem=recv,
            device_id=device_id, device_id_type=MESH,
        )

    def start(copies):
        for copy in copies:
            copy.start()

    def received(copies):
        for copy in copies:
            copy.wait_recv()

    def sent(copies):
        for copy in copies:
            copy.wait_send()

    def tell_near(semaphore):
        for neighbour in near:
            pl.semaphore_signal(semaphore, inc=1, device_id=neighbour, device_id_type=MESH)

    def rows_of(k):
        return pl.ds(k * OWN, OWN)

    def lanes(value):
        return value[:, 0:128] + value[:, 128:256] + value[:, 256:384]

    loads = [
        pltpu.make_async_copy(src, dst, load_sem.at[n])
        for n, (src, dst) in enumerate(((emb_hbm, emb_ref), (counts_hbm, counts_ref), (weights_hbm, weights_ref)))
    ]
    for load in loads:
        load.start()
    barrier = pltpu.get_barrier_semaphore()
    tell_near(barrier)
    loads[0].wait()

    emb = emb_ref[...]
    squares = jnp.sum(emb * emb, axis=1, keepdims=True)
    unit = (emb * lax.rsqrt(squares + 1e-6)).astype(jnp.bfloat16)
    unit_i[0:OWN, :] = unit
    unit_j[0:OWN, :] = unit

    unit_copies_i = {
        k: remote(
            device_i(k), unit_i.at[rows_of(0)], unit_i.at[rows_of(k)],
            send_unit_i.at[0 if k < 8 else 1], recv_unit_i.at[4 if k == 1 else k // 4],
        )
        for k in (1, 2, 4, 6, 8, 10, 12, 14)
    }
    unit_copies_j = {
        k: remote(
            device_j(k), unit_j.at[rows_of(0)], unit_j.at[rows_of(k)],
            send_unit_j.at[0 if k < 4 else 1], recv_unit_j.at[k // 2],
        )
        for k in range(1, PER_J)
    }
    forwards = {
        s: remote(
            sibling, unit_i.at[rows_of(2 * s)], unit_i.at[rows_of(2 * s + 1)],
            send_unit_i.at[2], recv_unit_i.at[5 + s // 2],
        )
        for s in range(1, 8)
    }

    def send_units(slots):
        for s in slots:
            unit_copies_i[2 * s].start()
            unit_copies_j[s].start()

    def units(buf, shares, semaphore):
        some = buf.at[pl.ds(0, shares * OWN)]
        return remote(sibling, some, some, semaphore, semaphore)

    pl.semaphore_wait(barrier, len(near))
    unit_copies_i[1].start()
    send_units((1, 2, 3))
    for hops in range(2):
        tell_near(ready.at[hops])
        pl.semaphore_wait(ready.at[hops], len(near))
    units(unit_i, 4, send_unit_i.at[0]).wait_send()
    units(unit_j, 3, send_unit_j.at[0]).wait_send()
    send_units((7, 4, 5, 6))

    def together(copies, left, landed, send, recv):
        return Together(
            copies, remote(sibling, left, left, send, recv), remote(sibling, landed, landed, send, recv)
        )

    def exchange_j(buf, index, send, recv):
        copies = [
            remote(device_j(k), buf.at[index, 0], buf.at[index, k], send.at[index], recv.at[index])
            for k in range(PER_J - 1, 0, -1)
        ]
        others = buf.at[index, pl.ds(1, PER_J - 1)]
        return [together(copies, others, others, send.at[index], recv.at[index])]

    def exchange_i(buf, index, send, recv):
        copies = [
            remote(device_i(k), buf.at[index, 0], buf.at[index, k], send.at[index], recv.at[index])
            for k in range(PER_I - 1, 0, -1)
        ]
        others = buf.at[index, pl.ds(1, PER_I - 1)]
        return [together(copies, others, others, send.at[index], recv.at[index])]

    other_i, other_j = pl.ds(OWN, ROWS - OWN), pl.ds(OWN, COLS - OWN)

    loads[1].wait()
    loads[2].wait()
    counts = counts_ref[...].astype(jnp.float32)
    raw_weights = weights_ref[...]
    eye = lax.broadcasted_iota(jnp.int32, (HIST, HIST), 0) == lax.broadcasted_iota(
        jnp.int32, (HIST, HIST), 1
    )
    weights = jnp.sum(
        jnp.where(eye, raw_weights / jnp.sum(raw_weights), 0.0), axis=1, keepdims=True
    )
    totals_j = exchange_j(wide_j, 0, send_wide_j, recv_wide_j)
    totals_i = exchange_i(wide_i, 0, send_wide_i, recv_wide_i)
    wide_eye = lax.broadcasted_iota(jnp.int32, (HIST, 128), 0) == lax.broadcasted_iota(
        jnp.int32, (HIST, 128), 1
    )

    def as_row(value):
        return jnp.sum(jnp.where(wide_eye, value, 0.0), axis=0, keepdims=True)

    wide_j[0, 0] = as_row(jnp.sum(lanes(counts), axis=1, keepdims=True))
    start(totals_j)
    first_part[...] = jnp.zeros_like(first_part)
    first_copies = {
        k: remote(
            owner_j(k), first_row.at[:, rows_of(k)], first_recv.at[k],
            send_first.at[0], recv_first.at[0],
        )
        for k in range(1, PER_J)
    }
    first_all = together(
        [], first_row.at[:, other_j], first_recv.at[pl.ds(1, PER_J - 1)], send_first.at[0], recv_first.at[0]
    )

    counts_all[:, 0:OWN] = counts.astype(jnp.bfloat16)
    counts_copies = [
        together(
            [
                remote(
                    device_i(k), counts_all.at[:, rows_of(0)], counts_all.at[:, rows_of(k)],
                    send_counts.at[0], recv_counts.at[0],
                )
                for k in range(PER_I - 1, 0, -1)
            ],
            counts_all.at[:, other_i], counts_all.at[:, other_i], send_counts.at[0], recv_counts.at[0],
        )
    ]

    def forward(slots):
        units(unit_i, len(slots), recv_unit_i.at[slots[0] // 2]).wait_recv()
        for s in slots:
            forwards[s].start()

    def columns_arrived(slots):
        units(unit_j, len(slots), recv_unit_j.at[slots[0] // 2]).wait_recv()

    def rows_arrived(slots):
        units(unit_i, len(slots), recv_unit_i.at[5 + slots[0] // 2]).wait_recv()

    def build_block(at_i, at_j):
        gram = lax.dot_general(
            unit_i[at_i, :], unit_j[at_j, :], (((1,), (1,)), ((), ())),
            preferred_element_type=jnp.float32,
        )
        value = jnp.exp2(gram * SLOPE - SLOPE)
        tile[at_i, at_j] = value.astype(jnp.bfloat16)
        first_part[:, at_j] += jnp.sum(
            value.reshape(at_i.size // 8, 8, at_j.size), axis=0
        )

    def build(n, carry):
        t = (n >= 1).astype(jnp.int32) + (n >= 4).astype(jnp.int32) + (n >= 9).astype(jnp.int32)
        m = n - t * t
        down = (m < t).astype(jnp.int32)
        i = down * m + (1 - down) * t
        j = down * t + (1 - down) * (2 * t - m)

        @pl.when(n == 0)
        def _():
            forward((1,))
            unit_copies_i[1].wait_recv()
            columns_arrived((1,))
            forward((2, 3))
            rows_arrived((1,))

        @pl.when(n == 1)
        def _():
            columns_arrived((2, 3))

        @pl.when(n == 2)
        def _():
            rows_arrived((2, 3))

        @pl.when(n == 4)
        def _():
            columns_arrived((4, 5))
            forward((4, 5))

        @pl.when(n == 6)
        def _():
            rows_arrived((4, 5))
            received(totals_j)
            wide_i[0, 0] = jnp.sum(wide_j[0], axis=0)
            start(totals_i)

        build_block(
            pl.ds(pl.multiple_of(i * BUILD_I, BUILD_I), BUILD_I),
            pl.ds(pl.multiple_of(j * BUILD_J, BUILD_J), BUILD_J),
        )
        return carry

    lax.fori_loop(0, 9, build, 0)
    columns_arrived((6, 7))
    forward((6, 7))
    build_block(pl.ds(0, 3 * BUILD_I), pl.ds(3 * BUILD_J, BUILD_J))
    rows_arrived((6, 7))
    start(counts_copies)
    for last in (1, 0):
        build_block(pl.ds(3 * BUILD_I, BUILD_I), pl.ds(last * 2 * BUILD_J, 2 * BUILD_J))
        done = pl.ds(last * 2 * BUILD_J, 2 * BUILD_J)
        first_row[:, done] = jnp.sum(first_part[:, done], axis=0, keepdims=True)
        start(first_copies[k] for k in range(4 * last + 3, 4 * last - 1, -1) if k)

    first_recv[0] = first_row[:, 0:OWN]
    units(unit_i, 4, send_unit_i.at[1]).wait_send()
    units(unit_j, 4, send_unit_j.at[1]).wait_send()
    units(unit_i, 7, send_unit_i.at[2]).wait_send()
    sent(counts_copies)
    sent(totals_j)
    received(totals_i)
    totals = jnp.sum(
        jnp.where(wide_eye, jnp.sum(wide_i[0], axis=0), 0.0), axis=1, keepdims=True
    )
    per_count = total_pts / totals
    target[...] = counts * per_count
    received(counts_copies)
    first_all.wait_recv()
    row_sum = jnp.sum(first_recv[...], axis=0)

    stores = [
        pltpu.make_async_copy(src, dst, store_sem.at[n])
        for n, (src, dst) in enumerate(
            (
                (center_ref, center_hbm),
                (scale_u_ref, scale_u_hbm),
                (scale_v_ref, scale_v_hbm),
                (misfit_ref, misfit_hbm),
            )
        )
    ]

    def gather(index, buf):
        copies = {
            k: remote(
                device_i(k), buf.at[:, rows_of(0)], buf.at[:, rows_of(k)],
                send_x.at[index], recv_x.at[index, min(k // 2, EARLY)],
            )
            for k in range(1, PER_I)
        }
        start(copies[k] for k in ORDER)

        def chips(first, last):
            at = pl.ds(max(2 * first, 1) * OWN, (2 * last - max(2 * first, 1)) * OWN)
            remote(
                sibling, buf.at[:, at], buf.at[:, at], send_x.at[index], recv_x.at[index, first]
            ).wait_recv()

        def leave():
            all_sent = buf.at[:, other_i]
            remote(sibling, all_sent, all_sent, send_x.at[index], recv_x.at[index, 0]).wait_send()

        return chips, leave

    def gather_value(index, value):
        x_buf[index, :, 0:OWN] = value.astype(jnp.bfloat16)
        return gather(index, x_buf.at[index])

    def gather_first(row_sum):
        row_all[:, 0:OWN] = row_sum
        chips, leave = gather(0, row_all)

        def arrive(first, last):
            chips(first, last)
            at = pl.ds(first * 2 * OWN, (last - first) * 2 * OWN)
            x_buf[0, :, at] = (
                counts_all[:, at].astype(jnp.float32) * per_count / row_all[:, at]
            ).astype(jnp.bfloat16)

        return arrive, leave

    def run_pass(index, gathered, before, between):
        arrive, leave = gathered
        copies = {
            k: remote(
                owner_j(k), y_send.at[index, :, rows_of(k)], y_recv.at[index, k],
                send_y.at[index], recv_y.at[index],
            )
            for k in range(1, PER_J)
        }
        y_part[...] = jnp.zeros_like(y_part)
        before()

        def by_rows(s, carry):
            for which in range(EARLY):

                @pl.when(s == which)
                def _():
                    arrive(which, which + 1)

            at = pl.ds(pl.multiple_of(s * 2 * OWN, 2 * OWN), 2 * OWN)
            y_part[...] += jnp.dot(
                x_buf[index, :, at], tile[at, :], preferred_element_type=jnp.float32
            )
            return carry

        lax.fori_loop(0, EARLY, by_rows, 0)
        between()
        arrive(EARLY, 8)
        late = pl.ds(EARLY * 2 * OWN, ROWS - EARLY * 2 * OWN)

        def by_columns(n, carry):
            q = 3 - n
            at = pl.ds(pl.multiple_of(q * PASS_J, PASS_J), PASS_J)
            value = y_part[:, at] + jnp.dot(
                x_buf[index, :, late], tile[late, at], preferred_element_type=jnp.float32
            )
            y_part[:, at] = value
            y_send[index, :, at] = value.astype(jnp.bfloat16)
            for which in range(4):

                @pl.when(q == which)
                def _():
                    for k in (2 * which + 1, 2 * which):
                        if k:
                            copies[k].start()

            return carry

        lax.fori_loop(0, 4, by_columns, 0)
        leave()
        y_all = together(
            [], y_send.at[index, :, other_j], y_recv.at[index, pl.ds(1, PER_J - 1)],
            send_y.at[index], recv_y.at[index],
        )
        y_all.wait_recv()
        total = y_part[:, 0:OWN]
        for k in range(1, PER_J):
            total += y_recv[index, k].astype(jnp.float32)
        return total, y_all.wait_send

    def raw(col_sum):
        return jnp.exp(jnp.sum(weights * jnp.log(col_sum), axis=0, keepdims=True))

    def scalar(value):
        return jnp.sum(value, axis=1, keepdims=True)

    def nothing():
        return None

    def first_sent():
        first_all.wait_send()
        sent(totals_i)

    col_sum, y_sent = run_pass(0, gather_first(row_sum), first_sent, nothing)
    raw_center = raw(col_sum)
    v_first[...] = raw_center / col_sum
    mass_copies_j = exchange_j(raw_j, 0, send_raw_j, recv_raw_j)
    mass_copies_i = exchange_i(mass_i, 0, send_mass_i, recv_mass_i)

    def mass_begin():
        raw_j[0, 0] = raw_center
        start(mass_copies_j)
        y_sent()

    def mass_next():
        received(mass_copies_j)
        mass_i[0, 0] = lanes(jnp.sum(raw_j[0], axis=0))
        start(mass_copies_i)
        sent(mass_copies_j)

    row_sum, y_sent = run_pass(1, gather_value(1, v_first[...]), mass_begin, mass_next)
    received(mass_copies_i)
    factor = total_pts / scalar(jnp.sum(mass_i[0], axis=0))
    scale_u = target[...] / (row_sum * factor)
    scale_v = v_first[...] * factor

    def second_sent():
        scale_u_ref[...] = scale_u
        stores[1].start()
        sent(mass_copies_i)
        y_sent()

    col_sum, y_sent = run_pass(2, gather_value(2, scale_u), second_sent, nothing)
    raw_center = raw(col_sum)
    raw_j[1, 0] = raw_center
    mass_copies_j = exchange_j(raw_j, 1, send_raw_j, recv_raw_j)
    start(mass_copies_j)
    mass_copies_i = exchange_i(mass_i, 1, send_mass_i, recv_mass_i)
    error_copies_j = exchange_j(moved_j, 0, send_moved_j, recv_moved_j)
    error_copies_i = exchange_i(mass_i, 2, send_mass_i, recv_mass_i)
    moved_j[0, 0] = scale_v * col_sum
    start(error_copies_j)
    y_sent()
    received(mass_copies_j)
    mass_i[1, 0] = lanes(jnp.sum(raw_j[1], axis=0))
    start(mass_copies_i)
    sent(mass_copies_j)
    received(error_copies_j)
    sent(error_copies_j)
    received(mass_copies_i)
    factor = total_pts / scalar(jnp.sum(mass_i[1], axis=0))
    error = jnp.zeros((HIST, OWN), jnp.float32)
    for k in range(PER_J):
        error += jnp.abs(moved_j[0, k] - raw_j[1, k] * factor)
    error = jnp.sum(lanes(error), axis=1, keepdims=True) / total_pts
    mass_i[2, 0] = as_row(error)
    start(error_copies_i)
    center = raw_center * factor
    center_ref[...] = center
    scale_v_ref[...] = center / col_sum
    stores[0].start()
    stores[2].start()
    sent(mass_copies_i)
    received(error_copies_i)
    misfit_ref[...] = jnp.sum(mass_i[2], axis=0)[:, 0:HIST]
    stores[3].start()
    sent(error_copies_i)
    for store in stores:
        store.wait()


def hand_over(center, scale_u, scale_v, misfit, center_out, scale_u_out, scale_v_out, misfit_out):
    center_out[...] = center[0]
    scale_u_out[...] = scale_u[...]
    scale_v_out[...] = scale_v[...]
    misfit_out[...] = misfit[0]


def shards(embeddings, counts, raw_weights):
    total_pts = embeddings.shape[0] * lax.axis_size("row") * lax.axis_size("col")
    vmem = pl.BlockSpec(memory_space=pltpu.VMEM)
    anywhere = pl.BlockSpec(memory_space=pl.ANY)
    f32, bf16, dma = jnp.float32, jnp.bfloat16, pltpu.SemaphoreType.DMA
    center, scale_u, scale_v, misfit = pl.pallas_call(
        functools.partial(body, total_pts),
        out_shape=(
            jax.ShapeDtypeStruct((1, OWN), f32),
            jax.ShapeDtypeStruct((HIST, OWN), f32),
            jax.ShapeDtypeStruct((HIST, OWN), f32),
            jax.ShapeDtypeStruct((1, HIST), f32),
        ),
        in_specs=[anywhere] * 3,
        out_specs=(anywhere,) * 4,
        scratch_shapes=[
            pltpu.VMEM((ROWS, COLS), bf16),
            pltpu.VMEM((ROWS, 128), bf16),
            pltpu.VMEM((COLS, 128), bf16),
            pltpu.VMEM((3, HIST, ROWS), bf16),
            pltpu.VMEM((HIST, COLS), f32),
            pltpu.VMEM((3, HIST, COLS), bf16),
            pltpu.VMEM((3, PER_J, HIST, OWN), bf16),
            pltpu.VMEM((8, COLS), f32),
            pltpu.VMEM((1, COLS), f32),
            pltpu.VMEM((PER_J, 1, OWN), f32),
            pltpu.VMEM((HIST, OWN), f32),
            pltpu.VMEM((HIST, OWN), f32),
            pltpu.VMEM((OWN, 128), f32),
            pltpu.VMEM((HIST, OWN), jnp.int32),
            pltpu.VMEM((1, HIST), f32),
            pltpu.VMEM((HIST, ROWS), bf16),
            pltpu.VMEM((1, ROWS), f32),
            pltpu.VMEM((1, PER_I, 1, 128), f32),
            pltpu.VMEM((1, PER_J, 1, 128), f32),
            pltpu.VMEM((1, PER_J, HIST, OWN), f32),
            pltpu.VMEM((3, PER_I, 1, 128), f32),
            pltpu.VMEM((2, PER_J, 1, OWN), f32),
            pltpu.VMEM((1, OWN), f32),
            pltpu.VMEM((HIST, OWN), f32),
            pltpu.VMEM((HIST, OWN), f32),
            pltpu.VMEM((1, HIST), f32),
            dma((3,)),
            dma((4,)),
            pltpu.SemaphoreType.REGULAR((2,)),
            dma((3,)),
            dma((9,)),
            dma((2,)),
            dma((4,)),
            *[dma((1,))] * 2,
            *[dma((1,))] * 2,
            dma((3,)),
            dma((3, EARLY + 1)),
            *[dma((3,))] * 2,
            *[dma((1,))] * 2,
            *[dma((1,))] * 2,
            *[dma((3,))] * 2,
            *[dma((2,))] * 2,
            *[dma((1,))] * 2,
        ],
        compiler_params=pltpu.CompilerParams(
            collective_id=0, has_side_effects=True, vmem_limit_bytes=62 * 1024 * 1024
        ),
    )(embeddings, counts, raw_weights.reshape(1, HIST))
    return pl.pallas_call(
        hand_over,
        out_shape=(
            jax.ShapeDtypeStruct((OWN,), f32),
            jax.ShapeDtypeStruct((HIST, OWN), f32),
            jax.ShapeDtypeStruct((HIST, OWN), f32),
            jax.ShapeDtypeStruct((HIST,), f32),
        ),
        in_specs=[vmem] * 4,
        out_specs=(vmem,) * 4,
    )(center, scale_u, scale_v, misfit)


def solution(mesh):
    placed = (P(("row", "col"), None), P(None, ("row", "col")), P())
    return jax.shard_map(
        shards,
        mesh=mesh,
        in_specs=placed,
        out_specs=(P(("row", "col")), P(None, ("row", "col")), P(None, ("row", "col")), P()),
        check_vma=False,
    )
```
